256 devices in a mesh: tile: 64 (over z, x, core), band: 4 (over y).
Axes of the slice: x: 4, y: 4, z: 8, core: 2. Of those that a mesh axis runs over, the one named last changes fastest.
Arguments:
- water_depth: float32 [512, 32768], P('band', 'tile'), may hold values from 0.05 to 2
- flux_east: float32 [512, 32768], P('band', 'tile'), may hold values from -3 to 3
- flux_south: float32 [512, 32768], P('band', 'tile'), may hold values from -3 to 3
- bed_level: float32 [512, 32768], P('band', 'tile'), may hold values from -4 to 4
- roughness: float32 [512, 32768], P('band', 'tile'), may hold values from 0.001 to 0.01
- link_rows: int32 [64, 4, 512], P('tile', 'band'), may hold values from 0 to 511, as said below
- link_blocks: int32 [64, 4, 512], P('tile', 'band'), may hold values from 0 to 8191, as said below
- reach_inverse: bfloat16 [8192, 128, 128], P(('tile', 'band'))
- reach_source: float32 [8192, 128], P(('tile', 'band')), may hold values from -6 to 6
- river_section: float32 [8192, 128], P(('tile', 'band')), may hold values from -4 to 4
- block_level: int32 [8192], P(('tile', 'band')), may hold values from 0 to 7, as said below
- block_down: int32 [8192], P(('tile', 'band')), may hold values from -1 to 8191, as said below
Outputs:
- final_depth: float32 [512, 32768], P('band', 'tile')
- final_east: float32 [512, 32768], P('band', 'tile')
- final_south: float32 [512, 32768], P('band', 'tile')
- discharge: float32 [8192, 128], P(('tile', 'band'))
The draws below stay inside these ranges and needn't reach their ends.
Inputs may be any that keep to these rules, and one draw needn't show every extreme that they name: `link_rows`: the entries of one device's list are distinct. `link_blocks`: each entry names a block held by a device of the same band index as the list's device; at most 16 entries of one list name blocks held at one tile index, and in every draw some tile index receives exactly 16 from every list. `block_level`: every level occurs. `block_down`: a block below level 7 names a block whose level is one higher; the blocks of level 7 hold -1.
All inputs are finite; a program needn't handle non-finite values.
Results may differ from the reference program's by a relative error of at most 0.0003.
Values sent between devices are 32-bit elements; how exact they have to be, the bound alone decides.
No kernel may reach another device: no remote copies, remote signals or barrier semaphores. Data moves between devices by JAX's collectives and lax.ppermute only.
A program may use at most 64 MiB of HBM per device.

```python
import math
import jax
import jax.numpy as jnp
from jax import lax

ROWS_DEV = 128
COLS_DEV = 512
LINKS_DEV = 512
BLOCKS_DEV = 32
REACH = 128
SUBSTEPS = 8
LEVELS = 8
GRID_ROWS = 512
GRID_COLS = 32768
BLOCKS = 8192
SLOTS = 16
N_TILE = 64
N_BAND = 4


def river_tree(key):
    level_key, order_key, pick_key = jax.random.split(key, 3)
    levels = jax.random.randint(level_key, (BLOCKS,), 0, LEVELS).astype(jnp.int32)
    shuffled = jax.random.permutation(order_key, BLOCKS)
    levels = levels.at[shuffled[:LEVELS]].set(jnp.arange(LEVELS, dtype=jnp.int32))
    ordering = jnp.argsort(levels, stable=True)
    counts = jnp.sum((levels[:, None] == jnp.arange(LEVELS)[None, :]).astype(jnp.int32), axis=0)
    starts = jnp.cumsum(counts) - counts
    next_level = jnp.minimum(levels + 1, LEVELS - 1)
    chance = jax.random.randint(pick_key, (BLOCKS,), 0, 2 ** 30)
    picked = ordering[starts[next_level] + chance % counts[next_level]]
    downstream = jnp.where(levels < LEVELS - 1, picked, -1)
    return (levels.astype(jnp.int32), downstream.astype(jnp.int32))


def draw_block_level(key, part):
    shared = river_tree(key)
    return shared[0]


def draw_block_down(key, part):
    shared = river_tree(key)
    return shared[1]


def draw_link_rows(key, part):
    key = jax.random.fold_in(key, 5)
    device_keys = jax.random.split(key, N_TILE * N_BAND)
    row_count = ROWS_DEV * COLS_DEV // 128
    chosen = jax.vmap(lambda single_key: jax.random.permutation(single_key, row_count)[:LINKS_DEV])(device_keys)
    return chosen.reshape(N_TILE, N_BAND, LINKS_DEV).astype(jnp.int32)


def draw_link_blocks(key, part):
    key = jax.random.fold_in(key, 7)
    busy_key, score_key, local_key, order_key = jax.random.split(key, 4)
    devices = N_TILE * N_BAND
    slot_total = N_TILE * SLOTS
    busiest = jax.random.randint(busy_key, (), 0, N_TILE)
    scores = jax.random.randint(score_key, (devices, slot_total), 0, 2 ** 30)
    slot_tile = jnp.arange(slot_total) // SLOTS
    scores = jnp.where(slot_tile[None, :] == busiest, -1, scores)
    chosen = jnp.argsort(scores, axis=1, stable=True)[:, :LINKS_DEV]
    dest_tile = chosen // SLOTS
    local_block = jax.random.randint(local_key, (devices, LINKS_DEV), 0, BLOCKS_DEV)
    band_of = (jnp.arange(devices) % N_BAND)[:, None]
    global_block = (dest_tile * N_BAND + band_of) * BLOCKS_DEV + local_block
    mixing = jnp.argsort(jax.random.randint(order_key, (devices, LINKS_DEV), 0, 2 ** 30), axis=1, stable=True)
    global_block = jnp.take_along_axis(global_block, mixing, axis=1)
    return global_block.reshape(N_TILE, N_BAND, LINKS_DEV).astype(jnp.int32)


def draw_reach_inverse(key, part):
    key = jax.random.fold_in(key, 3)
    diag_key, off_key, gain_key = jax.random.split(key, 3)
    diagonal = jax.random.uniform(diag_key, (BLOCKS, REACH, 1), jnp.float32, 0.6, 1.2)
    spread = jax.random.normal(off_key, (BLOCKS, REACH, REACH), jnp.float32) * (0.35 / REACH ** 0.5)
    entry_gain = jax.random.uniform(gain_key, (BLOCKS, REACH, 1), jnp.float32, 0.4, 0.9)
    row_index = jnp.arange(REACH)[:, None]
    col_index = jnp.arange(REACH)[None, :]
    matrix = jnp.where(row_index == col_index, diagonal, spread)
    matrix = matrix + jnp.where((col_index == 0) & (row_index > 0), entry_gain, 0.0)
    return matrix.astype(jnp.bfloat16)


def block_scale(rng, dims, cuts, low, top_value):
    loudness, own = 1.0, jax.random.fold_in(rng, 6)
    for axis_at, shards_of in cuts:
        draws = jnp.exp(jax.random.uniform(jax.random.fold_in(own, axis_at), (shards_of,), jnp.float32, low / len(cuts), top_value / len(cuts)))
        loudness = loudness * jnp.repeat(draws, dims[axis_at] // shards_of).reshape([-1 if axis == axis_at else 1 for axis in range(len(dims))])
    return loudness


def noise(own_key, extent, width, bound, cuts=(), held_as=jnp.bfloat16):
    entries = jax.random.normal(own_key, extent, jnp.float32) * width
    if len(cuts) > 0:
        entries = block_scale(own_key, extent, cuts, -0.22, 0.18) * entries
    return jnp.clip(entries, min=-bound, max=bound).astype(held_as)


def setup_inputs(seed: int = 0) -> dict:
    streams_of = jax.random.split(jax.random.key(seed), 13)
    water_depth = jnp.clip(jnp.exp(math.log(2.0) - 3.6888794 * jax.random.uniform(streams_of[0], (GRID_ROWS, GRID_COLS), jnp.float32) ** block_scale(streams_of[0], (GRID_ROWS, GRID_COLS), ((0, 4), (1, 64)), -0.2, 0.2)), 0.05, 2.0)
    flux_east = noise(streams_of[1], (GRID_ROWS, GRID_COLS), 0.5, 3.0, ((0, 4), (1, 64)), jnp.float32)
    flux_south = noise(streams_of[2], (GRID_ROWS, GRID_COLS), 0.5, 3.0, ((0, 4), (1, 64)), jnp.float32)
    bed_level = noise(streams_of[3], (GRID_ROWS, GRID_COLS), 1.0, 4.0, ((0, 4), (1, 64)), jnp.float32)
    roughness = jnp.clip(jnp.exp(math.log(0.01) - 2.30258502 * jax.random.uniform(streams_of[4], (GRID_ROWS, GRID_COLS), jnp.float32) ** block_scale(streams_of[4], (GRID_ROWS, GRID_COLS), ((0, 4), (1, 64)), -0.2, 0.2)), 0.001, 0.01)
    link_rows = draw_link_rows(jax.random.fold_in(streams_of[12], 71), 0)
    link_blocks = draw_link_blocks(jax.random.fold_in(streams_of[12], 71), 0)
    reach_inverse = draw_reach_inverse(jax.random.fold_in(streams_of[12], 71), 0)
    reach_source = noise(streams_of[8], (BLOCKS, REACH), 1.0, 6.0, ((0, 256),), jnp.float32)
    river_section = noise(streams_of[9], (BLOCKS, REACH), 1.0, 4.0, ((0, 256),), jnp.float32)
    block_level = draw_block_level(jax.random.fold_in(streams_of[12], 71), 0)
    block_down = draw_block_down(jax.random.fold_in(streams_of[12], 71), 0)
    return dict(water_depth=water_depth, flux_east=flux_east, flux_south=flux_south, bed_level=bed_level, roughness=roughness, link_rows=link_rows, link_blocks=link_blocks, reach_inverse=reach_inverse, reach_source=reach_source, river_section=river_section, block_level=block_level, block_down=block_down)


GRAVITY = 9.81
TIME_STEP = 3.0
CELL_WIDTH = 30.0
DEPTH_FLOOR = 0.2
FRICTION_POWER = 7.0 / 3.0
LATERAL_RATE = 0.2
PLAIN_SHARE = 0.8
RIVER_SHARE = 0.25


def face_flux(here_level, ahead_level, here_bed, ahead_bed, here_rough, old_flux):
    flow_depth = jnp.maximum(jnp.maximum(here_level, ahead_level) - jnp.maximum(here_bed, ahead_bed), DEPTH_FLOOR)
    surface_slope = (ahead_level - here_level) / CELL_WIDTH
    driven_flux = old_flux - GRAVITY * TIME_STEP * flow_depth * surface_slope
    return driven_flux / (1.0 + GRAVITY * TIME_STEP * here_rough * jnp.abs(old_flux) / jnp.power(flow_depth, FRICTION_POWER))


def to_tiles(field):
    return field.reshape(N_BAND, ROWS_DEV, N_TILE, COLS_DEV).transpose(2, 0, 1, 3).reshape(N_TILE, N_BAND, ROWS_DEV * COLS_DEV // 128, 128)


def from_tiles(tiled):
    return tiled.reshape(N_TILE, N_BAND, ROWS_DEV, COLS_DEV).transpose(1, 2, 0, 3).reshape(GRID_ROWS, GRID_COLS)


def reference(water_depth, flux_east, flux_south, bed_level, roughness, link_rows, link_blocks, reach_inverse, reach_source, river_section, block_level, block_down):
    surface = bed_level + water_depth
    picked = jax.vmap(jax.vmap(lambda table, chosen: table[chosen]))(to_tiles(surface), link_rows)
    lateral = LATERAL_RATE * (picked - river_section[link_blocks])
    lateral_sum = jax.ops.segment_sum(lateral.reshape(-1, REACH), link_blocks.reshape(-1), num_segments=BLOCKS)
    source = reach_source + RIVER_SHARE * lateral_sum
    inverse = reach_inverse.astype(jnp.float32)
    base_flow = jnp.einsum("bij,bj->bi", inverse, source, precision=lax.Precision.HIGHEST)
    inflow_gain = inverse[:, REACH - 1, 0]
    column = inverse[:, :, 0]
    target = jnp.where(block_down >= 0, block_down, BLOCKS)
    inflow = jnp.zeros((BLOCKS,), jnp.float32)
    for level_now in range(LEVELS):
        outflow = base_flow[:, REACH - 1] + inflow_gain * inflow
        level_share = jnp.where(block_level == level_now, outflow, 0.0)
        inflow = inflow.at[target].add(level_share, mode="drop")
    discharge = base_flow + column * inflow[:, None]

    water_now = water_depth
    east_flux = flux_east
    south_flux = flux_south
    last_column = jnp.arange(GRID_COLS) == GRID_COLS - 1
    last_row = jnp.arange(GRID_ROWS) == GRID_ROWS - 1
    for substep in range(SUBSTEPS):
        level = bed_level + water_now
        ahead_level = jnp.pad(level[:, 1:], ((0, 0), (0, 1)))
        ahead_bed = jnp.pad(bed_level[:, 1:], ((0, 0), (0, 1)))
        new_east = face_flux(level, ahead_level, bed_level, ahead_bed, roughness, east_flux)
        new_east = jnp.where(last_column[None, :], 0.0, new_east)
        below_level = jnp.pad(level[1:, :], ((0, 1), (0, 0)))
        below_bed = jnp.pad(bed_level[1:, :], ((0, 1), (0, 0)))
        new_south = face_flux(level, below_level, bed_level, below_bed, roughness, south_flux)
        new_south = jnp.where(last_row[:, None], 0.0, new_south)
        west_side = jnp.pad(new_east[:, :-1], ((0, 0), (1, 0)))
        north_side = jnp.pad(new_south[:-1, :], ((1, 0), (0, 0)))
        water_now = water_now + (TIME_STEP / CELL_WIDTH) * (west_side - new_east + north_side - new_south)
        east_flux = new_east
        south_flux = new_south
    updated = jax.vmap(jax.vmap(lambda table, chosen, values: table.at[chosen].add(values)))(to_tiles(water_now), link_rows, -PLAIN_SHARE * lateral)
    final_depth = from_tiles(updated)
    return final_depth, east_flux, south_flux, discharge
```

```python
import functools

import jax
import jax.numpy as jnp
from jax import lax
from jax.experimental import pallas as pl
from jax.experimental.pallas import tpu as pltpu
from jax.sharding import PartitionSpec as P

SUBSTEPS = 8
LEVELS = 8
HALO = 8
LANES = 128
SLOTS = 16
CHUNK = SLOTS + 1

GRAVITY = 9.81
TIME_STEP = 3.0
CELL_WIDTH = 30.0
DEPTH_FLOOR = 0.2
FRICTION_POWER = 7.0 / 3.0
LATERAL_RATE = 0.2
PLAIN_SHARE = 0.8
RIVER_SHARE = 0.25

F32 = jnp.float32
BF16 = jnp.bfloat16
VMEM = pl.BlockSpec(memory_space=pltpu.VMEM)
SMEM = pl.BlockSpec(memory_space=pltpu.SMEM)


def iota(shape, dim):
    return lax.broadcasted_iota(jnp.int32, shape, dim)


def halves(x):
    hi = x.astype(BF16)
    lo = (x - hi.astype(F32)).astype(BF16)
    return hi, lo


def paired(x):
    hi, lo = halves(x)
    return jnp.concatenate([hi, lo], axis=1)


def fold(x):
    return x[:, :LANES] + x[:, LANES:]


def mm(a, b, dims=((1,), (0,))):
    return lax.dot_general(a, b, (dims, ((), ())), preferred_element_type=F32)


def pack_kernel(water, bed, link_rows, link_blocks, table, out, slots):
    rows = link_rows[...]
    blocks = link_blocks[...]
    links = rows.shape[1]
    height = water.shape[0]
    groups = water.shape[1] // LANES
    tiles = out.shape[0] // CHUNK
    place = ((rows % groups) * height + rows // groups).astype(F32)
    dest = (blocks >> 7).astype(F32)
    local = (blocks & 31).astype(F32)
    pick = iota((8, links), 0)
    stacked = jnp.where(pick == 0, place, jnp.where(pick == 1, dest, local))
    turned = jnp.transpose(stacked)
    place_c, dest_c, local_c = turned[:, 0:1], turned[:, 1:2], turned[:, 2:3]
    earlier = (dest_c == dest) & (iota((links, links), 1) < iota((links, links), 0))
    ones = jnp.ones((links, LANES), BF16)
    rank = mm(earlier.astype(F32).astype(BF16), ones)
    position = dest_c * float(CHUNK) + rank
    position_c = position[:, 0:1]
    lane = iota((links, links), 1).astype(F32)
    slot_of = jnp.sum(jnp.where(place_c == lane, position_c, 0.0), axis=0, keepdims=True)
    slots[...] = jnp.broadcast_to(slot_of, slots.shape)
    dest_hot = (iota((tiles, links), 0).astype(F32) == dest).astype(F32).astype(BF16)
    rank_hot = jnp.where(rank == iota((links, LANES), 1).astype(F32), local_c + 1.0, 0.0)
    ids = mm(dest_hot, rank_hot.astype(BF16))
    level = water[...] + bed[...]
    by_block = jnp.concatenate(
        [level[:, c * LANES : (c + 1) * LANES] for c in range(groups)], axis=0
    )
    by_block = paired(by_block)
    step = 8 * CHUNK
    for start in range(0, out.shape[0], step):
        hot = (iota((step, links), 0) + start).astype(F32) == slot_of
        out[start : start + step, :] = fold(mm(hot.astype(F32).astype(BF16), by_block))
    out[pl.ds(SLOTS, tiles, CHUNK), :] = ids + table[0:1, :]


def lateral_kernel(rows_in, section, reach_source, last_row, out, source, ends):
    total = rows_in.shape[0]
    tiles = total // CHUNK
    blocks = section.shape[0]
    slot = iota((total, 1), 0).astype(F32)
    owner = jnp.floor((slot + 0.5) * (1.0 / CHUNK))
    within = slot - owner * CHUNK
    extras = rows_in[pl.ds(SLOTS, tiles, CHUNK), :]
    ids = jnp.where(iota((tiles, LANES), 1) < SLOTS, extras, 0.0).astype(BF16)
    spread = (iota((total, tiles), 1).astype(F32) == owner).astype(F32).astype(BF16)
    mine = mm(spread, ids)
    mine = jnp.where(iota((total, LANES), 1).astype(F32) == within, mine, 0.0)
    block = mm(mine.astype(BF16), jnp.ones((LANES, LANES), BF16)) - 1.0
    hot = (block == iota((total, LANES), 1).astype(F32)).astype(F32).astype(BF16)
    rows = rows_in[...]
    section_in = fold(mm(hot[:, :blocks], paired(section[...])))
    lateral = jnp.where(block >= 0.0, LATERAL_RATE * (rows - section_in), 0.0)
    out[...] = lateral
    sums = fold(mm(hot, paired(lateral), ((0,), (0,))))[:blocks]
    src = reach_source[...] + RIVER_SHARE * sums
    source[...] = src
    end = jnp.sum(src * last_row[...].astype(F32), axis=1, keepdims=True)
    ends[...] = jnp.broadcast_to(end, ends.shape)


def push_kernel(where, lateral, ends, table, own, one, two, three, out):
    band = where[1]
    bands = 4
    tiles = own.shape[0]
    blocks = ends.shape[0]
    lane = iota((tiles, LANES), 1)
    down = jnp.zeros((tiles, LANES), F32)
    gain = jnp.zeros((tiles, LANES), F32)
    for back, ref in enumerate((own, one, two, three)):
        source = (band + bands - back) % bands
        x = ref[...]
        here = (lane // blocks) == source
        y = x
        for turn in (1, 2, 3):
            y = jnp.where(lane // blocks == (turn + 1) % bands, pltpu.roll(x, turn * blocks, 1), y)
        down = jnp.where(here, y, down)
        y = x
        for turn in (1, 2, 3):
            y = jnp.where(lane // blocks == (turn + 2) % bands, pltpu.roll(x, turn * blocks, 1), y)
        gain = jnp.where(here, y, gain)
    high = jnp.floor(down * (1.0 / LANES))
    tables = jnp.concatenate([high + 1.0, down - high * LANES, gain], axis=1).astype(BF16)
    column = jnp.transpose(table[...])[blocks : 2 * blocks, 0:1]
    column_high = jnp.floor(column * (1.0 / LANES))
    high, low = column_high + 1.0, column - column_high * LANES
    factor = ends[...][:, 0:1]
    tile_lane = iota((blocks, tiles), 1).astype(F32) + 1.0
    block_lane = iota((blocks, LANES), 1).astype(F32)
    lefts, rights = [], []
    for hop in range(LEVELS - 1):
        left = (tile_lane == high).astype(F32)
        right = (block_lane == low).astype(F32)
        lefts.append(left * factor)
        rights.append(right.astype(BF16))
        if hop < LEVELS - 2:
            found = mm(left.astype(BF16), tables)
            high = jnp.sum(found[:, :LANES] * right, axis=1, keepdims=True)
            low = jnp.sum(found[:, LANES : 2 * LANES] * right, axis=1, keepdims=True)
            factor = factor * jnp.sum(found[:, 2 * LANES :] * right, axis=1, keepdims=True)
    left_hi, left_lo = halves(jnp.concatenate(lefts, axis=0))
    right = jnp.concatenate(rights, axis=0)
    pushed = mm(left_hi, right, ((0,), (0,))) + mm(left_lo, right, ((0,), (0,)))
    out[...] = lateral[...]
    out[pl.ds(SLOTS, tiles, CHUNK), :] = pushed


def flow_kernel(source, inverse, base, column):
    blocks = source.shape[0]
    hi, lo = halves(source[...])
    first = (iota((blocks, LANES), 1) == 0).astype(F32).astype(BF16)
    stacked = jnp.concatenate([hi, lo, first], axis=0)
    row = iota((blocks, LANES), 0)
    base_now = jnp.zeros((blocks, LANES), F32)
    column_now = jnp.zeros((blocks, LANES), F32)
    for g in range(blocks):
        x = mm(stacked, inverse[g], ((1,), (1,)))
        base_now = jnp.where(row == g, x[:blocks] + x[blocks : 2 * blocks], base_now)
        column_now = jnp.where(row == g, x[2 * blocks :], column_now)
    base[...] = base_now
    column[...] = column_now


def final_kernel(water, returned, slots, out):
    total = returned.shape[0]
    height = water.shape[0]
    groups = water.shape[1] // LANES
    slot_c = jnp.transpose(slots[...])[:, 0:1]
    rows = paired(returned[...])
    for c in range(groups):
        mine = slot_c[c * height : (c + 1) * height]
        hot = (iota((height, total), 1).astype(F32) == mine).astype(F32).astype(BF16)
        lateral = fold(mm(hot, rows))
        cols = slice(c * LANES, (c + 1) * LANES)
        out[:, cols] = water[:, cols] - PLAIN_SHARE * lateral


def strips_kernel(above, below, f0, f1, f2, f3, f4, left, right):
    fields = (f0, f1, f2, f3, f4)
    height, width = f0.shape
    tiles = height // 8 + 2
    lane = iota((8, LANES), 1)
    groups = left.shape[0] // 8
    lefts = [jnp.zeros((8, LANES), F32) for _ in range(groups)]
    rights = [jnp.zeros((8, LANES), F32) for _ in range(groups)]
    for a, field in enumerate(fields):
        for i in range(tiles):
            if i == 0:
                ref, rows = above, slice(a * HALO, a * HALO + 8)
            elif i == tiles - 1:
                ref, rows = below, slice(a * HALO, a * HALO + 8)
            else:
                ref, rows = field, slice(8 * i - 8, 8 * i)
            strip = a * tiles + i
            v, off = strip // 16, (strip % 16) * 8
            here = (lane >= off) & (lane < off + 8)
            x = ref[rows, 0:LANES]
            y = ref[rows, width - LANES : width]
            x = pltpu.roll(x, off, 1) if off else x
            y = pltpu.roll(y, (off + 8) % LANES, 1) if (off + 8) % LANES else y
            lefts[v] = jnp.where(here, x, lefts[v])
            rights[v] = jnp.where(here, y, rights[v])
    for v in range(groups):
        left[8 * v : 8 * v + 8, :] = lefts[v]
        right[8 * v : 8 * v + 8, :] = rights[v]


def flood_kernel(
    where, above, below, west, east, f0, f1, f2, f3, f4,
    water_out, east_out, south_out,
    level_s, bed_s, rough_s, qe_s, qs_s, mbe_s, mbs_s,
):
    height, width = f0.shape
    tiles = height // 8 + 2
    wide = width + LANES
    lane1 = iota((8, LANES), 1)
    scratch = (level_s, bed_s, rough_s, qe_s, qs_s)
    rate = GRAVITY * TIME_STEP
    tile_index, band_index, tile_last, band_last = where[0], where[1], where[2], where[3]
    for a, (field, dst) in enumerate(zip((f0, f1, f2, f3, f4), scratch)):
        for i in range(tiles):
            if i == 0:
                ref, rows = above, slice(a * HALO, a * HALO + 8)
            elif i == tiles - 1:
                ref, rows = below, slice(a * HALO, a * HALO + 8)
            else:
                ref, rows = field, slice(8 * i - 8, 8 * i)
            strip = a * tiles + i
            v, off = strip // 16, (strip % 16) * 8
            x = east[8 * v : 8 * v + 8, :]
            y = west[8 * v : 8 * v + 8, :]
            x = pltpu.roll(x, LANES - off, 1) if off else x
            y = pltpu.roll(y, (LANES - 8 - off) % LANES, 1) if (LANES - 8 - off) % LANES else y
            edge = jnp.where(lane1 < 8, x, jnp.where(lane1 >= LANES - 8, y, 0.0))
            body = ref[rows, :]
            if a == 2:
                body, edge = rate * body, rate * edge
            dst[8 * i : 8 * i + 8, :width] = body
            dst[8 * i : 8 * i + 8, width:] = edge
    lane = iota((8, wide), 1)
    sub = iota((8, wide), 0)
    shut_e = ((lane == width - 1) & (tile_index == tile_last)) | ((lane == wide - 1) & (tile_index == 0))
    ce = jnp.where(shut_e, 0.0, rate / CELL_WIDTH)
    shut_n = (sub == 7) & (band_index == 0)
    shut_s = (sub == 7) & (band_index == band_last)
    cs_first = jnp.where(shut_n, 0.0, rate / CELL_WIDTH)
    cs_last = jnp.where(shut_s, 0.0, rate / CELL_WIDTH)
    nxt = bed_s[0:8, :]
    nxt_up = pltpu.roll(nxt, 7, 0)
    for i in range(tiles):
        rows = slice(8 * i, 8 * i + 8)
        bed, up = nxt, nxt_up
        if i + 1 < tiles:
            nxt = bed_s[8 * i + 8 : 8 * i + 16, :]
            nxt_up = pltpu.roll(nxt, 7, 0)
        mbe_s[rows, :] = jnp.maximum(bed, pltpu.roll(bed, wide - 1, 1))
        mbs_s[rows, :] = jnp.maximum(bed, jnp.where(sub == 7, nxt_up, up))
        qe_s[rows, :] = jnp.where(shut_e, 0.0, qe_s[rows, :])
    last = slice(height, height + 8)
    qs_s[last, :] = jnp.where(shut_s, 0.0, qs_s[last, :])

    def face(here, ahead, bed_max, rough, old, factor):
        depth = jnp.maximum(jnp.maximum(here, ahead) - bed_max, DEPTH_FLOOR)
        drag = rough * jnp.abs(old) * jnp.exp(-FRICTION_POWER * jnp.log(depth)) + 1.0
        near = pl.reciprocal(drag, approx=True)
        near = near * (2.0 - drag * near)
        return (old - factor * depth * (ahead - here)) * near

    def substep(_, carry):
        nxt = level_s[0:8, :]
        nxt_up = pltpu.roll(nxt, 7, 0)
        north_turned = jnp.zeros((8, wide), F32)
        for i in range(tiles):
            rows = slice(8 * i, 8 * i + 8)
            level, up = nxt, nxt_up
            if i + 1 < tiles:
                nxt = level_s[8 * i + 8 : 8 * i + 16, :]
                nxt_up = pltpu.roll(nxt, 7, 0)
            rough = rough_s[rows, :]
            cs = cs_first if i == 0 else cs_last if i == tiles - 2 else rate / CELL_WIDTH
            qe = face(level, pltpu.roll(level, wide - 1, 1), mbe_s[rows, :], rough, qe_s[rows, :], ce)
            below_level = jnp.where(sub == 7, nxt_up, up)
            qs = face(level, below_level, mbs_s[rows, :], rough, qs_s[rows, :], cs)
            qe_s[rows, :] = qe
            qs_s[rows, :] = qs
            turned = pltpu.roll(qs, 1, 0)
            north = jnp.where(sub == 0, north_turned, turned)
            north_turned = turned
            gained = pltpu.roll(qe, 1, 1) - qe + north - qs
            level_s[rows, :] = level + (TIME_STEP / CELL_WIDTH) * gained
        return carry

    lax.fori_loop(0, SUBSTEPS, substep, 0)
    inner = slice(HALO, HALO + height)
    water_out[...] = level_s[inner, :width] - bed_s[inner, :width]
    east_out[...] = qe_s[inner, :width]
    south_out[...] = qs_s[inner, :width]


def shaped(*shape):
    return jax.ShapeDtypeStruct(shape, F32)


def call(kernel, out_shape, specs, scratch=(), flops=0, size=0, exps=0):
    return pl.pallas_call(
        kernel,
        out_shape=out_shape,
        in_specs=specs,
        out_specs=jax.tree.map(lambda _: VMEM, out_shape),
        scratch_shapes=list(scratch),
        compiler_params=pltpu.CompilerParams(vmem_limit_bytes=40 * 1024 * 1024),
        cost_estimate=pl.CostEstimate(flops=flops, bytes_accessed=size, transcendentals=exps),
        name=kernel.__name__,
    )


def per_device(
    water_depth, flux_east, flux_south, bed_level, roughness, link_rows, link_blocks,
    reach_inverse, reach_source, river_section, block_level, block_down,
):
    tiles = lax.axis_size("tile")
    bands = lax.axis_size("band")
    tile_index = lax.axis_index("tile")
    band_index = lax.axis_index("band")
    height, width = water_depth.shape
    blocks, reach = reach_source.shape
    total = tiles * CHUNK
    links = link_rows.shape[-1]
    where = jnp.stack(
        [tile_index, band_index, jnp.int32(tiles - 1), jnp.int32(bands - 1)]
    ).astype(jnp.int32)
    ring = [[(i, (i + k) % bands) for i in range(bands)] for k in range(bands)]

    last_row = reach_inverse[:, reach - 1, :]
    gain = last_row[:, 0].astype(F32)
    table = jnp.concatenate(
        [jnp.zeros((blocks,), F32), block_down.astype(F32), gain, jnp.zeros((blocks,), F32)]
    )
    table = jnp.broadcast_to(table[None, :], (8, LANES))

    payload, slots = call(
        pack_kernel, (shaped(total, LANES), shaped(8, links)), [VMEM] * 5, flops=10**9, size=10**6
    )(water_depth, bed_level, link_rows.reshape(1, links), link_blocks.reshape(1, links), table)
    rows_in = lax.all_to_all(
        payload.reshape(tiles, CHUNK, 1, LANES), "tile", split_axis=0, concat_axis=0, tiled=True
    )

    fields = (bed_level + water_depth, bed_level, roughness, flux_east, flux_south)
    top = jnp.concatenate([f[:HALO] for f in fields], axis=0)
    bottom = jnp.concatenate([f[height - HALO :] for f in fields], axis=0)
    above = lax.ppermute(bottom, "band", [(i, i + 1) for i in range(bands - 1)])
    below = lax.ppermute(top, "band", [(i + 1, i) for i in range(bands - 1)])
    left, right = call(
        strips_kernel, (shaped(48, LANES), shaped(48, LANES)), [VMEM] * 7, flops=10**6, size=10**6
    )(above, below, *fields)
    west = lax.ppermute(right, "tile", [(i, i + 1) for i in range(tiles - 1)])
    east = lax.ppermute(left, "tile", [(i + 1, i) for i in range(tiles - 1)])

    extras = rows_in.reshape(tiles, CHUNK, LANES)[:, SLOTS, :]
    others = [lax.ppermute(extras, "band", ring[k]) for k in (1, 2, 3)]
    lateral, source, ends = call(
        lateral_kernel,
        (shaped(total, LANES), shaped(blocks, LANES), shaped(blocks, LANES)),
        [VMEM] * 4,
        flops=10**9,
        size=10**6,
    )(rows_in.reshape(total, LANES), river_section, reach_source, last_row)
    answer = call(
        push_kernel, shaped(total, LANES), [SMEM] + [VMEM] * 7, flops=10**8, size=10**6
    )(where, lateral, ends, table, extras, *others)
    returned = lax.all_to_all(
        answer.reshape(tiles, CHUNK, 1, LANES), "tile", split_axis=0, concat_axis=0, tiled=True
    )

    wide = width + LANES
    tall = height + 2 * HALO
    water_now, final_east, final_south = call(
        flood_kernel,
        (shaped(height, width),) * 3,
        [SMEM] + [VMEM] * 9,
        scratch=[pltpu.VMEM((tall, wide), F32)] * 7,
        flops=10**8,
        size=10**7,
        exps=10**7,
    )(where, above, below, west, east, *fields)
    base_flow, column = call(
        flow_kernel, (shaped(blocks, reach),) * 2, [VMEM] * 2, flops=10**8, size=10**6
    )(source, reach_inverse)

    pushed = jnp.sum(returned.reshape(tiles, CHUNK, LANES)[:, SLOTS, :], axis=0, keepdims=True)
    parts = [pushed] + [lax.ppermute(pushed, "band", ring[k]) for k in (1, 2, 3)]
    final_depth = call(
        final_kernel, shaped(height, width), [VMEM] * 3, flops=10**9, size=10**6
    )(water_now, returned.reshape(total, LANES), slots)
    inflow = lax.dynamic_slice_in_dim(sum(parts)[0], band_index * blocks, blocks)
    discharge = base_flow + column * inflow[:, None]
    return (final_depth, final_east, final_south, discharge)


def solution(mesh):
    grid = P("band", "tile")
    owned = P(("tile", "band"))
    lists = P("tile", "band", None)
    return jax.shard_map(
        per_device,
        mesh=mesh,
        in_specs=(grid,) * 5 + (lists,) * 2 + (owned,) * 5,
        out_specs=(grid, grid, grid, owned),
        check_vma=False,
    )
```

```python
import functools

import jax
import jax.numpy as jnp
from jax import lax
from jax.experimental import pallas as pl
from jax.experimental.pallas import tpu as pltpu
from jax.sharding import PartitionSpec as P

SUBSTEPS = 8
LEVELS = 8
HALO = 8
LANES = 128
SLOTS = 16
CHUNK = SLOTS + 1
GAIN_LANE = 64
ID_LANE = 96

GRAVITY = 9.81
TIME_STEP = 3.0
CELL_WIDTH = 30.0
DEPTH_FLOOR = 0.2
FRICTION_POWER = 7.0 / 3.0
LATERAL_RATE = 0.2
PLAIN_SHARE = 0.8
RIVER_SHARE = 0.25

F32 = jnp.float32
BF16 = jnp.bfloat16
VMEM = pl.BlockSpec(memory_space=pltpu.VMEM)
SMEM = pl.BlockSpec(memory_space=pltpu.SMEM)
HBM = pl.BlockSpec(memory_space=pltpu.HBM)
ANY = pl.BlockSpec(memory_space=pl.ANY)


def iota(shape, dim):
    return lax.broadcasted_iota(jnp.int32, shape, dim)


def halves(x):
    hi = x.astype(BF16)
    lo = (x - hi.astype(F32)).astype(BF16)
    return hi, lo


def paired(x):
    hi, lo = halves(x)
    return jnp.concatenate([hi, lo], axis=1)


def fold(x):
    return x[:, :LANES] + x[:, LANES:]


def mm(a, b, dims=((1,), (0,))):
    return lax.dot_general(a, b, (dims, ((), ())), preferred_element_type=F32)


def pack_kernel(
    water_h, bed_h, rows_h, blocks_h, inverse_h, down,
    out, slots, tables, last_out,
    water, bed, link_rows, link_blocks, tails, row_s, sems,
):
    blocks_own, reach = last_out.shape
    moves = (
        (rows_h, link_rows),
        (blocks_h, link_blocks),
        (water_h, water),
        (bed_h, bed),
        (inverse_h.at[:, reach - 16 : reach, :], tails),
    )
    copies = [pltpu.make_async_copy(src, dst, sems.at[i]) for i, (src, dst) in enumerate(moves)]
    for copy in copies:
        copy.start()
    copies[0].wait()
    copies[1].wait()
    rows = link_rows[...]
    blocks = link_blocks[...]
    links = rows.shape[1]
    height = water.shape[0]
    groups = water.shape[1] // LANES
    tiles = out.shape[0] // SLOTS
    bands = tables.shape[0] // tiles
    place = ((rows % groups) * height + rows // groups).astype(F32)
    dest = (blocks >> 7).astype(F32)
    local = (blocks & 31).astype(F32)
    pick = iota((8, links), 0)
    stacked = jnp.where(pick == 0, place, jnp.where(pick == 1, dest, local))
    turned = jnp.transpose(stacked)
    place_c, dest_c, local_c = turned[:, 0:1], turned[:, 1:2], turned[:, 2:3]
    earlier = (dest_c == dest) & (iota((links, links), 1) < iota((links, links), 0))
    ones = jnp.ones((links, LANES), BF16)
    rank = mm(earlier.astype(F32).astype(BF16), ones)
    position = dest_c * float(SLOTS) + rank
    position_c = position[:, 0:1]
    lane = iota((links, links), 1).astype(F32)
    slot_of = jnp.sum(jnp.where(place_c == lane, position_c, 0.0), axis=0, keepdims=True)
    slots[...] = jnp.broadcast_to(slot_of, slots.shape)
    copies[2].wait()
    copies[3].wait()
    level = water[...] + bed[...]
    by_block = jnp.concatenate(
        [level[:, c * LANES : (c + 1) * LANES] for c in range(groups)], axis=0
    )
    by_block = paired(by_block)
    step = 128
    for start in range(0, out.shape[0], step):
        hot = (iota((step, links), 0) + start).astype(F32) == slot_of
        out[start : start + step, :] = fold(mm(hot.astype(F32).astype(BF16), by_block))
    dest_hot = (iota((tiles, links), 0).astype(F32) == dest).astype(F32).astype(BF16)
    seat = iota((links, LANES), 1).astype(F32) - float(ID_LANE)
    rank_hot = jnp.where(rank == seat, local_c + 1.0, 0.0)
    ids = mm(dest_hot, rank_hot.astype(BF16))
    copies[4].wait()
    last = tails[:, 15, :].astype(F32)
    last_out[...] = last
    first = (iota((8, reach), 1) == 0).astype(F32).astype(BF16)
    seated = jnp.concatenate(
        [jnp.zeros((GAIN_LANE, reach), F32), last, jnp.zeros((LANES - GAIN_LANE - blocks_own, reach), F32)],
        axis=0,
    )
    gain = mm(first, seated.astype(BF16), ((1,), (1,)))
    row_s[...] = jnp.zeros(row_s.shape, F32)
    row_s[0:1, 0:blocks_own] = down[...].astype(F32)
    entry = ids + (row_s[0:1, :] + gain[0:1, :])
    for b in range(bands):
        tables[pl.ds(b, tiles, bands), :] = entry


def river_kernel(
    where, rows_in, tables_in, section, reach_source, last_row, down, order, out, source
):
    total = rows_in.shape[0]
    tiles = total // SLOTS
    blocks = section.shape[0]
    bands = tables_in.shape[0] // tiles
    band = where[1]
    group = iota((tiles, LANES), 1) // blocks
    turns = LANES // blocks
    downs = jnp.zeros((tiles, LANES), F32)
    gains = jnp.zeros((tiles, LANES), F32)
    mine = jnp.zeros((tiles, LANES), F32)
    for b in range(bands):
        x = tables_in[pl.ds(b, tiles, bands), :]
        mine = jnp.where(band == b, x, mine)
        y = pltpu.roll(x, b * blocks, 1) if b else x
        downs = jnp.where(group == b, y, downs)
        turn = (b * blocks - GAIN_LANE) % LANES
        y = pltpu.roll(x, turn, 1) if turn else x
        gains = jnp.where(group == b, y, gains)
    high = jnp.floor(downs * (1.0 / LANES))
    tables = jnp.concatenate([high + 1.0, downs - high * LANES, gains], axis=1).astype(BF16)

    slot = iota((total, 1), 0)
    owner = slot // SLOTS
    within = slot % SLOTS + ID_LANE
    spread = (iota((total, tiles), 1) == owner).astype(F32).astype(BF16)
    seat = mm(spread, mine.astype(BF16))
    seat = jnp.where(iota((total, LANES), 1) == within, seat, 0.0)
    block = mm(seat.astype(BF16), jnp.ones((LANES, LANES), BF16)) - 1.0
    hot = (block == iota((total, LANES), 1).astype(F32)).astype(F32).astype(BF16)
    section_in = fold(mm(hot[:, :blocks], paired(section[...])))
    lateral = jnp.where(block >= 0.0, LATERAL_RATE * (rows_in[...] - section_in), 0.0)
    sums = fold(mm(hot, paired(lateral), ((0,), (0,))))[:blocks]
    src = reach_source[...] + RIVER_SHARE * sums
    source[...] = src
    ends = jnp.sum(src * last_row[...], axis=1, keepdims=True)

    column = jnp.transpose(down[...])[:, 0:1]
    column_high = jnp.floor(column * (1.0 / LANES))
    high, low = column_high + 1.0, column - column_high * LANES
    factor = jnp.ones((blocks, 1), F32)
    tile_lane = iota((blocks, tiles), 1).astype(F32) + 1.0
    block_lane = iota((blocks, LANES), 1).astype(F32)
    lefts, rights = [], []
    for hop in range(LEVELS - 1):
        left = (tile_lane == high).astype(F32)
        right = (block_lane == low).astype(F32)
        lefts.append(left * factor)
        rights.append(right.astype(BF16))
        if hop < LEVELS - 2:
            found = mm(left.astype(BF16), tables)
            high = jnp.sum(found[:, :LANES] * right, axis=1, keepdims=True)
            low = jnp.sum(found[:, LANES : 2 * LANES] * right, axis=1, keepdims=True)
            factor = factor * jnp.sum(found[:, 2 * LANES :] * right, axis=1, keepdims=True)
    left = jnp.concatenate([x * ends for x in lefts], axis=0)
    left_hi, left_lo = halves(left)
    right = jnp.concatenate(rights, axis=0)
    pushed = mm(left_hi, right, ((0,), (0,))) + mm(left_lo, right, ((0,), (0,)))
    for t in range(tiles):
        out[t * CHUNK : t * CHUNK + SLOTS, :] = lateral[t * SLOTS : (t + 1) * SLOTS]
    out[pl.ds(SLOTS, tiles, CHUNK), :] = pushed


def flow_kernel(source, inverse, base, column):
    blocks = source.shape[0]
    hi, lo = halves(source[...])
    first = (iota((blocks, LANES), 1) == 0).astype(F32).astype(BF16)
    stacked = jnp.concatenate([hi, lo, first], axis=0)
    row = iota((blocks, LANES), 0)
    base_now = jnp.zeros((blocks, LANES), F32)
    column_now = jnp.zeros((blocks, LANES), F32)
    for g in range(blocks):
        x = mm(stacked, inverse[g], ((1,), (1,)))
        base_now = jnp.where(row == g, x[:blocks] + x[blocks : 2 * blocks], base_now)
        column_now = jnp.where(row == g, x[2 * blocks :], column_now)
    base[...] = base_now
    column[...] = column_now


def final_kernel(water, returned, slots, out):
    total = returned.shape[0]
    height = water.shape[0]
    groups = water.shape[1] // LANES
    slot = slots[...]
    slot_c = jnp.transpose(slot + jnp.floor(slot * (1.0 / SLOTS)))[:, 0:1]
    rows = paired(returned[...])
    for c in range(groups):
        mine = slot_c[c * height : (c + 1) * height]
        hot = (iota((height, total), 1).astype(F32) == mine).astype(F32).astype(BF16)
        lateral = fold(mm(hot, rows))
        cols = slice(c * LANES, (c + 1) * LANES)
        out[:, cols] = water[:, cols] - PLAIN_SHARE * lateral


def strips_kernel(above, below, f0, f1, f2, f3, f4, left, right):
    fields = (f0, f1, f2, f3, f4)
    height, width = f0.shape
    tiles = height // 8 + 2
    lane = iota((8, LANES), 1)
    groups = left.shape[0] // 8
    lefts = [jnp.zeros((8, LANES), F32) for _ in range(groups)]
    rights = [jnp.zeros((8, LANES), F32) for _ in range(groups)]
    for a, field in enumerate(fields):
        for i in range(tiles):
            if i == 0:
                ref, rows = above, slice(a * HALO, a * HALO + 8)
            elif i == tiles - 1:
                ref, rows = below, slice(a * HALO, a * HALO + 8)
            else:
                ref, rows = field, slice(8 * i - 8, 8 * i)
            strip = a * tiles + i
            v, off = strip // 16, (strip % 16) * 8
            here = (lane >= off) & (lane < off + 8)
            x = ref[rows, 0:LANES]
            y = ref[rows, width - LANES : width]
            x = pltpu.roll(x, off, 1) if off else x
            y = pltpu.roll(y, (off + 8) % LANES, 1) if (off + 8) % LANES else y
            lefts[v] = jnp.where(here, x, lefts[v])
            rights[v] = jnp.where(here, y, rights[v])
    for v in range(groups):
        left[8 * v : 8 * v + 8, :] = lefts[v]
        right[8 * v : 8 * v + 8, :] = rights[v]


def flood_kernel(
    where, above, below, west, east, f0, f1, f2, f3, f4,
    water_out, east_out, south_out,
    level_s, bed_s, rough_s, qe_s, qs_s, mbe_s, mbs_s,
):
    height, width = f0.shape
    tiles = height // 8 + 2
    wide = width + LANES
    lane1 = iota((8, LANES), 1)
    scratch = (level_s, bed_s, rough_s, qe_s, qs_s)
    rate = GRAVITY * TIME_STEP
    tile_index, band_index, tile_last, band_last = where[0], where[1], where[2], where[3]
    for a, (field, dst) in enumerate(zip((f0, f1, f2, f3, f4), scratch)):
        for i in range(tiles):
            if i == 0:
                ref, rows = above, slice(a * HALO, a * HALO + 8)
            elif i == tiles - 1:
                ref, rows = below, slice(a * HALO, a * HALO + 8)
            else:
                ref, rows = field, slice(8 * i - 8, 8 * i)
            strip = a * tiles + i
            v, off = strip // 16, (strip % 16) * 8
            x = east[8 * v : 8 * v + 8, :]
            y = west[8 * v : 8 * v + 8, :]
            x = pltpu.roll(x, LANES - off, 1) if off else x
            y = pltpu.roll(y, (LANES - 8 - off) % LANES, 1) if (LANES - 8 - off) % LANES else y
            edge = jnp.where(lane1 < 8, x, jnp.where(lane1 >= LANES - 8, y, 0.0))
            body = ref[rows, :]
            if a == 2:
                body, edge = rate * body, rate * edge
            dst[8 * i : 8 * i + 8, :width] = body
            dst[8 * i : 8 * i + 8, width:] = edge
    lane = iota((8, wide), 1)
    sub = iota((8, wide), 0)
    shut_e = ((lane == width - 1) & (tile_index == tile_last)) | ((lane == wide - 1) & (tile_index == 0))
    ce = jnp.where(shut_e, 0.0, rate / CELL_WIDTH)
    shut_n = (sub == 7) & (band_index == 0)
    shut_s = (sub == 7) & (band_index == band_last)
    cs_first = jnp.where(shut_n, 0.0, rate / CELL_WIDTH)
    cs_last = jnp.where(shut_s, 0.0, rate / CELL_WIDTH)
    nxt = bed_s[0:8, :]
    nxt_up = pltpu.roll(nxt, 7, 0)
    for i in range(tiles):
        rows = slice(8 * i, 8 * i + 8)
        bed, up = nxt, nxt_up
        if i + 1 < tiles:
            nxt = bed_s[8 * i + 8 : 8 * i + 16, :]
            nxt_up = pltpu.roll(nxt, 7, 0)
        mbe_s[rows, :] = jnp.maximum(bed, pltpu.roll(bed, wide - 1, 1))
        mbs_s[rows, :] = jnp.maximum(bed, jnp.where(sub == 7, nxt_up, up))
        qe_s[rows, :] = jnp.where(shut_e, 0.0, qe_s[rows, :])
    last = slice(height, height + 8)
    qs_s[last, :] = jnp.where(shut_s, 0.0, qs_s[last, :])

    def face(here, ahead, bed_max, rough, old, factor):
        depth = jnp.maximum(jnp.maximum(here, ahead) - bed_max, DEPTH_FLOOR)
        drag = rough * jnp.abs(old) * jnp.exp(-FRICTION_POWER * jnp.log(depth)) + 1.0
        near = pl.reciprocal(drag, approx=True)
        near = near * (2.0 - drag * near)
        return (old - factor * depth * (ahead - here)) * near

    def substep(_, carry):
        nxt = level_s[0:8, :]
        nxt_up = pltpu.roll(nxt, 7, 0)
        north_turned = jnp.zeros((8, wide), F32)
        for i in range(tiles):
            rows = slice(8 * i, 8 * i + 8)
            level, up = nxt, nxt_up
            if i + 1 < tiles:
                nxt = level_s[8 * i + 8 : 8 * i + 16, :]
                nxt_up = pltpu.roll(nxt, 7, 0)
            rough = rough_s[rows, :]
            cs = cs_first if i == 0 else cs_last if i == tiles - 2 else rate / CELL_WIDTH
            qe = face(level, pltpu.roll(level, wide - 1, 1), mbe_s[rows, :], rough, qe_s[rows, :], ce)
            below_level = jnp.where(sub == 7, nxt_up, up)
            qs = face(level, below_level, mbs_s[rows, :], rough, qs_s[rows, :], cs)
            qe_s[rows, :] = qe
            qs_s[rows, :] = qs
            turned = pltpu.roll(qs, 1, 0)
            north = jnp.where(sub == 0, north_turned, turned)
            north_turned = turned
            gained = pltpu.roll(qe, 1, 1) - qe + north - qs
            level_s[rows, :] = level + (TIME_STEP / CELL_WIDTH) * gained
        return carry

    lax.fori_loop(0, SUBSTEPS, substep, 0)
    inner = slice(HALO, HALO + height)
    water_out[...] = level_s[inner, :width] - bed_s[inner, :width]
    east_out[...] = qe_s[inner, :width]
    south_out[...] = qs_s[inner, :width]


def shaped(*shape):
    return jax.ShapeDtypeStruct(shape, F32)


def call(kernel, out_shape, specs, scratch=(), flops=0, size=0, exps=0):
    return pl.pallas_call(
        kernel,
        out_shape=out_shape,
        in_specs=specs,
        out_specs=jax.tree.map(lambda _: VMEM, out_shape),
        scratch_shapes=list(scratch),
        compiler_params=pltpu.CompilerParams(vmem_limit_bytes=40 * 1024 * 1024),
        cost_estimate=pl.CostEstimate(flops=flops, bytes_accessed=size, transcendentals=exps),
        name=kernel.__name__,
    )


def per_device(
    water_depth, flux_east, flux_south, bed_level, roughness, link_rows, link_blocks,
    reach_inverse, reach_source, river_section, block_level, block_down,
):
    tiles = lax.axis_size("tile")
    bands = lax.axis_size("band")
    tile_index = lax.axis_index("tile")
    band_index = lax.axis_index("band")
    height, width = water_depth.shape
    blocks, reach = reach_source.shape
    total = tiles * CHUNK
    links = link_rows.shape[-1]
    where = jnp.stack(
        [tile_index, band_index, jnp.int32(tiles - 1), jnp.int32(bands - 1)]
    ).astype(jnp.int32)
    ring = [[(i, (i + k) % bands) for i in range(bands)] for k in range(bands)]

    down = block_down.reshape(1, blocks)
    payload, slots, tables, last_row = call(
        pack_kernel,
        (shaped(tiles * SLOTS, LANES), shaped(8, links), shaped(tiles * bands, LANES), shaped(blocks, reach)),
        [HBM] * 5 + [VMEM],
        scratch=[
            pltpu.VMEM((height, width), F32),
            pltpu.VMEM((height, width), F32),
            pltpu.VMEM((1, links), jnp.int32),
            pltpu.VMEM((1, links), jnp.int32),
            pltpu.VMEM((blocks, 16, reach), BF16),
            pltpu.VMEM((8, LANES), F32),
            pltpu.SemaphoreType.DMA((5,)),
        ],
        flops=10**9,
        size=10**6,
    )(water_depth, bed_level, link_rows.reshape(1, links), link_blocks.reshape(1, links), reach_inverse, down)
    rows_in = lax.all_to_all(
        payload.reshape(tiles, SLOTS, LANES), "tile", split_axis=0, concat_axis=0, tiled=True
    )
    tables_in = lax.all_to_all(
        tables.reshape(tiles * bands, 1, LANES), ("tile", "band"), split_axis=0, concat_axis=0, tiled=True
    )

    fields = (bed_level + water_depth, bed_level, roughness, flux_east, flux_south)
    top = jnp.concatenate([f[:HALO] for f in fields], axis=0)
    bottom = jnp.concatenate([f[height - HALO :] for f in fields], axis=0)
    above = lax.ppermute(bottom, "band", [(i, i + 1) for i in range(bands - 1)])
    below = lax.ppermute(top, "band", [(i + 1, i) for i in range(bands - 1)])
    left, right = call(
        strips_kernel, (shaped(48, LANES), shaped(48, LANES)), [VMEM] * 7, flops=10**6, size=10**6
    )(above, below, *fields)
    west = lax.ppermute(right, "tile", [(i, i + 1) for i in range(tiles - 1)])
    east = lax.ppermute(left, "tile", [(i + 1, i) for i in range(tiles - 1)])

    column_down = jnp.broadcast_to(block_down.astype(F32)[None, :], (8, blocks))
    answer, source = call(
        river_kernel,
        (shaped(total, LANES), shaped(blocks, LANES)),
        [SMEM] + [VMEM] * 6 + [ANY],
        flops=10**9,
        size=10**6,
    )(
        where,
        rows_in.reshape(tiles * SLOTS, LANES),
        tables_in.reshape(tiles * bands, LANES),
        river_section,
        reach_source,
        last_row,
        column_down,
        left,
    )
    returned = lax.all_to_all(
        answer.reshape(tiles, CHUNK, 1, LANES), "tile", split_axis=0, concat_axis=0, tiled=True
    )

    wide = width + LANES
    tall = height + 2 * HALO
    water_now, final_east, final_south = call(
        flood_kernel,
        (shaped(height, width),) * 3,
        [SMEM] + [VMEM] * 9,
        scratch=[pltpu.VMEM((tall, wide), F32)] * 7,
        flops=10**8,
        size=10**7,
        exps=10**7,
    )(where, above, below, west, east, *fields)
    base_flow, column = call(
        flow_kernel, (shaped(blocks, reach),) * 2, [VMEM] * 2, flops=10**8, size=10**6
    )(source, reach_inverse)

    pushed = jnp.sum(returned.reshape(tiles, CHUNK, LANES)[:, SLOTS, :], axis=0, keepdims=True)
    parts = [pushed] + [lax.ppermute(pushed, "band", ring[k]) for k in (1, 2, 3)]
    final_depth = call(
        final_kernel, shaped(height, width), [VMEM] * 3, flops=10**9, size=10**6
    )(water_now, returned.reshape(total, LANES), slots)
    inflow = lax.dynamic_slice_in_dim(sum(parts)[0], band_index * blocks, blocks)
    discharge = base_flow + column * inflow[:, None]
    return (final_depth, final_east, final_south, discharge)


def solution(mesh):
    grid = P("band", "tile")
    owned = P(("tile", "band"))
    lists = P("tile", "band", None)
    return jax.shard_map(
        per_device,
        mesh=mesh,
        in_specs=(grid,) * 5 + (lists,) * 2 + (owned,) * 5,
        out_specs=(grid, grid, grid, owned),
        check_vma=False,
    )
```

```python
import functools

import jax
import jax.numpy as jnp
from jax import lax
from jax.experimental import pallas as pl
from jax.experimental.pallas import tpu as pltpu
from jax.sharding import PartitionSpec as P

SUBSTEPS = 8
LEVELS = 8
HALO = 8
LANES = 128
SLOTS = 16
CHUNK = SLOTS + 1
GAIN_LANE = 64
ID_LANE = 96

GRAVITY = 9.81
TIME_STEP = 3.0
CELL_WIDTH = 30.0
DEPTH_FLOOR = 0.2
FRICTION_POWER = 7.0 / 3.0
LATERAL_RATE = 0.2
PLAIN_SHARE = 0.8
RIVER_SHARE = 0.25

F32 = jnp.float32
BF16 = jnp.bfloat16
VMEM = pl.BlockSpec(memory_space=pltpu.VMEM)
SMEM = pl.BlockSpec(memory_space=pltpu.SMEM)
HBM = pl.BlockSpec(memory_space=pltpu.HBM)
ANY = pl.BlockSpec(memory_space=pl.ANY)


def iota(shape, dim):
    return lax.broadcasted_iota(jnp.int32, shape, dim)


def halves(x):
    hi = x.astype(BF16)
    lo = (x - hi.astype(F32)).astype(BF16)
    return hi, lo


def paired(x):
    hi, lo = halves(x)
    return jnp.concatenate([hi, lo], axis=1)


def fold(x):
    return x[:, :LANES] + x[:, LANES:]


def mm(a, b, dims=((1,), (0,))):
    return lax.dot_general(a, b, (dims, ((), ())), preferred_element_type=F32)


def pack_kernel(
    water_h, bed_h, rows_h, blocks_h, inverse_h, down,
    out, slots, last_out,
    water, bed, link_rows, link_blocks, tails, row_s, sems,
):
    blocks_own, reach = last_out.shape
    moves = (
        (rows_h, link_rows),
        (blocks_h, link_blocks),
        (water_h, water),
        (bed_h, bed),
        (inverse_h.at[:, reach - 16 : reach, :], tails),
    )
    copies = [pltpu.make_async_copy(src, dst, sems.at[i]) for i, (src, dst) in enumerate(moves)]
    for copy in copies:
        copy.start()
    copies[0].wait()
    copies[1].wait()
    rows = link_rows[...]
    blocks = link_blocks[...]
    links = rows.shape[1]
    height = water.shape[0]
    groups = water.shape[1] // LANES
    tiles = out.shape[0] // CHUNK
    place = ((rows % groups) * height + rows // groups).astype(F32)
    dest = (blocks >> 7).astype(F32)
    local = (blocks & 31).astype(F32)
    pick = iota((8, links), 0)
    stacked = jnp.where(pick == 0, place, jnp.where(pick == 1, dest, local))
    turned = jnp.transpose(stacked)
    place_c, dest_c, local_c = turned[:, 0:1], turned[:, 1:2], turned[:, 2:3]
    earlier = (dest_c == dest) & (iota((links, links), 1) < iota((links, links), 0))
    ones = jnp.ones((links, LANES), BF16)
    rank = mm(earlier.astype(F32).astype(BF16), ones)
    position = dest_c * float(CHUNK) + rank
    position_c = position[:, 0:1]
    lane = iota((links, links), 1).astype(F32)
    slot_of = jnp.sum(jnp.where(place_c == lane, position_c, 0.0), axis=0, keepdims=True)
    slots[...] = jnp.broadcast_to(slot_of, slots.shape)
    copies[2].wait()
    copies[3].wait()
    level = water[...] + bed[...]
    by_block = jnp.concatenate(
        [level[:, c * LANES : (c + 1) * LANES] for c in range(groups)], axis=0
    )
    by_block = paired(by_block)
    step = 8 * CHUNK
    for start in range(0, out.shape[0], step):
        hot = (iota((step, links), 0) + start).astype(F32) == slot_of
        out[start : start + step, :] = fold(mm(hot.astype(F32).astype(BF16), by_block))
    dest_hot = (iota((tiles, links), 0).astype(F32) == dest).astype(F32).astype(BF16)
    seat = iota((links, LANES), 1).astype(F32) - float(ID_LANE)
    rank_hot = jnp.where(rank == seat, local_c + 1.0, 0.0)
    ids = mm(dest_hot, rank_hot.astype(BF16))
    copies[4].wait()
    last = tails[:, 15, :].astype(F32)
    last_out[...] = last
    first = (iota((8, reach), 1) == 0).astype(F32).astype(BF16)
    seated = jnp.concatenate(
        [jnp.zeros((GAIN_LANE, reach), F32), last, jnp.zeros((LANES - GAIN_LANE - blocks_own, reach), F32)],
        axis=0,
    )
    gain = mm(first, seated.astype(BF16), ((1,), (1,)))
    row_s[...] = jnp.zeros(row_s.shape, F32)
    row_s[0:1, 0:blocks_own] = down[...].astype(F32)
    out[pl.ds(SLOTS, tiles, CHUNK), :] = ids + (row_s[0:1, :] + gain[0:1, :])


def lateral_kernel(rows_in, section, reach_source, last_row, order, out, source):
    total = rows_in.shape[0]
    tiles = total // CHUNK
    blocks = section.shape[0]
    slot = iota((total, 1), 0).astype(F32)
    owner = jnp.floor((slot + 0.5) * (1.0 / CHUNK))
    within = slot - owner * CHUNK + ID_LANE
    lane = iota((total, LANES), 1).astype(F32)
    extras = rows_in[pl.ds(SLOTS, tiles, CHUNK), :]
    ids_here = iota((tiles, LANES), 1)
    ids_here = (ids_here >= ID_LANE) & (ids_here < ID_LANE + SLOTS)
    ids = jnp.where(ids_here, extras, 0.0).astype(BF16)
    spread = (iota((total, tiles), 1).astype(F32) == owner).astype(F32).astype(BF16)
    seat = jnp.where(lane == within, mm(spread, ids), 0.0)
    block = mm(seat.astype(BF16), jnp.ones((LANES, LANES), BF16)) - 1.0
    hot = (block == lane).astype(F32).astype(BF16)
    section_in = fold(mm(hot[:, :blocks], paired(section[...])))
    lateral = jnp.where(block >= 0.0, LATERAL_RATE * (rows_in[...] - section_in), 0.0)
    out[...] = lateral
    sums = fold(mm(hot, paired(lateral), ((0,), (0,))))[:blocks]
    src = reach_source[...] + RIVER_SHARE * sums
    source[...] = src
    ends = jnp.concatenate([src * last_row[...], jnp.zeros((LANES - blocks, LANES), F32)], axis=0)
    ends_hi, ends_lo = halves(ends)
    ones = jnp.ones((8, LANES), BF16)
    row = mm(ones, ends_hi, ((1,), (1,))) + mm(ones, ends_lo, ((1,), (1,)))
    out[pl.ds(SLOTS, tiles, CHUNK), :] = jnp.broadcast_to(row[0:1, :], (tiles, LANES))


def dense(ref, blocks, start, step, count):
    turns = LANES // blocks
    group = iota((count // turns, LANES), 1) // blocks
    rows = jnp.zeros((count // turns, LANES), F32)
    for turn in range(turns):
        x = ref[pl.ds(start + turn * step, count // turns, turns * step), :]
        x = pltpu.roll(x, turn * blocks, 1) if turn else x
        rows = jnp.where(group == turn, x, rows)
    return rows


def paths_kernel(where, own, one, two, three, reach):
    bands = 4
    band, me = where[1], where[0].astype(F32) + 1.0
    tiles = own.shape[0]
    blocks = LANES // bands
    group = iota((tiles, LANES), 1) // blocks
    downs = jnp.zeros((tiles, LANES), F32)
    gains = jnp.zeros((tiles, LANES), F32)
    for back, ref in enumerate((own, one, two, three)):
        here = group == (band + bands - back) % bands
        x = ref[...]
        down, gain = x, x
        for turn in (1, 2, 3):
            y = pltpu.roll(x, turn * blocks, 1)
            down = jnp.where(group == turn, y, down)
            gain = jnp.where(group == (turn + GAIN_LANE // blocks) % bands, y, gain)
        downs = jnp.where(here, down, downs)
        gains = jnp.where(here, gain, gains)
    high = jnp.floor(downs * (1.0 / LANES))
    parts = (high + 1.0, downs - high * LANES, gains)
    tables = jnp.concatenate([jnp.transpose(x) for x in parts], axis=0).astype(BF16)
    sources = dense(own, blocks, 0, 1, tiles)
    chunks = sources.shape[0]
    high = jnp.floor(sources * (1.0 / LANES))
    low = sources - high * LANES
    high = high + 1.0
    tile_row = iota((tiles, LANES), 0).astype(F32) + 1.0
    block_row = iota((LANES, LANES), 0).astype(F32)
    state = [(high[i : i + 1], low[i : i + 1], jnp.ones((1, LANES), F32)) for i in range(chunks)]
    for hop in range(LEVELS - 1):
        for i, (hi, lo, factor) in enumerate(state):
            cols = slice(i * LANES, (i + 1) * LANES)
            hit = block_row == lo
            mine = jnp.where(hit, jnp.where(hi == me, factor, 0.0), 0.0)
            reach[:, cols] = mine if hop == 0 else reach[:, cols] + mine
            if hop < LEVELS - 2:
                found = mm(tables, (tile_row == hi).astype(F32).astype(BF16))
                next_hi = jnp.sum(jnp.where(hit, found[:LANES], 0.0), axis=0, keepdims=True)
                next_lo = jnp.sum(jnp.where(hit, found[LANES : 2 * LANES], 0.0), axis=0, keepdims=True)
                gain = jnp.sum(jnp.where(hit, found[2 * LANES :], 0.0), axis=0, keepdims=True)
                state[i] = (next_hi, next_lo, factor * gain)


def gather_kernel(returned, reach, out):
    tiles = returned.shape[0] // CHUNK
    blocks = reach.shape[1] // tiles
    ends = dense(returned, blocks, SLOTS, CHUNK, tiles)
    total = jnp.zeros((LANES, LANES), F32)
    for i in range(ends.shape[0]):
        total = total + reach[:, i * LANES : (i + 1) * LANES] * ends[i : i + 1, :]
    hi, lo = halves(total)
    ones = jnp.ones((8, LANES), BF16)
    out[...] = mm(ones, hi, ((1,), (1,))) + mm(ones, lo, ((1,), (1,)))


def flow_kernel(source, inverse, base, column):
    blocks = source.shape[0]
    hi, lo = halves(source[...])
    first = (iota((blocks, LANES), 1) == 0).astype(F32).astype(BF16)
    stacked = jnp.concatenate([hi, lo, first], axis=0)
    row = iota((blocks, LANES), 0)
    base_now = jnp.zeros((blocks, LANES), F32)
    column_now = jnp.zeros((blocks, LANES), F32)
    for g in range(blocks):
        x = mm(stacked, inverse[g], ((1,), (1,)))
        base_now = jnp.where(row == g, x[:blocks] + x[blocks : 2 * blocks], base_now)
        column_now = jnp.where(row == g, x[2 * blocks :], column_now)
    base[...] = base_now
    column[...] = column_now


def final_kernel(water, returned, slots, out):
    total = returned.shape[0]
    height = water.shape[0]
    groups = water.shape[1] // LANES
    slot_c = jnp.transpose(slots[...])[:, 0:1]
    rows = paired(returned[...])
    for c in range(groups):
        mine = slot_c[c * height : (c + 1) * height]
        hot = (iota((height, total), 1).astype(F32) == mine).astype(F32).astype(BF16)
        lateral = fold(mm(hot, rows))
        cols = slice(c * LANES, (c + 1) * LANES)
        out[:, cols] = water[:, cols] - PLAIN_SHARE * lateral


def strips_kernel(above, below, f0, f1, f2, f3, f4, left, right):
    fields = (f0, f1, f2, f3, f4)
    height, width = f0.shape
    tiles = height // 8 + 2
    lane = iota((8, LANES), 1)
    groups = left.shape[0] // 8
    lefts = [jnp.zeros((8, LANES), F32) for _ in range(groups)]
    rights = [jnp.zeros((8, LANES), F32) for _ in range(groups)]
    for a, field in enumerate(fields):
        for i in range(tiles):
            if i == 0:
                ref, rows = above, slice(a * HALO, a * HALO + 8)
            elif i == tiles - 1:
                ref, rows = below, slice(a * HALO, a * HALO + 8)
            else:
                ref, rows = field, slice(8 * i - 8, 8 * i)
            strip = a * tiles + i
            v, off = strip // 16, (strip % 16) * 8
            here = (lane >= off) & (lane < off + 8)
            x = ref[rows, 0:LANES]
            y = ref[rows, width - LANES : width]
            x = pltpu.roll(x, off, 1) if off else x
            y = pltpu.roll(y, (off + 8) % LANES, 1) if (off + 8) % LANES else y
            lefts[v] = jnp.where(here, x, lefts[v])
            rights[v] = jnp.where(here, y, rights[v])
    for v in range(groups):
        left[8 * v : 8 * v + 8, :] = lefts[v]
        right[8 * v : 8 * v + 8, :] = rights[v]


def flood_kernel(
    where, above, below, west, east, f0, f1, f2, f3, f4,
    water_out, east_out, south_out,
    level_s, bed_s, rough_s, qe_s, qs_s, mbe_s, mbs_s,
):
    height, width = f0.shape
    tiles = height // 8 + 2
    wide = width + LANES
    lane1 = iota((8, LANES), 1)
    scratch = (level_s, bed_s, rough_s, qe_s, qs_s)
    rate = GRAVITY * TIME_STEP
    tile_index, band_index, tile_last, band_last = where[0], where[1], where[2], where[3]
    for a, (field, dst) in enumerate(zip((f0, f1, f2, f3, f4), scratch)):
        for i in range(tiles):
            if i == 0:
                ref, rows = above, slice(a * HALO, a * HALO + 8)
            elif i == tiles - 1:
                ref, rows = below, slice(a * HALO, a * HALO + 8)
            else:
                ref, rows = field, slice(8 * i - 8, 8 * i)
            strip = a * tiles + i
            v, off = strip // 16, (strip % 16) * 8
            x = east[8 * v : 8 * v + 8, :]
            y = west[8 * v : 8 * v + 8, :]
            x = pltpu.roll(x, LANES - off, 1) if off else x
            y = pltpu.roll(y, (LANES - 8 - off) % LANES, 1) if (LANES - 8 - off) % LANES else y
            edge = jnp.where(lane1 < 8, x, jnp.where(lane1 >= LANES - 8, y, 0.0))
            body = ref[rows, :]
            if a == 2:
                body, edge = rate * body, rate * edge
            dst[8 * i : 8 * i + 8, :width] = body
            dst[8 * i : 8 * i + 8, width:] = edge
    lane = iota((8, wide), 1)
    sub = iota((8, wide), 0)
    shut_e = ((lane == width - 1) & (tile_index == tile_last)) | ((lane == wide - 1) & (tile_index == 0))
    ce = jnp.where(shut_e, 0.0, rate / CELL_WIDTH)
    shut_n = (sub == 7) & (band_index == 0)
    shut_s = (sub == 7) & (band_index == band_last)
    cs_first = jnp.where(shut_n, 0.0, rate / CELL_WIDTH)
    cs_last = jnp.where(shut_s, 0.0, rate / CELL_WIDTH)
    nxt = bed_s[0:8, :]
    nxt_up = pltpu.roll(nxt, 7, 0)
    for i in range(tiles):
        rows = slice(8 * i, 8 * i + 8)
        bed, up = nxt, nxt_up
        if i + 1 < tiles:
            nxt = bed_s[8 * i + 8 : 8 * i + 16, :]
            nxt_up = pltpu.roll(nxt, 7, 0)
        mbe_s[rows, :] = jnp.maximum(bed, pltpu.roll(bed, wide - 1, 1))
        mbs_s[rows, :] = jnp.maximum(bed, jnp.where(sub == 7, nxt_up, up))
        qe_s[rows, :] = jnp.where(shut_e, 0.0, qe_s[rows, :])
    last = slice(height, height + 8)
    qs_s[last, :] = jnp.where(shut_s, 0.0, qs_s[last, :])

    def face(here, ahead, bed_max, rough, old, factor):
        depth = jnp.maximum(jnp.maximum(here, ahead) - bed_max, DEPTH_FLOOR)
        drag = rough * jnp.abs(old) * jnp.exp(-FRICTION_POWER * jnp.log(depth)) + 1.0
        near = pl.reciprocal(drag, approx=True)
        near = near * (2.0 - drag * near)
        return (old - factor * depth * (ahead - here)) * near

    def substep(_, carry):
        nxt = level_s[0:8, :]
        nxt_up = pltpu.roll(nxt, 7, 0)
        north_turned = jnp.zeros((8, wide), F32)
        for i in range(tiles):
            rows = slice(8 * i, 8 * i + 8)
            level, up = nxt, nxt_up
            if i + 1 < tiles:
                nxt = level_s[8 * i + 8 : 8 * i + 16, :]
                nxt_up = pltpu.roll(nxt, 7, 0)
            rough = rough_s[rows, :]
            cs = cs_first if i == 0 else cs_last if i == tiles - 2 else rate / CELL_WIDTH
            qe = face(level, pltpu.roll(level, wide - 1, 1), mbe_s[rows, :], rough, qe_s[rows, :], ce)
            below_level = jnp.where(sub == 7, nxt_up, up)
            qs = face(level, below_level, mbs_s[rows, :], rough, qs_s[rows, :], cs)
            qe_s[rows, :] = qe
            qs_s[rows, :] = qs
            turned = pltpu.roll(qs, 1, 0)
            north = jnp.where(sub == 0, north_turned, turned)
            north_turned = turned
            gained = pltpu.roll(qe, 1, 1) - qe + north - qs
            level_s[rows, :] = level + (TIME_STEP / CELL_WIDTH) * gained
        return carry

    lax.fori_loop(0, SUBSTEPS, substep, 0)
    inner = slice(HALO, HALO + height)
    water_out[...] = level_s[inner, :width] - bed_s[inner, :width]
    east_out[...] = qe_s[inner, :width]
    south_out[...] = qs_s[inner, :width]


def shaped(*shape):
    return jax.ShapeDtypeStruct(shape, F32)


def call(kernel, out_shape, specs, scratch=(), flops=0, size=0, exps=0):
    return pl.pallas_call(
        kernel,
        out_shape=out_shape,
        in_specs=specs,
        out_specs=jax.tree.map(lambda _: VMEM, out_shape),
        scratch_shapes=list(scratch),
        compiler_params=pltpu.CompilerParams(vmem_limit_bytes=40 * 1024 * 1024),
        cost_estimate=pl.CostEstimate(flops=flops, bytes_accessed=size, transcendentals=exps),
        name=kernel.__name__,
    )


def per_device(
    water_depth, flux_east, flux_south, bed_level, roughness, link_rows, link_blocks,
    reach_inverse, reach_source, river_section, block_level, block_down,
):
    tiles = lax.axis_size("tile")
    bands = lax.axis_size("band")
    tile_index = lax.axis_index("tile")
    band_index = lax.axis_index("band")
    height, width = water_depth.shape
    blocks, reach = reach_source.shape
    total = tiles * CHUNK
    links = link_rows.shape[-1]
    where = jnp.stack(
        [tile_index, band_index, jnp.int32(tiles - 1), jnp.int32(bands - 1)]
    ).astype(jnp.int32)
    ring = [[(i, (i + k) % bands) for i in range(bands)] for k in range(bands)]

    down = block_down.reshape(1, blocks)
    payload, slots, last_row = call(
        pack_kernel,
        (shaped(total, LANES), shaped(8, links), shaped(blocks, reach)),
        [HBM] * 5 + [VMEM],
        scratch=[
            pltpu.VMEM((height, width), F32),
            pltpu.VMEM((height, width), F32),
            pltpu.VMEM((1, links), jnp.int32),
            pltpu.VMEM((1, links), jnp.int32),
            pltpu.VMEM((blocks, 16, reach), BF16),
            pltpu.VMEM((8, LANES), F32),
            pltpu.SemaphoreType.DMA((5,)),
        ],
        flops=10**9,
        size=10**6,
    )(water_depth, bed_level, link_rows.reshape(1, links), link_blocks.reshape(1, links), reach_inverse, down)
    rows_in = lax.all_to_all(
        payload.reshape(tiles, CHUNK, 1, LANES), "tile", split_axis=0, concat_axis=0, tiled=True
    )

    fields = (bed_level + water_depth, bed_level, roughness, flux_east, flux_south)
    top = jnp.concatenate([f[:HALO] for f in fields], axis=0)
    bottom = jnp.concatenate([f[height - HALO :] for f in fields], axis=0)
    above = lax.ppermute(bottom, "band", [(i, i + 1) for i in range(bands - 1)])
    below = lax.ppermute(top, "band", [(i + 1, i) for i in range(bands - 1)])
    left, right = call(
        strips_kernel, (shaped(48, LANES), shaped(48, LANES)), [VMEM] * 7, flops=10**6, size=10**6
    )(above, below, *fields)
    west = lax.ppermute(right, "tile", [(i, i + 1) for i in range(tiles - 1)])
    east = lax.ppermute(left, "tile", [(i + 1, i) for i in range(tiles - 1)])

    answer, source = call(
        lateral_kernel,
        (shaped(total, LANES), shaped(blocks, LANES)),
        [VMEM] * 4 + [ANY],
        flops=10**9,
        size=10**6,
    )(rows_in.reshape(total, LANES), river_section, reach_source, last_row, west)
    returned = lax.all_to_all(
        answer.reshape(tiles, CHUNK, 1, LANES), "tile", split_axis=0, concat_axis=0, tiled=True
    )

    wide = width + LANES
    tall = height + 2 * HALO
    water_now, final_east, final_south = call(
        flood_kernel,
        (shaped(height, width),) * 3,
        [SMEM] + [VMEM] * 9,
        scratch=[pltpu.VMEM((tall, wide), F32)] * 7,
        flops=10**8,
        size=10**7,
        exps=10**7,
    )(where, above, below, west, east, *fields)
    base_flow, column = call(
        flow_kernel, (shaped(blocks, reach),) * 2, [VMEM] * 2, flops=10**8, size=10**6
    )(source, reach_inverse)
    extras = rows_in.reshape(tiles, CHUNK, LANES)[:, SLOTS, :]
    others = [lax.ppermute(extras, "band", ring[k]) for k in (1, 2, 3)]
    reached = call(
        paths_kernel, shaped(LANES, tiles * blocks), [SMEM] + [VMEM] * 4, flops=10**9, size=10**6
    )(where, extras, *others)

    pushed = call(gather_kernel, shaped(8, LANES), [VMEM] * 2, flops=10**6, size=10**6)(
        returned.reshape(total, LANES), reached
    )[0:1]
    parts = [pushed] + [lax.ppermute(pushed, "band", ring[k]) for k in (1, 2, 3)]
    final_depth = call(
        final_kernel, shaped(height, width), [VMEM] * 3, flops=10**9, size=10**6
    )(water_now, returned.reshape(total, LANES), slots)
    inflow = lax.dynamic_slice_in_dim(sum(parts)[0], band_index * blocks, blocks)
    discharge = base_flow + column * inflow[:, None]
    return (final_depth, final_east, final_south, discharge)


def solution(mesh):
    grid = P("band", "tile")
    owned = P(("tile", "band"))
    lists = P("tile", "band", None)
    return jax.shard_map(
        per_device,
        mesh=mesh,
        in_specs=(grid,) * 5 + (lists,) * 2 + (owned,) * 5,
        out_specs=(grid, grid, grid, owned),
        check_vma=False,
    )
```

```python
import functools

import jax
import jax.numpy as jnp
from jax import lax
from jax.experimental import pallas as pl
from jax.experimental.pallas import tpu as pltpu
from jax.sharding import PartitionSpec as P

SUBSTEPS = 8
LEVELS = 8
HALO = 8
LANES = 128
SLOTS = 16
CHUNK = SLOTS + 1
GAIN_LANE = 64
ID_LANE = 96

GRAVITY = 9.81
TIME_STEP = 3.0
CELL_WIDTH = 30.0
DEPTH_FLOOR = 0.2
FRICTION_POWER = 7.0 / 3.0
LATERAL_RATE = 0.2
PLAIN_SHARE = 0.8
RIVER_SHARE = 0.25

F32 = jnp.float32
BF16 = jnp.bfloat16
VMEM = pl.BlockSpec(memory_space=pltpu.VMEM)
SMEM = pl.BlockSpec(memory_space=pltpu.SMEM)
HBM = pl.BlockSpec(memory_space=pltpu.HBM)
ANY = pl.BlockSpec(memory_space=pl.ANY)


def iota(shape, dim):
    return lax.broadcasted_iota(jnp.int32, shape, dim)


def halves(x):
    hi = x.astype(BF16)
    lo = (x - hi.astype(F32)).astype(BF16)
    return hi, lo


def paired(x):
    hi, lo = halves(x)
    return jnp.concatenate([hi, lo], axis=1)


def fold(x):
    return x[:, :LANES] + x[:, LANES:]


def mm(a, b, dims=((1,), (0,))):
    return lax.dot_general(a, b, (dims, ((), ())), preferred_element_type=F32)


def pack_kernel(
    water_h, bed_h, rows_h, blocks_h, inverse_h, rough_h, east_h, south_h, down,
    out, slots, last_out, top, bottom,
    water, bed, link_rows, link_blocks, tails, row_s, sems,
):
    blocks_own, reach = last_out.shape
    moves = (
        (rows_h, link_rows),
        (blocks_h, link_blocks),
        (water_h, water),
        (bed_h, bed),
        (inverse_h.at[:, reach - 16 : reach, :], tails),
    )
    height = water.shape[0]
    for a, field in enumerate((rough_h, east_h, south_h)):
        rows = pl.ds((a + 2) * HALO, HALO)
        moves += (
            (field.at[0:HALO, :], top.at[rows, :]),
            (field.at[height - HALO : height, :], bottom.at[rows, :]),
        )
    copies = [pltpu.make_async_copy(src, dst, sems.at[i]) for i, (src, dst) in enumerate(moves)]
    for copy in copies:
        copy.start()
    copies[0].wait()
    copies[1].wait()
    rows = link_rows[...]
    blocks = link_blocks[...]
    links = rows.shape[1]
    groups = water.shape[1] // LANES
    tiles = out.shape[0] // CHUNK
    place = ((rows % groups) * height + rows // groups).astype(F32)
    dest = (blocks >> 7).astype(F32)
    local = (blocks & 31).astype(F32)
    pick = iota((8, links), 0)
    stacked = jnp.where(pick == 0, place, jnp.where(pick == 1, dest, local))
    turned = jnp.transpose(stacked)
    place_c, dest_c, local_c = turned[:, 0:1], turned[:, 1:2], turned[:, 2:3]
    earlier = (dest_c == dest) & (iota((links, links), 1) < iota((links, links), 0))
    ones = jnp.ones((links, LANES), BF16)
    rank = mm(earlier.astype(F32).astype(BF16), ones)
    position = dest_c * float(CHUNK) + rank
    position_c = position[:, 0:1]
    lane = iota((links, links), 1).astype(F32)
    slot_of = jnp.sum(jnp.where(place_c == lane, position_c, 0.0), axis=0, keepdims=True)
    slots[...] = jnp.broadcast_to(slot_of, slots.shape)
    copies[2].wait()
    copies[3].wait()
    level = water[...] + bed[...]
    top[0:HALO, :] = level[:HALO]
    top[HALO : 2 * HALO, :] = bed[0:HALO, :]
    bottom[0:HALO, :] = level[height - HALO :]
    bottom[HALO : 2 * HALO, :] = bed[height - HALO : height, :]
    by_block = jnp.concatenate(
        [level[:, c * LANES : (c + 1) * LANES] for c in range(groups)], axis=0
    )
    by_block = paired(by_block)
    step = 8 * CHUNK
    for start in range(0, out.shape[0], step):
        hot = (iota((step, links), 0) + start).astype(F32) == slot_of
        out[start : start + step, :] = fold(mm(hot.astype(F32).astype(BF16), by_block))
    dest_hot = (iota((tiles, links), 0).astype(F32) == dest).astype(F32).astype(BF16)
    seat = iota((links, LANES), 1).astype(F32) - float(ID_LANE)
    rank_hot = jnp.where(rank == seat, local_c + 1.0, 0.0)
    ids = mm(dest_hot, rank_hot.astype(BF16))
    copies[4].wait()
    last = tails[:, 15, :].astype(F32)
    last_out[...] = last
    first = (iota((8, reach), 1) == 0).astype(F32).astype(BF16)
    seated = jnp.concatenate(
        [jnp.zeros((GAIN_LANE, reach), F32), last, jnp.zeros((LANES - GAIN_LANE - blocks_own, reach), F32)],
        axis=0,
    )
    gain = mm(first, seated.astype(BF16), ((1,), (1,)))
    row_s[...] = jnp.zeros(row_s.shape, F32)
    row_s[0:1, 0:blocks_own] = down[...].astype(F32)
    out[pl.ds(SLOTS, tiles, CHUNK), :] = ids + (row_s[0:1, :] + gain[0:1, :])
    for copy in copies[5:]:
        copy.wait()


def lateral_kernel(rows_in, section, reach_source, last_row, order0, order1, out, source):
    total = rows_in.shape[0]
    tiles = total // CHUNK
    blocks = section.shape[0]
    slot = iota((total, 1), 0).astype(F32)
    owner = jnp.floor((slot + 0.5) * (1.0 / CHUNK))
    within = slot - owner * CHUNK + ID_LANE
    lane = iota((total, LANES), 1).astype(F32)
    extras = rows_in[pl.ds(SLOTS, tiles, CHUNK), :]
    ids_here = iota((tiles, LANES), 1)
    ids_here = (ids_here >= ID_LANE) & (ids_here < ID_LANE + SLOTS)
    ids = jnp.where(ids_here, extras, 0.0).astype(BF16)
    spread = (iota((total, tiles), 1).astype(F32) == owner).astype(F32).astype(BF16)
    seat = jnp.where(lane == within, mm(spread, ids), 0.0)
    block = mm(seat.astype(BF16), jnp.ones((LANES, LANES), BF16)) - 1.0
    hot = (block == lane).astype(F32).astype(BF16)
    section_in = fold(mm(hot[:, :blocks], paired(section[...])))
    lateral = jnp.where(block >= 0.0, LATERAL_RATE * (rows_in[...] - section_in), 0.0)
    out[...] = lateral
    sums = fold(mm(hot, paired(lateral), ((0,), (0,))))[:blocks]
    src = reach_source[...] + RIVER_SHARE * sums
    source[...] = src
    ends = jnp.concatenate([src * last_row[...], jnp.zeros((LANES - blocks, LANES), F32)], axis=0)
    ends_hi, ends_lo = halves(ends)
    ones = jnp.ones((8, LANES), BF16)
    row = mm(ones, ends_hi, ((1,), (1,))) + mm(ones, ends_lo, ((1,), (1,)))
    out[pl.ds(SLOTS, tiles, CHUNK), :] = jnp.broadcast_to(row[0:1, :], (tiles, LANES))


def dense(ref, blocks, start, step, count):
    turns = LANES // blocks
    group = iota((count // turns, LANES), 1) // blocks
    rows = jnp.zeros((count // turns, LANES), F32)
    for turn in range(turns):
        x = ref[pl.ds(start + turn * step, count // turns, turns * step), :]
        x = pltpu.roll(x, turn * blocks, 1) if turn else x
        rows = jnp.where(group == turn, x, rows)
    return rows


def paths_kernel(where, own, one, two, three, reach):
    bands = 4
    band, me = where[1], where[0].astype(F32) + 1.0
    tiles = own.shape[0]
    blocks = LANES // bands
    group = iota((tiles, LANES), 1) // blocks
    downs = jnp.zeros((tiles, LANES), F32)
    gains = jnp.zeros((tiles, LANES), F32)
    for back, ref in enumerate((own, one, two, three)):
        here = group == (band + bands - back) % bands
        x = ref[...]
        down, gain = x, x
        for turn in (1, 2, 3):
            y = pltpu.roll(x, turn * blocks, 1)
            down = jnp.where(group == turn, y, down)
            gain = jnp.where(group == (turn + GAIN_LANE // blocks) % bands, y, gain)
        downs = jnp.where(here, down, downs)
        gains = jnp.where(here, gain, gains)
    high = jnp.floor(downs * (1.0 / LANES))
    tables = jnp.concatenate([high + 1.0, downs - high * LANES, gains], axis=0).astype(BF16)
    sources = dense(own, blocks, 0, 1, tiles)
    chunks = sources.shape[0]
    high = jnp.floor(sources * (1.0 / LANES))
    low = sources - high * LANES
    high = high + 1.0
    tile_row = iota((tiles, LANES), 0).astype(F32) + 1.0
    block_row = iota((LANES, LANES), 0).astype(F32)
    state = [(high[i : i + 1], low[i : i + 1], jnp.ones((1, LANES), F32)) for i in range(chunks)]
    for hop in range(LEVELS - 1):
        for i in range(0, chunks, 2):
            hits = [block_row == state[k][1] for k in (i, i + 1)]
            if hop < LEVELS - 2:
                hot = jnp.concatenate([jnp.where(hit, 1.0, 0.0).astype(BF16) for hit in hits], axis=1)
                founds = mm(tables, hot)
            for k, hit in zip((i, i + 1), hits):
                hi, lo, factor = state[k]
                cols = slice(k * LANES, (k + 1) * LANES)
                mine = jnp.where(hit, jnp.where(hi == me, factor, 0.0), 0.0)
                reach[:, cols] = mine if hop == 0 else reach[:, cols] + mine
                if hop < LEVELS - 2:
                    found = founds[:, (k - i) * LANES : (k - i + 1) * LANES]
                    here = tile_row == hi
                    picks = [
                        jnp.sum(jnp.where(here, found[p * tiles : (p + 1) * tiles], 0.0), axis=0, keepdims=True)
                        for p in range(3)
                    ]
                    state[k] = (picks[0], picks[1], factor * picks[2])


def gather_kernel(returned, reach, out):
    tiles = returned.shape[0] // CHUNK
    blocks = reach.shape[1] // tiles
    ends = dense(returned, blocks, SLOTS, CHUNK, tiles)
    total = jnp.zeros((LANES, LANES), F32)
    for i in range(ends.shape[0]):
        total = total + reach[:, i * LANES : (i + 1) * LANES] * ends[i : i + 1, :]
    hi, lo = halves(total)
    ones = jnp.ones((8, LANES), BF16)
    out[...] = mm(ones, hi, ((1,), (1,))) + mm(ones, lo, ((1,), (1,)))


def flow_kernel(source, inverse, base, column):
    blocks = source.shape[0]
    hi, lo = halves(source[...])
    first = (iota((blocks, LANES), 1) == 0).astype(F32).astype(BF16)
    stacked = jnp.concatenate([hi, lo, first], axis=0)
    row = iota((blocks, LANES), 0)
    base_now = jnp.zeros((blocks, LANES), F32)
    column_now = jnp.zeros((blocks, LANES), F32)
    for g in range(blocks):
        x = mm(stacked, inverse[g], ((1,), (1,)))
        base_now = jnp.where(row == g, x[:blocks] + x[blocks : 2 * blocks], base_now)
        column_now = jnp.where(row == g, x[2 * blocks :], column_now)
    base[...] = base_now
    column[...] = column_now


def final_kernel(water, returned, slots, out):
    total = returned.shape[0]
    height = water.shape[0]
    groups = water.shape[1] // LANES
    slot_c = jnp.transpose(slots[...])[:, 0:1]
    rows = paired(returned[...])
    for c in range(groups):
        mine = slot_c[c * height : (c + 1) * height]
        hot = (iota((height, total), 1).astype(F32) == mine).astype(F32).astype(BF16)
        lateral = fold(mm(hot, rows))
        cols = slice(c * LANES, (c + 1) * LANES)
        out[:, cols] = water[:, cols] - PLAIN_SHARE * lateral


def strips_kernel(above, below, f0, f1, f2, f3, f4, left, right):
    fields = (f0, f1, f2, f3, f4)
    height, width = f0.shape
    tiles = height // 8 + 2
    lane = iota((8, LANES), 1)
    groups = left.shape[0] // 8
    lefts = [jnp.zeros((8, LANES), F32) for _ in range(groups)]
    rights = [jnp.zeros((8, LANES), F32) for _ in range(groups)]
    for a, field in enumerate(fields):
        for i in range(tiles):
            if i == 0:
                ref, rows = above, slice(a * HALO, a * HALO + 8)
            elif i == tiles - 1:
                ref, rows = below, slice(a * HALO, a * HALO + 8)
            else:
                ref, rows = field, slice(8 * i - 8, 8 * i)
            strip = a * tiles + i
            v, off = strip // 16, (strip % 16) * 8
            here = (lane >= off) & (lane < off + 8)
            x = ref[rows, 0:LANES]
            y = ref[rows, width - LANES : width]
            if ref is f0:
                x = x + f1[rows, 0:LANES]
                y = y + f1[rows, width - LANES : width]
            x = pltpu.roll(x, off, 1) if off else x
            y = pltpu.roll(y, (off + 8) % LANES, 1) if (off + 8) % LANES else y
            lefts[v] = jnp.where(here, x, lefts[v])
            rights[v] = jnp.where(here, y, rights[v])
    for v in range(groups):
        left[8 * v : 8 * v + 8, :] = lefts[v]
        right[8 * v : 8 * v + 8, :] = rights[v]


def flood_kernel(
    where, above, below, west, east, f0, f1, f2, f3, f4,
    water_out, east_out, south_out,
    level_s, bed_s, rough_s, qe_s, qs_s, mbe_s, mbs_s,
):
    height, width = f0.shape
    tiles = height // 8 + 2
    wide = width + LANES
    lane1 = iota((8, LANES), 1)
    scratch = (level_s, bed_s, rough_s, qe_s, qs_s)
    share = TIME_STEP / CELL_WIDTH
    rate = GRAVITY * TIME_STEP
    slope_rate = share * rate / CELL_WIDTH
    tile_index, band_index, tile_last, band_last = where[0], where[1], where[2], where[3]
    for a, (field, dst) in enumerate(zip((f0, f1, f2, f3, f4), scratch)):
        for i in range(tiles):
            if i == 0:
                ref, rows = above, slice(a * HALO, a * HALO + 8)
            elif i == tiles - 1:
                ref, rows = below, slice(a * HALO, a * HALO + 8)
            else:
                ref, rows = field, slice(8 * i - 8, 8 * i)
            strip = a * tiles + i
            v, off = strip // 16, (strip % 16) * 8
            x = east[8 * v : 8 * v + 8, :]
            y = west[8 * v : 8 * v + 8, :]
            x = pltpu.roll(x, LANES - off, 1) if off else x
            y = pltpu.roll(y, (LANES - 8 - off) % LANES, 1) if (LANES - 8 - off) % LANES else y
            edge = jnp.where(lane1 < 8, x, jnp.where(lane1 >= LANES - 8, y, 0.0))
            body = ref[rows, :]
            if ref is f0:
                body = body + f1[rows, :]
            if a >= 2:
                scale = rate / share if a == 2 else share
                body, edge = scale * body, scale * edge
            dst[8 * i : 8 * i + 8, :width] = body
            dst[8 * i : 8 * i + 8, width:] = edge
    lane = iota((8, wide), 1)
    sub = iota((8, wide), 0)
    shut_e = ((lane == width - 1) & (tile_index == tile_last)) | ((lane == wide - 1) & (tile_index == 0))
    ce = jnp.where(shut_e, 0.0, slope_rate)
    shut_n = (sub == 7) & (band_index == 0)
    shut_s = (sub == 7) & (band_index == band_last)
    cs_first = jnp.where(shut_n, 0.0, slope_rate)
    cs_last = jnp.where(shut_s, 0.0, slope_rate)
    nxt = bed_s[0:8, :]
    nxt_up = pltpu.roll(nxt, 7, 0)
    for i in range(tiles):
        rows = slice(8 * i, 8 * i + 8)
        bed, up = nxt, nxt_up
        if i + 1 < tiles:
            nxt = bed_s[8 * i + 8 : 8 * i + 16, :]
            nxt_up = pltpu.roll(nxt, 7, 0)
        mbe_s[rows, :] = jnp.maximum(bed, pltpu.roll(bed, wide - 1, 1))
        mbs_s[rows, :] = jnp.maximum(bed, jnp.where(sub == 7, nxt_up, up))
        qe_s[rows, :] = jnp.where(shut_e, 0.0, qe_s[rows, :])
    last = slice(height, height + 8)
    qs_s[last, :] = jnp.where(shut_s, 0.0, qs_s[last, :])

    def face(here, ahead, bed_max, rough, old, factor):
        depth = jnp.maximum(jnp.maximum(here, ahead) - bed_max, DEPTH_FLOOR)
        drag = rough * jnp.abs(old) * jnp.exp2(-FRICTION_POWER * jnp.log2(depth)) + 1.0
        near = pl.reciprocal(drag, approx=True)
        return (old - factor * depth * (ahead - here)) * near

    def substep(_, carry):
        nxt = level_s[0:8, :]
        nxt_up = pltpu.roll(nxt, 7, 0)
        north_turned = jnp.zeros((8, wide), F32)
        for i in range(tiles):
            rows = slice(8 * i, 8 * i + 8)
            level, up = nxt, nxt_up
            if i + 1 < tiles:
                nxt = level_s[8 * i + 8 : 8 * i + 16, :]
                nxt_up = pltpu.roll(nxt, 7, 0)
            rough = rough_s[rows, :]
            cs = cs_first if i == 0 else cs_last if i == tiles - 2 else slope_rate
            qe = face(level, pltpu.roll(level, wide - 1, 1), mbe_s[rows, :], rough, qe_s[rows, :], ce)
            below_level = jnp.where(sub == 7, nxt_up, up)
            qs = face(level, below_level, mbs_s[rows, :], rough, qs_s[rows, :], cs)
            qe_s[rows, :] = qe
            qs_s[rows, :] = qs
            turned = pltpu.roll(qs, 1, 0)
            north = jnp.where(sub == 0, north_turned, turned)
            north_turned = turned
            gained = pltpu.roll(qe, 1, 1) - qe + north - qs
            level_s[rows, :] = level + gained
        return carry

    lax.fori_loop(0, SUBSTEPS, substep, 0)
    inner = slice(HALO, HALO + height)
    water_out[...] = level_s[inner, :width] - bed_s[inner, :width]
    east_out[...] = (1.0 / share) * qe_s[inner, :width]
    south_out[...] = (1.0 / share) * qs_s[inner, :width]


def shaped(*shape):
    return jax.ShapeDtypeStruct(shape, F32)


def call(kernel, out_shape, specs, scratch=(), flops=0, size=0, exps=0, limit=40 * 1024 * 1024):
    return pl.pallas_call(
        kernel,
        out_shape=out_shape,
        in_specs=specs,
        out_specs=jax.tree.map(lambda _: VMEM, out_shape),
        scratch_shapes=list(scratch),
        compiler_params=pltpu.CompilerParams(vmem_limit_bytes=limit),
        cost_estimate=pl.CostEstimate(flops=flops, bytes_accessed=size, transcendentals=exps),
        name=kernel.__name__,
    )


def per_device(
    water_depth, flux_east, flux_south, bed_level, roughness, link_rows, link_blocks,
    reach_inverse, reach_source, river_section, block_level, block_down,
):
    tiles = lax.axis_size("tile")
    bands = lax.axis_size("band")
    tile_index = lax.axis_index("tile")
    band_index = lax.axis_index("band")
    height, width = water_depth.shape
    blocks, reach = reach_source.shape
    total = tiles * CHUNK
    links = link_rows.shape[-1]
    where = jnp.stack(
        [tile_index, band_index, jnp.int32(tiles - 1), jnp.int32(bands - 1)]
    ).astype(jnp.int32)
    ring = [[(i, (i + k) % bands) for i in range(bands)] for k in range(bands)]

    down = block_down.reshape(1, blocks)
    edge = shaped(5 * HALO, width)
    payload, slots, last_row, top, bottom = call(
        pack_kernel,
        (shaped(total, LANES), shaped(8, links), shaped(blocks, reach), edge, edge),
        [HBM] * 8 + [VMEM],
        scratch=[
            pltpu.VMEM((height, width), F32),
            pltpu.VMEM((height, width), F32),
            pltpu.VMEM((1, links), jnp.int32),
            pltpu.VMEM((1, links), jnp.int32),
            pltpu.VMEM((blocks, 16, reach), BF16),
            pltpu.VMEM((8, LANES), F32),
            pltpu.SemaphoreType.DMA((11,)),
        ],
        limit=None,
        flops=10**9,
        size=10**6,
    )(
        water_depth,
        bed_level,
        link_rows.reshape(1, links),
        link_blocks.reshape(1, links),
        reach_inverse,
        roughness,
        flux_east,
        flux_south,
        down,
    )
    rows_in = lax.all_to_all(
        payload.reshape(tiles, CHUNK, 1, LANES), "tile", split_axis=0, concat_axis=0, tiled=True
    )

    fields = (water_depth, bed_level, roughness, flux_east, flux_south)
    above = lax.ppermute(bottom, "band", [(i, i + 1) for i in range(bands - 1)])
    below = lax.ppermute(top, "band", [(i + 1, i) for i in range(bands - 1)])
    left, right = call(
        strips_kernel, (shaped(48, LANES), shaped(48, LANES)), [VMEM] * 7, flops=10**6, size=10**6
    )(above, below, *fields)
    west = lax.ppermute(right, "tile", [(i, i + 1) for i in range(tiles - 1)])
    east = lax.ppermute(left, "tile", [(i + 1, i) for i in range(tiles - 1)])

    answer, source = call(
        lateral_kernel,
        (shaped(total, LANES), shaped(blocks, LANES)),
        [VMEM] * 4 + [ANY] * 2,
        flops=10**9,
        size=10**6,
    )(rows_in.reshape(total, LANES), river_section, reach_source, last_row, west, east)
    returned = lax.all_to_all(
        answer.reshape(tiles, CHUNK, 1, LANES), "tile", split_axis=0, concat_axis=0, tiled=True
    )

    wide = width + LANES
    tall = height + 2 * HALO
    water_now, final_east, final_south = call(
        flood_kernel,
        (shaped(height, width),) * 3,
        [SMEM] + [VMEM] * 9,
        scratch=[pltpu.VMEM((tall, wide), F32)] * 7,
        flops=10**8,
        size=10**7,
        exps=10**7,
    )(where, above, below, west, east, *fields)
    base_flow, column = call(
        flow_kernel, (shaped(blocks, reach),) * 2, [VMEM] * 2, flops=10**8, size=10**6
    )(source, reach_inverse)
    extras = rows_in.reshape(tiles, CHUNK, LANES)[:, SLOTS, :]
    others = [lax.ppermute(extras, "band", ring[k]) for k in (1, 2, 3)]
    reached = call(
        paths_kernel, shaped(LANES, tiles * blocks), [SMEM] + [VMEM] * 4, flops=10**9, size=10**6
    )(where, extras, *others)

    pushed = call(gather_kernel, shaped(8, LANES), [VMEM] * 2, flops=10**6, size=10**6)(
        returned.reshape(total, LANES), reached
    )
    parts = [pushed] + [lax.ppermute(pushed, "band", ring[k]) for k in (1, 2, 3)]
    final_depth = call(
        final_kernel, shaped(height, width), [VMEM] * 3, flops=10**9, size=10**6
    )(water_now, returned.reshape(total, LANES), slots)
    inflow = lax.dynamic_slice_in_dim(sum(parts)[0], band_index * blocks, blocks)
    discharge = base_flow + column * inflow[:, None]
    return (final_depth, final_east, final_south, discharge)


def solution(mesh):
    grid = P("band", "tile")
    owned = P(("tile", "band"))
    lists = P("tile", "band", None)
    return jax.shard_map(
        per_device,
        mesh=mesh,
        in_specs=(grid,) * 5 + (lists,) * 2 + (owned,) * 5,
        out_specs=(grid, grid, grid, owned),
        check_vma=False,
    )
```

```python
import functools

import jax
import jax.numpy as jnp
from jax import lax
from jax.experimental import pallas as pl
from jax.experimental.pallas import tpu as pltpu
from jax.sharding import PartitionSpec as P

SUBSTEPS = 8
LEVELS = 8
HALO = 8
LANES = 128
SLOTS = 16
CHUNK = SLOTS + 1
GAIN_LANE = 64
ID_LANE = 96

GRAVITY = 9.81
TIME_STEP = 3.0
CELL_WIDTH = 30.0
DEPTH_FLOOR = 0.2
FRICTION_POWER = 7.0 / 3.0
LATERAL_RATE = 0.2
PLAIN_SHARE = 0.8
RIVER_SHARE = 0.25

F32 = jnp.float32
BF16 = jnp.bfloat16
VMEM = pl.BlockSpec(memory_space=pltpu.VMEM)
SMEM = pl.BlockSpec(memory_space=pltpu.SMEM)
HBM = pl.BlockSpec(memory_space=pltpu.HBM)
ANY = pl.BlockSpec(memory_space=pl.ANY)


def iota(shape, dim):
    return lax.broadcasted_iota(jnp.int32, shape, dim)


def halves(x):
    hi = x.astype(BF16)
    lo = (x - hi.astype(F32)).astype(BF16)
    return hi, lo


def paired(x):
    hi, lo = halves(x)
    return jnp.concatenate([hi, lo], axis=1)


def fold(x):
    return x[:, :LANES] + x[:, LANES:]


def mm(a, b, dims=((1,), (0,))):
    return lax.dot_general(a, b, (dims, ((), ())), preferred_element_type=F32)


def pack_kernel(
    water_h, bed_h, rows_h, blocks_h, inverse_h, rough_h, east_h, south_h, down,
    out, slots, last_out, edge_a, edge_b,
    water, bed, link_rows, link_blocks, tails, row_s, sems,
):
    blocks_own, reach = last_out.shape
    moves = (
        (rows_h, link_rows),
        (blocks_h, link_blocks),
        (water_h, water),
        (bed_h, bed),
        (inverse_h.at[:, reach - 16 : reach, :], tails),
    )
    height = water.shape[0]
    odd = lax.axis_index("band") % 2
    start_a = pl.multiple_of((1 - odd) * (height - HALO), HALO)
    start_b = pl.multiple_of(odd * (height - HALO), HALO)
    for a, field in enumerate((rough_h, east_h, south_h)):
        rows = pl.ds((a + 2) * HALO, HALO)
        moves += (
            (field.at[pl.ds(start_a, HALO), :], edge_a.at[rows, :]),
            (field.at[pl.ds(start_b, HALO), :], edge_b.at[rows, :]),
        )
    copies = [pltpu.make_async_copy(src, dst, sems.at[i]) for i, (src, dst) in enumerate(moves)]
    for copy in copies:
        copy.start()
    copies[0].wait()
    copies[1].wait()
    rows = link_rows[...]
    blocks = link_blocks[...]
    links = rows.shape[1]
    groups = water.shape[1] // LANES
    tiles = out.shape[0] // CHUNK
    place = ((rows % groups) * height + rows // groups).astype(F32)
    dest = (blocks >> 7).astype(F32)
    local = (blocks & 31).astype(F32)
    pick = iota((8, links), 0)
    stacked = jnp.where(pick == 0, place, jnp.where(pick == 1, dest, local))
    turned = jnp.transpose(stacked)
    place_c, dest_c, local_c = turned[:, 0:1], turned[:, 1:2], turned[:, 2:3]
    earlier = (dest_c == dest) & (iota((links, links), 1) < iota((links, links), 0))
    ones = jnp.ones((links, LANES), BF16)
    rank = mm(earlier.astype(F32).astype(BF16), ones)
    position = dest_c * float(CHUNK) + rank
    position_c = position[:, 0:1]
    lane = iota((links, links), 1).astype(F32)
    slot_of = jnp.sum(jnp.where(place_c == lane, position_c, 0.0), axis=0, keepdims=True)
    slots[...] = jnp.broadcast_to(slot_of, slots.shape)
    copies[2].wait()
    copies[3].wait()
    level = water[...] + bed[...]
    for edge, start in ((edge_a, start_a), (edge_b, start_b)):
        edge[HALO : 2 * HALO, :] = bed[pl.ds(start, HALO), :]
        edge[0:HALO, :] = water[pl.ds(start, HALO), :] + bed[pl.ds(start, HALO), :]
    by_block = jnp.concatenate(
        [level[:, c * LANES : (c + 1) * LANES] for c in range(groups)], axis=0
    )
    by_block = paired(by_block)
    hot = iota((out.shape[0], links), 0).astype(F32) == slot_of
    out[...] = fold(mm(jnp.where(hot, 1.0, 0.0).astype(BF16), by_block))
    dest_hot = (iota((tiles, links), 0).astype(F32) == dest).astype(F32).astype(BF16)
    seat = iota((links, LANES), 1).astype(F32) - float(ID_LANE)
    rank_hot = jnp.where(rank == seat, local_c + 1.0, 0.0)
    ids = mm(dest_hot, rank_hot.astype(BF16))
    copies[4].wait()
    last = tails[:, 15, :].astype(F32)
    last_out[...] = last
    first = (iota((8, reach), 1) == 0).astype(F32).astype(BF16)
    seated = jnp.concatenate(
        [jnp.zeros((GAIN_LANE, reach), F32), last, jnp.zeros((LANES - GAIN_LANE - blocks_own, reach), F32)],
        axis=0,
    )
    gain = mm(first, seated.astype(BF16), ((1,), (1,)))
    row_s[...] = jnp.zeros(row_s.shape, F32)
    row_s[0:1, 0:blocks_own] = down[...].astype(F32)
    out[pl.ds(SLOTS, tiles, CHUNK), :] = ids + (row_s[0:1, :] + gain[0:1, :])
    for copy in copies[5:]:
        copy.wait()


def lateral_kernel(rows_in, section, reach_source, last_row, order0, order1, out, source):
    total = rows_in.shape[0]
    tiles = total // CHUNK
    blocks = section.shape[0]
    slot = iota((total, 1), 0).astype(F32)
    owner = jnp.floor((slot + 0.5) * (1.0 / CHUNK))
    within = slot - owner * CHUNK + ID_LANE
    lane = iota((total, LANES), 1).astype(F32)
    extras = rows_in[pl.ds(SLOTS, tiles, CHUNK), :]
    ids_here = iota((tiles, LANES), 1)
    ids_here = (ids_here >= ID_LANE) & (ids_here < ID_LANE + SLOTS)
    ids = jnp.where(ids_here, extras, 0.0).astype(BF16)
    spread = (iota((total, tiles), 1).astype(F32) == owner).astype(F32).astype(BF16)
    seat = jnp.where(lane == within, mm(spread, ids), 0.0)
    block = mm(seat.astype(BF16), jnp.ones((LANES, LANES), BF16)) - 1.0
    hot = (block == lane).astype(F32).astype(BF16)
    section_in = fold(mm(hot[:, :blocks], paired(section[...])))
    lateral = jnp.where(block >= 0.0, LATERAL_RATE * (rows_in[...] - section_in), 0.0)
    out[...] = lateral
    sums = fold(mm(hot, paired(lateral), ((0,), (0,))))[:blocks]
    src = reach_source[...] + RIVER_SHARE * sums
    source[...] = src
    ends = jnp.concatenate([src * last_row[...], jnp.zeros((LANES - blocks, LANES), F32)], axis=0)
    ends_hi, ends_lo = halves(ends)
    ones = jnp.ones((8, LANES), BF16)
    row = mm(ones, ends_hi, ((1,), (1,))) + mm(ones, ends_lo, ((1,), (1,)))
    out[pl.ds(SLOTS, tiles, CHUNK), :] = jnp.broadcast_to(row[0:1, :], (tiles, LANES))


def dense(ref, blocks, start, step, count):
    turns = LANES // blocks
    group = iota((count // turns, LANES), 1) // blocks
    rows = jnp.zeros((count // turns, LANES), F32)
    for turn in range(turns):
        x = ref[pl.ds(start + turn * step, count // turns, turns * step), :]
        x = pltpu.roll(x, turn * blocks, 1) if turn else x
        rows = jnp.where(group == turn, x, rows)
    return rows


def paths_kernel(where, own, one, two, three, reach):
    bands = 4
    band, me = where[1], where[0].astype(F32) + 1.0
    tiles = own.shape[0]
    blocks = LANES // bands
    group = iota((tiles, LANES), 1) // blocks
    downs = jnp.zeros((tiles, LANES), F32)
    gains = jnp.zeros((tiles, LANES), F32)
    for back, ref in enumerate((own, one, two, three)):
        here = group == band ^ back
        x = ref[...]
        down, gain = x, x
        for turn in (1, 2, 3):
            y = pltpu.roll(x, turn * blocks, 1)
            down = jnp.where(group == turn, y, down)
            gain = jnp.where(group == (turn + GAIN_LANE // blocks) % bands, y, gain)
        downs = jnp.where(here, down, downs)
        gains = jnp.where(here, gain, gains)
    high = jnp.floor(downs * (1.0 / LANES))
    tables = jnp.concatenate([high + 1.0, downs - high * LANES, gains], axis=0).astype(BF16)
    sources = dense(own, blocks, 0, 1, tiles)
    chunks = sources.shape[0]
    high = jnp.floor(sources * (1.0 / LANES))
    low = sources - high * LANES
    high = high + 1.0
    tile_row = iota((tiles, LANES), 0).astype(F32) + 1.0
    block_row = iota((LANES, LANES), 0).astype(F32)
    state = [(high[i : i + 1], low[i : i + 1], jnp.ones((1, LANES), F32)) for i in range(chunks)]
    for hop in range(LEVELS - 1):
        for i in range(0, chunks, 2):
            hits = [block_row == state[k][1] for k in (i, i + 1)]
            if hop < LEVELS - 2:
                hot = jnp.concatenate([jnp.where(hit, 1.0, 0.0).astype(BF16) for hit in hits], axis=1)
                founds = mm(tables, hot)
            for k, hit in zip((i, i + 1), hits):
                hi, lo, factor = state[k]
                cols = slice(k * LANES, (k + 1) * LANES)
                mine = jnp.where(hit, jnp.where(hi == me, factor, 0.0), 0.0)
                reach[:, cols] = mine if hop == 0 else reach[:, cols] + mine
                if hop < LEVELS - 2:
                    found = founds[:, (k - i) * LANES : (k - i + 1) * LANES]
                    here = tile_row == hi
                    picks = [
                        jnp.sum(jnp.where(here, found[p * tiles : (p + 1) * tiles], 0.0), axis=0, keepdims=True)
                        for p in range(3)
                    ]
                    state[k] = (picks[0], picks[1], factor * picks[2])


def gather_kernel(returned, reach, out):
    tiles = returned.shape[0] // CHUNK
    blocks = reach.shape[1] // tiles
    ends = dense(returned, blocks, SLOTS, CHUNK, tiles)
    total = jnp.zeros((LANES, LANES), F32)
    for i in range(ends.shape[0]):
        total = total + reach[:, i * LANES : (i + 1) * LANES] * ends[i : i + 1, :]
    hi, lo = halves(total)
    ones = jnp.ones((8, LANES), BF16)
    out[...] = mm(ones, hi, ((1,), (1,))) + mm(ones, lo, ((1,), (1,)))


def flow_kernel(source, inverse, base, column):
    blocks = source.shape[0]
    hi, lo = halves(source[...])
    first = (iota((blocks, LANES), 1) == 0).astype(F32).astype(BF16)
    stacked = jnp.concatenate([hi, lo, first], axis=0)
    row = iota((blocks, LANES), 0)
    base_now = jnp.zeros((blocks, LANES), F32)
    column_now = jnp.zeros((blocks, LANES), F32)
    for g in range(blocks):
        x = mm(stacked, inverse[g], ((1,), (1,)))
        base_now = jnp.where(row == g, x[:blocks] + x[blocks : 2 * blocks], base_now)
        column_now = jnp.where(row == g, x[2 * blocks :], column_now)
    base[...] = base_now
    column[...] = column_now


def final_kernel(water, returned, slots, out):
    total = returned.shape[0]
    height = water.shape[0]
    groups = water.shape[1] // LANES
    slot_c = jnp.transpose(slots[...])[:, 0:1]
    rows = paired(returned[...])
    hot = iota((height * groups, total), 1).astype(F32) == slot_c
    lateral = fold(mm(jnp.where(hot, 1.0, 0.0).astype(BF16), rows))
    for c in range(groups):
        cols = slice(c * LANES, (c + 1) * LANES)
        out[:, cols] = water[:, cols] - PLAIN_SHARE * lateral[c * height : (c + 1) * height]


def strips_kernel(where, got_a, got_b, f0, f1, f2, f3, f4, side_a, side_b):
    fields = (f0, f1, f2, f3, f4)
    height, width = f0.shape
    tiles = height // 8 + 2
    lane = iota((8, LANES), 1)
    groups = side_a.shape[0] // 8
    odd_band, odd_tile = where[1] % 2 == 1, where[0] % 2 == 1
    lefts = [jnp.zeros((8, LANES), F32) for _ in range(groups)]
    rights = [jnp.zeros((8, LANES), F32) for _ in range(groups)]
    for a, field in enumerate(fields):
        for i in range(tiles):
            strip = a * tiles + i
            v, off = strip // 16, (strip % 16) * 8
            here = (lane >= off) & (lane < off + 8)
            first, last = slice(0, LANES), slice(width - LANES, width)
            if i in (0, tiles - 1):
                rows = slice(a * HALO, a * HALO + 8)
                from_a = odd_band if i == 0 else jnp.logical_not(odd_band)
                x = jnp.where(from_a, got_a[rows, first], got_b[rows, first])
                y = jnp.where(from_a, got_a[rows, last], got_b[rows, last])
            else:
                rows = slice(8 * i - 8, 8 * i)
                x, y = field[rows, first], field[rows, last]
                if a == 0:
                    x, y = x + f1[rows, first], y + f1[rows, last]
            x = pltpu.roll(x, off, 1) if off else x
            y = pltpu.roll(y, (off + 8) % LANES, 1) if (off + 8) % LANES else y
            lefts[v] = jnp.where(here, x, lefts[v])
            rights[v] = jnp.where(here, y, rights[v])
    for v in range(groups):
        side_a[8 * v : 8 * v + 8, :] = jnp.where(odd_tile, lefts[v], rights[v])
        side_b[8 * v : 8 * v + 8, :] = jnp.where(odd_tile, rights[v], lefts[v])


def flood_kernel(
    where, got_a, got_b, col_a, col_b, f0, f1, f2, f3, f4,
    water_out, east_out, south_out,
    level_s, bed_s, rough_s, qe_s, qs_s, mbe_s, mbs_s,
):
    height, width = f0.shape
    tiles = height // 8 + 2
    wide = width + LANES
    lane1 = iota((8, LANES), 1)
    scratch = (level_s, bed_s, rough_s, qe_s, qs_s)
    share = TIME_STEP / CELL_WIDTH
    rate = GRAVITY * TIME_STEP
    slope_rate = share * rate / CELL_WIDTH
    tile_index, band_index, tile_last, band_last = where[0], where[1], where[2], where[3]
    odd_band, odd_tile = band_index % 2 == 1, tile_index % 2 == 1
    easts, wests = [], []
    for v in range(col_a.shape[0] // 8):
        x, y = col_a[8 * v : 8 * v + 8, :], col_b[8 * v : 8 * v + 8, :]
        easts.append(jnp.where(odd_tile, y, x))
        wests.append(jnp.where(odd_tile, x, y))
    for a, (field, dst) in enumerate(zip((f0, f1, f2, f3, f4), scratch)):
        for i in range(tiles):
            strip = a * tiles + i
            v, off = strip // 16, (strip % 16) * 8
            x, y = easts[v], wests[v]
            x = pltpu.roll(x, LANES - off, 1) if off else x
            y = pltpu.roll(y, (LANES - 8 - off) % LANES, 1) if (LANES - 8 - off) % LANES else y
            edge = jnp.where(lane1 < 8, x, jnp.where(lane1 >= LANES - 8, y, 0.0))
            if i in (0, tiles - 1):
                rows = slice(a * HALO, a * HALO + 8)
                from_a = odd_band if i == 0 else jnp.logical_not(odd_band)
                body = jnp.where(from_a, got_a[rows, :], got_b[rows, :])
            else:
                rows = slice(8 * i - 8, 8 * i)
                body = field[rows, :]
                if a == 0:
                    body = body + f1[rows, :]
            if a >= 2:
                scale = rate / share if a == 2 else share
                body, edge = scale * body, scale * edge
            dst[8 * i : 8 * i + 8, :width] = body
            dst[8 * i : 8 * i + 8, width:] = edge
    lane = iota((8, wide), 1)
    sub = iota((8, wide), 0)
    shut_e = ((lane == width - 1) & (tile_index == tile_last)) | ((lane == wide - 1) & (tile_index == 0))
    ce = jnp.where(shut_e, 0.0, slope_rate)
    shut_n = (sub == 7) & (band_index == 0)
    shut_s = (sub == 7) & (band_index == band_last)
    cs_first = jnp.where(shut_n, 0.0, slope_rate)
    cs_last = jnp.where(shut_s, 0.0, slope_rate)
    nxt = bed_s[0:8, :]
    nxt_up = pltpu.roll(nxt, 7, 0)
    for i in range(tiles):
        rows = slice(8 * i, 8 * i + 8)
        bed, up = nxt, nxt_up
        if i + 1 < tiles:
            nxt = bed_s[8 * i + 8 : 8 * i + 16, :]
            nxt_up = pltpu.roll(nxt, 7, 0)
        mbe_s[rows, :] = jnp.maximum(bed, pltpu.roll(bed, wide - 1, 1))
        mbs_s[rows, :] = jnp.maximum(bed, jnp.where(sub == 7, nxt_up, up))
        qe_s[rows, :] = jnp.where(shut_e, 0.0, qe_s[rows, :])
    last = slice(height, height + 8)
    qs_s[last, :] = jnp.where(shut_s, 0.0, qs_s[last, :])

    def face(here, ahead, bed_max, rough, old, factor):
        depth = jnp.maximum(jnp.maximum(here, ahead) - bed_max, DEPTH_FLOOR)
        drag = rough * jnp.abs(old) * jnp.exp2(-FRICTION_POWER * jnp.log2(depth)) + 1.0
        near = pl.reciprocal(drag, approx=True)
        return (old - factor * depth * (ahead - here)) * near

    def substep(_, carry):
        nxt = level_s[0:8, :]
        nxt_up = pltpu.roll(nxt, 7, 0)
        north_turned = jnp.zeros((8, wide), F32)
        for i in range(tiles):
            rows = slice(8 * i, 8 * i + 8)
            level, up = nxt, nxt_up
            if i + 1 < tiles:
                nxt = level_s[8 * i + 8 : 8 * i + 16, :]
                nxt_up = pltpu.roll(nxt, 7, 0)
            rough = rough_s[rows, :]
            cs = cs_first if i == 0 else cs_last if i == tiles - 2 else slope_rate
            qe = face(level, pltpu.roll(level, wide - 1, 1), mbe_s[rows, :], rough, qe_s[rows, :], ce)
            below_level = jnp.where(sub == 7, nxt_up, up)
            qs = face(level, below_level, mbs_s[rows, :], rough, qs_s[rows, :], cs)
            qe_s[rows, :] = qe
            qs_s[rows, :] = qs
            turned = pltpu.roll(qs, 1, 0)
            north = jnp.where(sub == 0, north_turned, turned)
            north_turned = turned
            gained = pltpu.roll(qe, 1, 1) - qe + north - qs
            level_s[rows, :] = level + gained
        return carry

    lax.fori_loop(0, SUBSTEPS, substep, 0)
    inner = slice(HALO, HALO + height)
    water_out[...] = level_s[inner, :width] - bed_s[inner, :width]
    east_out[...] = (1.0 / share) * qe_s[inner, :width]
    south_out[...] = (1.0 / share) * qs_s[inner, :width]


def shaped(*shape):
    return jax.ShapeDtypeStruct(shape, F32)


def call(kernel, out_shape, specs, scratch=(), flops=0, size=0, exps=0, limit=40 * 1024 * 1024):
    return pl.pallas_call(
        kernel,
        out_shape=out_shape,
        in_specs=specs,
        out_specs=jax.tree.map(lambda _: VMEM, out_shape),
        scratch_shapes=list(scratch),
        compiler_params=pltpu.CompilerParams(vmem_limit_bytes=limit),
        cost_estimate=pl.CostEstimate(flops=flops, bytes_accessed=size, transcendentals=exps),
        name=kernel.__name__,
    )


def per_device(
    water_depth, flux_east, flux_south, bed_level, roughness, link_rows, link_blocks,
    reach_inverse, reach_source, river_section, block_level, block_down,
):
    tiles = lax.axis_size("tile")
    bands = lax.axis_size("band")
    tile_index = lax.axis_index("tile")
    band_index = lax.axis_index("band")
    height, width = water_depth.shape
    blocks, reach = reach_source.shape
    total = tiles * CHUNK
    links = link_rows.shape[-1]
    where = jnp.stack(
        [tile_index, band_index, jnp.int32(tiles - 1), jnp.int32(bands - 1)]
    ).astype(jnp.int32)
    ring = [[(i, i ^ k) for i in range(bands)] for k in range(bands)]

    down = block_down.reshape(1, blocks)
    edge = shaped(5 * HALO, width)
    payload, slots, last_row, edge_a, edge_b = call(
        pack_kernel,
        (shaped(total, LANES), shaped(8, links), shaped(blocks, reach), edge, edge),
        [HBM] * 8 + [VMEM],
        scratch=[
            pltpu.VMEM((height, width), F32),
            pltpu.VMEM((height, width), F32),
            pltpu.VMEM((1, links), jnp.int32),
            pltpu.VMEM((1, links), jnp.int32),
            pltpu.VMEM((blocks, 16, reach), BF16),
            pltpu.VMEM((8, LANES), F32),
            pltpu.SemaphoreType.DMA((11,)),
        ],
        limit=None,
        flops=10**9,
        size=10**6,
    )(
        water_depth,
        bed_level,
        link_rows.reshape(1, links),
        link_blocks.reshape(1, links),
        reach_inverse,
        roughness,
        flux_east,
        flux_south,
        down,
    )
    rows_in = lax.all_to_all(
        payload.reshape(tiles, CHUNK, 1, LANES), "tile", split_axis=0, concat_axis=0, tiled=True
    )

    fields = (water_depth, bed_level, roughness, flux_east, flux_south)
    def pairs(count, first):
        return [(j, i) for k in range(first, count - 1, 2) for i, j in ((k, k + 1), (k + 1, k))]

    got_a = lax.ppermute(edge_a, "band", pairs(bands, 0))
    got_b = lax.ppermute(edge_b, "band", pairs(bands, 1))
    side_a, side_b = call(
        strips_kernel, (shaped(48, LANES), shaped(48, LANES)), [SMEM] + [VMEM] * 7, flops=10**6, size=10**6
    )(where, got_a, got_b, *fields)
    col_a = lax.ppermute(side_a, "tile", pairs(tiles, 0))
    col_b = lax.ppermute(side_b, "tile", pairs(tiles, 1))

    answer, source = call(
        lateral_kernel,
        (shaped(total, LANES), shaped(blocks, LANES)),
        [VMEM] * 4 + [ANY] * 2,
        flops=10**9,
        size=10**6,
    )(rows_in.reshape(total, LANES), river_section, reach_source, last_row, col_a, col_b)
    returned = lax.all_to_all(
        answer.reshape(tiles, CHUNK, 1, LANES), "tile", split_axis=0, concat_axis=0, tiled=True
    )

    wide = width + LANES
    tall = height + 2 * HALO
    water_now, final_east, final_south = call(
        flood_kernel,
        (shaped(height, width),) * 3,
        [SMEM] + [VMEM] * 9,
        scratch=[pltpu.VMEM((tall, wide), F32)] * 7,
        flops=10**8,
        size=10**7,
        exps=10**7,
    )(where, got_a, got_b, col_a, col_b, *fields)
    base_flow, column = call(
        flow_kernel, (shaped(blocks, reach),) * 2, [VMEM] * 2, flops=10**8, size=10**6
    )(source, reach_inverse)
    extras = rows_in.reshape(tiles, CHUNK, LANES)[:, SLOTS, :]
    others = [lax.ppermute(extras, "band", ring[k]) for k in (1, 2, 3)]
    reached = call(
        paths_kernel, shaped(LANES, tiles * blocks), [SMEM] + [VMEM] * 4, flops=10**9, size=10**6
    )(where, extras, *others)

    pushed = call(gather_kernel, shaped(8, LANES), [VMEM] * 2, flops=10**6, size=10**6)(
        returned.reshape(total, LANES), reached
    )
    parts = [pushed] + [lax.ppermute(pushed, "band", ring[k]) for k in (1, 2, 3)]
    final_depth = call(
        final_kernel, shaped(height, width), [VMEM] * 3, flops=10**9, size=10**6
    )(water_now, returned.reshape(total, LANES), slots)
    inflow = lax.dynamic_slice_in_dim(sum(parts)[0], band_index * blocks, blocks)
    discharge = base_flow + column * inflow[:, None]
    return (final_depth, final_east, final_south, discharge)


def solution(mesh):
    grid = P("band", "tile")
    owned = P(("tile", "band"))
    lists = P("tile", "band", None)
    return jax.shard_map(
        per_device,
        mesh=mesh,
        in_specs=(grid,) * 5 + (lists,) * 2 + (owned,) * 5,
        out_specs=(grid, grid, grid, owned),
        check_vma=False,
    )
```

```python
import functools

import jax
import jax.numpy as jnp
from jax import lax
from jax.experimental import pallas as pl
from jax.experimental.pallas import tpu as pltpu
from jax.sharding import PartitionSpec as P

SUBSTEPS = 8
LEVELS = 8
HALO = 8
LANES = 128
SLOTS = 16
CHUNK = SLOTS + 1
GAIN_LANE = 64
ID_LANE = 96

GRAVITY = 9.81
TIME_STEP = 3.0
CELL_WIDTH = 30.0
DEPTH_FLOOR = 0.2
FRICTION_POWER = 7.0 / 3.0
LATERAL_RATE = 0.2
PLAIN_SHARE = 0.8
RIVER_SHARE = 0.25

F32 = jnp.float32
BF16 = jnp.bfloat16
VMEM = pl.BlockSpec(memory_space=pltpu.VMEM)
HBM = pl.BlockSpec(memory_space=pltpu.HBM)
ANY = pl.BlockSpec(memory_space=pl.ANY)


def iota(shape, dim):
    return lax.broadcasted_iota(jnp.int32, shape, dim)


def halves(x):
    hi = x.astype(BF16)
    lo = (x - hi.astype(F32)).astype(BF16)
    return hi, lo


def paired(x):
    hi, lo = halves(x)
    return jnp.concatenate([hi, lo], axis=1)


def fold(x):
    return x[:, :LANES] + x[:, LANES:]


def mm(a, b, dims=((1,), (0,))):
    return lax.dot_general(a, b, (dims, ((), ())), preferred_element_type=F32)


def pack_kernel(
    water_h, bed_h, rows_h, blocks_h, inverse_h, rough_h, east_h, south_h, down,
    out, slots, last_out, edge_a, edge_b,
    water, bed, link_rows, link_blocks, tails, row_s, sems,
):
    blocks_own, reach = last_out.shape
    moves = (
        (rows_h, link_rows),
        (blocks_h, link_blocks),
        (water_h, water),
        (bed_h, bed),
        (inverse_h.at[:, reach - 16 : reach, :], tails),
    )
    height = water.shape[0]
    odd = lax.axis_index("band") % 2
    start_a = pl.multiple_of((1 - odd) * (height - HALO), HALO)
    start_b = pl.multiple_of(odd * (height - HALO), HALO)
    for a, field in enumerate((rough_h, east_h, south_h)):
        rows = pl.ds((a + 2) * HALO, HALO)
        moves += (
            (field.at[pl.ds(start_a, HALO), :], edge_a.at[rows, :]),
            (field.at[pl.ds(start_b, HALO), :], edge_b.at[rows, :]),
        )
    copies = [pltpu.make_async_copy(src, dst, sems.at[i]) for i, (src, dst) in enumerate(moves)]
    for copy in copies:
        copy.start()
    copies[0].wait()
    copies[1].wait()
    rows = link_rows[...]
    blocks = link_blocks[...]
    links = rows.shape[1]
    groups = water.shape[1] // LANES
    tiles = out.shape[0] // CHUNK
    place = ((rows % groups) * height + rows // groups).astype(F32)
    dest = (blocks >> 7).astype(F32)
    local = (blocks & 31).astype(F32)
    pick = iota((8, links), 0)
    stacked = jnp.where(pick == 0, place, jnp.where(pick == 1, dest, local))
    turned = jnp.transpose(stacked)
    place_c, dest_c, local_c = turned[:, 0:1], turned[:, 1:2], turned[:, 2:3]
    earlier = (dest_c == dest) & (iota((links, links), 1) < iota((links, links), 0))
    ones = jnp.ones((links, LANES), BF16)
    rank = mm(earlier.astype(F32).astype(BF16), ones)
    position = dest_c * float(CHUNK) + rank
    position_c = position[:, 0:1]
    lane = iota((links, links), 1).astype(F32)
    slot_of = jnp.sum(jnp.where(place_c == lane, position_c, 0.0), axis=0, keepdims=True)
    slots[...] = jnp.broadcast_to(slot_of, slots.shape)
    copies[2].wait()
    copies[3].wait()
    level = water[...] + bed[...]
    for edge, start in ((edge_a, start_a), (edge_b, start_b)):
        edge[HALO : 2 * HALO, :] = bed[pl.ds(start, HALO), :]
        edge[0:HALO, :] = water[pl.ds(start, HALO), :] + bed[pl.ds(start, HALO), :]
    by_block = jnp.concatenate(
        [level[:, c * LANES : (c + 1) * LANES] for c in range(groups)], axis=0
    )
    by_block = paired(by_block)
    hot = iota((out.shape[0], links), 0).astype(F32) == slot_of
    out[...] = fold(mm(jnp.where(hot, 1.0, 0.0).astype(BF16), by_block))
    dest_hot = (iota((tiles, links), 0).astype(F32) == dest).astype(F32).astype(BF16)
    seat = iota((links, LANES), 1).astype(F32) - float(ID_LANE)
    rank_hot = jnp.where(rank == seat, local_c + 1.0, 0.0)
    ids = mm(dest_hot, rank_hot.astype(BF16))
    copies[4].wait()
    last = tails[:, 15, :].astype(F32)
    last_out[...] = last
    first = (iota((8, reach), 1) == 0).astype(F32).astype(BF16)
    seated = jnp.concatenate(
        [jnp.zeros((GAIN_LANE, reach), F32), last, jnp.zeros((LANES - GAIN_LANE - blocks_own, reach), F32)],
        axis=0,
    )
    gain = mm(first, seated.astype(BF16), ((1,), (1,)))
    row_s[...] = jnp.zeros(row_s.shape, F32)
    row_s[0:1, 0:blocks_own] = down[...].astype(F32)
    out[pl.ds(SLOTS, tiles, CHUNK), :] = ids + (row_s[0:1, :] + gain[0:1, :])
    for copy in copies[5:]:
        copy.wait()


def lateral_kernel(rows_in, section, reach_source, last_row, order0, order1, out, source):
    total = rows_in.shape[0]
    tiles = total // CHUNK
    blocks = section.shape[0]
    slot = iota((total, 1), 0).astype(F32)
    owner = jnp.floor((slot + 0.5) * (1.0 / CHUNK))
    within = slot - owner * CHUNK + ID_LANE
    lane = iota((total, LANES), 1).astype(F32)
    extras = rows_in[pl.ds(SLOTS, tiles, CHUNK), :]
    ids_here = iota((tiles, LANES), 1)
    ids_here = (ids_here >= ID_LANE) & (ids_here < ID_LANE + SLOTS)
    ids = jnp.where(ids_here, extras, 0.0).astype(BF16)
    spread = (iota((total, tiles), 1).astype(F32) == owner).astype(F32).astype(BF16)
    seat = jnp.where(lane == within, mm(spread, ids), 0.0)
    block = mm(seat.astype(BF16), jnp.ones((LANES, LANES), BF16)) - 1.0
    hot = (block == lane).astype(F32).astype(BF16)
    section_in = fold(mm(hot[:, :blocks], paired(section[...])))
    lateral = jnp.where(block >= 0.0, LATERAL_RATE * (rows_in[...] - section_in), 0.0)
    out[...] = lateral
    sums = fold(mm(hot, paired(lateral), ((0,), (0,))))[:blocks]
    src = reach_source[...] + RIVER_SHARE * sums
    source[...] = src
    ends = jnp.concatenate([src * last_row[...], jnp.zeros((LANES - blocks, LANES), F32)], axis=0)
    ends_hi, ends_lo = halves(ends)
    ones = jnp.ones((8, LANES), BF16)
    row = mm(ones, ends_hi, ((1,), (1,))) + mm(ones, ends_lo, ((1,), (1,)))
    out[pl.ds(SLOTS, tiles, CHUNK), :] = jnp.broadcast_to(row[0:1, :], (tiles, LANES))


def dense(ref, blocks, start, step, count):
    turns = LANES // blocks
    group = iota((count // turns, LANES), 1) // blocks
    rows = jnp.zeros((count // turns, LANES), F32)
    for turn in range(turns):
        x = ref[pl.ds(start + turn * step, count // turns, turns * step), :]
        x = pltpu.roll(x, turn * blocks, 1) if turn else x
        rows = jnp.where(group == turn, x, rows)
    return rows


def paths_kernel(own, one, two, three, reach):
    bands = 4
    band, me = lax.axis_index("band"), lax.axis_index("tile").astype(F32) + 1.0
    tiles = own.shape[0]
    blocks = LANES // bands
    group = iota((tiles, LANES), 1) // blocks
    downs = jnp.zeros((tiles, LANES), F32)
    gains = jnp.zeros((tiles, LANES), F32)
    for back, ref in enumerate((own, one, two, three)):
        here = group == band ^ back
        x = ref[...]
        down, gain = x, x
        for turn in (1, 2, 3):
            y = pltpu.roll(x, turn * blocks, 1)
            down = jnp.where(group == turn, y, down)
            gain = jnp.where(group == (turn + GAIN_LANE // blocks) % bands, y, gain)
        downs = jnp.where(here, down, downs)
        gains = jnp.where(here, gain, gains)
    high = jnp.floor(downs * (1.0 / LANES))
    tables = jnp.concatenate([high + 1.0, downs - high * LANES, gains], axis=0).astype(BF16)
    sources = dense(own, blocks, 0, 1, tiles)
    chunks = sources.shape[0]
    high = jnp.floor(sources * (1.0 / LANES))
    low = sources - high * LANES
    high = high + 1.0
    tile_row = iota((tiles, LANES), 0).astype(F32) + 1.0
    block_row = iota((LANES, LANES), 0).astype(F32)
    state = [(high[i : i + 1], low[i : i + 1], jnp.ones((1, LANES), F32)) for i in range(chunks)]
    for hop in range(LEVELS - 1):
        for i in range(0, chunks, 2):
            hits = [block_row == state[k][1] for k in (i, i + 1)]
            if hop < LEVELS - 2:
                hot = jnp.concatenate([jnp.where(hit, 1.0, 0.0).astype(BF16) for hit in hits], axis=1)
                founds = mm(tables, hot)
            for k, hit in zip((i, i + 1), hits):
                hi, lo, factor = state[k]
                cols = slice(k * LANES, (k + 1) * LANES)
                mine = jnp.where(hit, jnp.where(hi == me, factor, 0.0), 0.0)
                reach[:, cols] = mine if hop == 0 else reach[:, cols] + mine
                if hop < LEVELS - 2:
                    found = founds[:, (k - i) * LANES : (k - i + 1) * LANES]
                    here = tile_row == hi
                    picks = [
                        jnp.sum(jnp.where(here, found[p * tiles : (p + 1) * tiles], 0.0), axis=0, keepdims=True)
                        for p in range(3)
                    ]
                    state[k] = (picks[0], picks[1], factor * picks[2])


def gather_kernel(returned, reach, out):
    tiles = returned.shape[0] // CHUNK
    blocks = reach.shape[1] // tiles
    ends = dense(returned, blocks, SLOTS, CHUNK, tiles)
    total = jnp.zeros((LANES, LANES), F32)
    for i in range(ends.shape[0]):
        total = total + reach[:, i * LANES : (i + 1) * LANES] * ends[i : i + 1, :]
    hi, lo = halves(total)
    ones = jnp.ones((8, LANES), BF16)
    out[...] = mm(ones, hi, ((1,), (1,))) + mm(ones, lo, ((1,), (1,)))


def flow_kernel(source, inverse, base, column):
    blocks = source.shape[0]
    hi, lo = halves(source[...])
    first = (iota((blocks, LANES), 1) == 0).astype(F32).astype(BF16)
    stacked = jnp.concatenate([hi, lo, first], axis=0)
    row = iota((blocks, LANES), 0)
    base_now = jnp.zeros((blocks, LANES), F32)
    column_now = jnp.zeros((blocks, LANES), F32)
    for g in range(blocks):
        x = mm(stacked, inverse[g], ((1,), (1,)))
        base_now = jnp.where(row == g, x[:blocks] + x[blocks : 2 * blocks], base_now)
        column_now = jnp.where(row == g, x[2 * blocks :], column_now)
    base[...] = base_now
    column[...] = column_now


def final_kernel(water, returned, slots, out):
    total = returned.shape[0]
    height = water.shape[0]
    groups = water.shape[1] // LANES
    slot_c = jnp.transpose(slots[...])[:, 0:1]
    rows = paired(returned[...])
    hot = iota((height * groups, total), 1).astype(F32) == slot_c
    lateral = fold(mm(jnp.where(hot, 1.0, 0.0).astype(BF16), rows))
    for c in range(groups):
        cols = slice(c * LANES, (c + 1) * LANES)
        out[:, cols] = water[:, cols] - PLAIN_SHARE * lateral[c * height : (c + 1) * height]


def strips_kernel(got_a, got_b, f0, f1, f2, f3, f4, side_a, side_b):
    fields = (f0, f1, f2, f3, f4)
    height, width = f0.shape
    tiles = height // 8 + 2
    lane = iota((8, LANES), 1)
    groups = side_a.shape[0] // 8
    odd_band, odd_tile = lax.axis_index("band") % 2 == 1, lax.axis_index("tile") % 2 == 1
    lefts = [jnp.zeros((8, LANES), F32) for _ in range(groups)]
    rights = [jnp.zeros((8, LANES), F32) for _ in range(groups)]
    for a, field in enumerate(fields):
        for i in range(tiles):
            strip = a * tiles + i
            v, off = strip // 16, (strip % 16) * 8
            here = (lane >= off) & (lane < off + 8)
            first, last = slice(0, LANES), slice(width - LANES, width)
            if i in (0, tiles - 1):
                rows = slice(a * HALO, a * HALO + 8)
                from_a = odd_band if i == 0 else jnp.logical_not(odd_band)
                x = jnp.where(from_a, got_a[rows, first], got_b[rows, first])
                y = jnp.where(from_a, got_a[rows, last], got_b[rows, last])
            else:
                rows = slice(8 * i - 8, 8 * i)
                x, y = field[rows, first], field[rows, last]
                if a == 0:
                    x, y = x + f1[rows, first], y + f1[rows, last]
            x = pltpu.roll(x, off, 1) if off else x
            y = pltpu.roll(y, (off + 8) % LANES, 1) if (off + 8) % LANES else y
            lefts[v] = jnp.where(here, x, lefts[v])
            rights[v] = jnp.where(here, y, rights[v])
    for v in range(groups):
        side_a[8 * v : 8 * v + 8, :] = jnp.where(odd_tile, lefts[v], rights[v])
        side_b[8 * v : 8 * v + 8, :] = jnp.where(odd_tile, rights[v], lefts[v])


def flood_kernel(
    got_a, got_b, col_a, col_b, f0, f1, f2, f3, f4,
    water_out, east_out, south_out,
    level_s, bed_s, rough_s, qe_s, qs_s, mbe_s, mbs_s,
):
    height, width = f0.shape
    tiles = height // 8 + 2
    wide = width + LANES
    lane1 = iota((8, LANES), 1)
    scratch = (level_s, bed_s, rough_s, qe_s, qs_s)
    share = TIME_STEP / CELL_WIDTH
    rate = GRAVITY * TIME_STEP
    slope_rate = share * rate / CELL_WIDTH
    tile_index, band_index = lax.axis_index("tile"), lax.axis_index("band")
    tile_last, band_last = lax.axis_size("tile") - 1, lax.axis_size("band") - 1
    odd_band, odd_tile = band_index % 2 == 1, tile_index % 2 == 1
    easts, wests = [], []
    for v in range(col_a.shape[0] // 8):
        x, y = col_a[8 * v : 8 * v + 8, :], col_b[8 * v : 8 * v + 8, :]
        easts.append(jnp.where(odd_tile, y, x))
        wests.append(jnp.where(odd_tile, x, y))
    for a, (field, dst) in enumerate(zip((f0, f1, f2, f3, f4), scratch)):
        for i in range(tiles):
            strip = a * tiles + i
            v, off = strip // 16, (strip % 16) * 8
            x, y = easts[v], wests[v]
            x = pltpu.roll(x, LANES - off, 1) if off else x
            y = pltpu.roll(y, (LANES - 8 - off) % LANES, 1) if (LANES - 8 - off) % LANES else y
            edge = jnp.where(lane1 < 8, x, jnp.where(lane1 >= LANES - 8, y, 0.0))
            if i in (0, tiles - 1):
                rows = slice(a * HALO, a * HALO + 8)
                from_a = odd_band if i == 0 else jnp.logical_not(odd_band)
                body = jnp.where(from_a, got_a[rows, :], got_b[rows, :])
            else:
                rows = slice(8 * i - 8, 8 * i)
                body = field[rows, :]
                if a == 0:
                    body = body + f1[rows, :]
            if a >= 2:
                scale = rate / share if a == 2 else share
                body, edge = scale * body, scale * edge
            dst[8 * i : 8 * i + 8, :width] = body
            dst[8 * i : 8 * i + 8, width:] = edge
    lane = iota((8, wide), 1)
    sub = iota((8, wide), 0)
    shut_e = ((lane == width - 1) & (tile_index == tile_last)) | ((lane == wide - 1) & (tile_index == 0))
    ce = jnp.where(shut_e, 0.0, slope_rate)
    shut_n = (sub == 7) & (band_index == 0)
    shut_s = (sub == 7) & (band_index == band_last)
    cs_first = jnp.where(shut_n, 0.0, slope_rate)
    cs_last = jnp.where(shut_s, 0.0, slope_rate)
    nxt = bed_s[0:8, :]
    nxt_up = pltpu.roll(nxt, 7, 0)
    for i in range(tiles):
        rows = slice(8 * i, 8 * i + 8)
        bed, up = nxt, nxt_up
        if i + 1 < tiles:
            nxt = bed_s[8 * i + 8 : 8 * i + 16, :]
            nxt_up = pltpu.roll(nxt, 7, 0)
        mbe_s[rows, :] = jnp.maximum(bed, pltpu.roll(bed, wide - 1, 1))
        mbs_s[rows, :] = jnp.maximum(bed, jnp.where(sub == 7, nxt_up, up))
        qe_s[rows, :] = jnp.where(shut_e, 0.0, qe_s[rows, :])
    last = slice(height, height + 8)
    qs_s[last, :] = jnp.where(shut_s, 0.0, qs_s[last, :])

    def face(here, ahead, bed_max, rough, old, factor):
        depth = jnp.maximum(jnp.maximum(here, ahead) - bed_max, DEPTH_FLOOR)
        drag = rough * jnp.abs(old) * jnp.exp2(-FRICTION_POWER * jnp.log2(depth)) + 1.0
        near = pl.reciprocal(drag, approx=True)
        return (old - factor * depth * (ahead - here)) * near

    def substep(_, carry):
        nxt = level_s[0:8, :]
        nxt_up = pltpu.roll(nxt, 7, 0)
        north_turned = jnp.zeros((8, wide), F32)
        for i in range(tiles):
            rows = slice(8 * i, 8 * i + 8)
            level, up = nxt, nxt_up
            if i + 1 < tiles:
                nxt = level_s[8 * i + 8 : 8 * i + 16, :]
                nxt_up = pltpu.roll(nxt, 7, 0)
            rough = rough_s[rows, :]
            cs = cs_first if i == 0 else cs_last if i == tiles - 2 else slope_rate
            qe = face(level, pltpu.roll(level, wide - 1, 1), mbe_s[rows, :], rough, qe_s[rows, :], ce)
            below_level = jnp.where(sub == 7, nxt_up, up)
            qs = face(level, below_level, mbs_s[rows, :], rough, qs_s[rows, :], cs)
            qe_s[rows, :] = qe
            qs_s[rows, :] = qs
            turned = pltpu.roll(qs, 1, 0)
            north = jnp.where(sub == 0, north_turned, turned)
            north_turned = turned
            gained = pltpu.roll(qe, 1, 1) - qe + north - qs
            level_s[rows, :] = level + gained
        return carry

    lax.fori_loop(0, SUBSTEPS, substep, 0)
    inner = slice(HALO, HALO + height)
    water_out[...] = level_s[inner, :width] - bed_s[inner, :width]
    east_out[...] = (1.0 / share) * qe_s[inner, :width]
    south_out[...] = (1.0 / share) * qs_s[inner, :width]


def shaped(*shape):
    return jax.ShapeDtypeStruct(shape, F32)


def call(kernel, out_shape, specs, scratch=(), flops=0, size=0, exps=0, limit=40 * 1024 * 1024):
    return pl.pallas_call(
        kernel,
        out_shape=out_shape,
        in_specs=specs,
        out_specs=jax.tree.map(lambda _: VMEM, out_shape),
        scratch_shapes=list(scratch),
        compiler_params=pltpu.CompilerParams(vmem_limit_bytes=limit),
        cost_estimate=pl.CostEstimate(flops=flops, bytes_accessed=size, transcendentals=exps),
        name=kernel.__name__,
    )


def per_device(
    water_depth, flux_east, flux_south, bed_level, roughness, link_rows, link_blocks,
    reach_inverse, reach_source, river_section, block_level, block_down,
):
    tiles = lax.axis_size("tile")
    bands = lax.axis_size("band")
    tile_index = lax.axis_index("tile")
    band_index = lax.axis_index("band")
    height, width = water_depth.shape
    blocks, reach = reach_source.shape
    total = tiles * CHUNK
    links = link_rows.shape[-1]
    ring = [[(i, i ^ k) for i in range(bands)] for k in range(bands)]

    down = block_down.reshape(1, blocks)
    edge = shaped(5 * HALO, width)
    payload, slots, last_row, edge_a, edge_b = call(
        pack_kernel,
        (shaped(total, LANES), shaped(8, links), shaped(blocks, reach), edge, edge),
        [HBM] * 8 + [VMEM],
        scratch=[
            pltpu.VMEM((height, width), F32),
            pltpu.VMEM((height, width), F32),
            pltpu.VMEM((1, links), jnp.int32),
            pltpu.VMEM((1, links), jnp.int32),
            pltpu.VMEM((blocks, 16, reach), BF16),
            pltpu.VMEM((8, LANES), F32),
            pltpu.SemaphoreType.DMA((11,)),
        ],
        limit=None,
        flops=10**9,
        size=10**6,
    )(
        water_depth,
        bed_level,
        link_rows.reshape(1, links),
        link_blocks.reshape(1, links),
        reach_inverse,
        roughness,
        flux_east,
        flux_south,
        down,
    )
    rows_in = lax.all_to_all(
        payload.reshape(tiles, CHUNK, 1, LANES), "tile", split_axis=0, concat_axis=0, tiled=True
    )

    fields = (water_depth, bed_level, roughness, flux_east, flux_south)
    def pairs(count, first):
        return [(j, i) for k in range(first, count - 1, 2) for i, j in ((k, k + 1), (k + 1, k))]

    got_a = lax.ppermute(edge_a, "band", pairs(bands, 0))
    got_b = lax.ppermute(edge_b, "band", pairs(bands, 1))
    side_a, side_b = call(
        strips_kernel, (shaped(48, LANES), shaped(48, LANES)), [VMEM] * 7, flops=10**6, size=10**6
    )(got_a, got_b, *fields)
    col_a = lax.ppermute(side_a, "tile", pairs(tiles, 0))
    col_b = lax.ppermute(side_b, "tile", pairs(tiles, 1))

    answer, source = call(
        lateral_kernel,
        (shaped(total, LANES), shaped(blocks, LANES)),
        [VMEM] * 4 + [ANY] * 2,
        flops=10**9,
        size=10**6,
    )(rows_in.reshape(total, LANES), river_section, reach_source, last_row, col_a, col_b)
    returned = lax.all_to_all(
        answer.reshape(tiles, CHUNK, 1, LANES), "tile", split_axis=0, concat_axis=0, tiled=True
    )

    wide = width + LANES
    tall = height + 2 * HALO
    water_now, final_east, final_south = call(
        flood_kernel,
        (shaped(height, width),) * 3,
        [VMEM] * 9,
        scratch=[pltpu.VMEM((tall, wide), F32)] * 7,
        flops=10**8,
        size=10**7,
        exps=10**7,
    )(got_a, got_b, col_a, col_b, *fields)
    base_flow, column = call(
        flow_kernel, (shaped(blocks, reach),) * 2, [VMEM] * 2, flops=10**8, size=10**6
    )(source, reach_inverse)
    extras = rows_in.reshape(tiles, CHUNK, LANES)[:, SLOTS, :]
    others = [lax.ppermute(extras, "band", ring[k]) for k in (1, 2, 3)]
    reached = call(
        paths_kernel, shaped(LANES, tiles * blocks), [VMEM] * 4, flops=10**9, size=10**6
    )(extras, *others)

    pushed = call(gather_kernel, shaped(8, LANES), [VMEM] * 2, flops=10**6, size=10**6)(
        returned.reshape(total, LANES), reached
    )
    parts = [pushed] + [lax.ppermute(pushed, "band", ring[k]) for k in (1, 2, 3)]
    final_depth = call(
        final_kernel, shaped(height, width), [VMEM] * 3, flops=10**9, size=10**6
    )(water_now, returned.reshape(total, LANES), slots)
    inflow = lax.dynamic_slice_in_dim(sum(parts)[0], band_index * blocks, blocks)
    discharge = base_flow + column * inflow[:, None]
    return (final_depth, final_east, final_south, discharge)


def solution(mesh):
    grid = P("band", "tile")
    owned = P(("tile", "band"))
    lists = P("tile", "band", None)
    return jax.shard_map(
        per_device,
        mesh=mesh,
        in_specs=(grid,) * 5 + (lists,) * 2 + (owned,) * 5,
        out_specs=(grid, grid, grid, owned),
        check_vma=False,
    )
```

```python
import functools

import jax
import jax.numpy as jnp
from jax import lax
from jax.experimental import pallas as pl
from jax.experimental.pallas import tpu as pltpu
from jax.sharding import PartitionSpec as P

SUBSTEPS = 8
LEVELS = 8
HALO = 8
LANES = 128
SLOTS = 16
CHUNK = SLOTS + 1
GAIN_LANE = 64
ID_LANE = 96

GRAVITY = 9.81
TIME_STEP = 3.0
CELL_WIDTH = 30.0
DEPTH_FLOOR = 0.2
FRICTION_POWER = 7.0 / 3.0
LATERAL_RATE = 0.2
PLAIN_SHARE = 0.8
RIVER_SHARE = 0.25

F32 = jnp.float32
BF16 = jnp.bfloat16
VMEM = pl.BlockSpec(memory_space=pltpu.VMEM)
HBM = pl.BlockSpec(memory_space=pltpu.HBM)
ANY = pl.BlockSpec(memory_space=pl.ANY)


def iota(shape, dim):
    return lax.broadcasted_iota(jnp.int32, shape, dim)


def halves(x):
    hi = x.astype(BF16)
    lo = (x - hi.astype(F32)).astype(BF16)
    return hi, lo


def paired(x):
    hi, lo = halves(x)
    return jnp.concatenate([hi, lo], axis=1)


def fold(x):
    return x[:, :LANES] + x[:, LANES:]


def mm(a, b, dims=((1,), (0,))):
    return lax.dot_general(a, b, (dims, ((), ())), preferred_element_type=F32)


def pack_kernel(
    water_h, bed_h, rows_h, blocks_h, inverse_h, rough_h, east_h, south_h, down_h,
    out, slots, last_out, edge_a, edge_b,
    water, bed, link_rows, link_blocks, tails, row_s, down, sems,
):
    blocks_own, reach = last_out.shape
    moves = (
        (rows_h, link_rows),
        (blocks_h, link_blocks),
        (water_h, water),
        (bed_h, bed),
        (inverse_h.at[:, reach - 16 : reach, :], tails),
        (down_h, down),
    )
    height = water.shape[0]
    odd = lax.axis_index("band") % 2
    start_a = pl.multiple_of((1 - odd) * (height - HALO), HALO)
    start_b = pl.multiple_of(odd * (height - HALO), HALO)
    for a, field in enumerate((rough_h, east_h, south_h)):
        rows = pl.ds((a + 2) * HALO, HALO)
        moves += (
            (field.at[pl.ds(start_a, HALO), :], edge_a.at[rows, :]),
            (field.at[pl.ds(start_b, HALO), :], edge_b.at[rows, :]),
        )
    copies = [pltpu.make_async_copy(src, dst, sems.at[i]) for i, (src, dst) in enumerate(moves)]
    for copy in copies:
        copy.start()
    copies[0].wait()
    copies[1].wait()
    rows = link_rows[...]
    blocks = link_blocks[...]
    links = rows.shape[1]
    groups = water.shape[1] // LANES
    tiles = out.shape[0] // CHUNK
    place = ((rows % groups) * height + rows // groups).astype(F32)
    dest = (blocks >> 7).astype(F32)
    local = (blocks & 31).astype(F32)
    pick = iota((8, links), 0)
    stacked = jnp.where(pick == 0, place, jnp.where(pick == 1, dest, local))
    turned = jnp.transpose(stacked)
    place_c, dest_c, local_c = turned[:, 0:1], turned[:, 1:2], turned[:, 2:3]
    earlier = (dest_c == dest) & (iota((links, links), 1) < iota((links, links), 0))
    ones = jnp.ones((links, LANES), BF16)
    rank = mm(earlier.astype(F32).astype(BF16), ones)
    position = dest_c * float(CHUNK) + rank
    position_c = position[:, 0:1]
    lane = iota((links, links), 1).astype(F32)
    slot_of = jnp.sum(jnp.where(place_c == lane, position_c, 0.0), axis=0, keepdims=True)
    slots[...] = jnp.broadcast_to(slot_of, slots.shape)
    copies[2].wait()
    copies[3].wait()
    level = water[...] + bed[...]
    for edge, start in ((edge_a, start_a), (edge_b, start_b)):
        edge[HALO : 2 * HALO, :] = bed[pl.ds(start, HALO), :]
        edge[0:HALO, :] = water[pl.ds(start, HALO), :] + bed[pl.ds(start, HALO), :]
    by_block = jnp.concatenate(
        [level[:, c * LANES : (c + 1) * LANES] for c in range(groups)], axis=0
    )
    by_block = paired(by_block)
    hot = iota((out.shape[0], links), 0).astype(F32) == slot_of
    out[...] = fold(mm(jnp.where(hot, 1.0, 0.0).astype(BF16), by_block))
    dest_hot = (iota((tiles, links), 0).astype(F32) == dest).astype(F32).astype(BF16)
    seat = iota((links, LANES), 1).astype(F32) - float(ID_LANE)
    rank_hot = jnp.where(rank == seat, local_c + 1.0, 0.0)
    ids = mm(dest_hot, rank_hot.astype(BF16))
    for copy in copies[4:]:
        copy.wait()
    last = tails[:, 15, :].astype(F32)
    last_out[...] = last
    first = (iota((8, reach), 1) == 0).astype(F32).astype(BF16)
    seated = jnp.concatenate(
        [jnp.zeros((GAIN_LANE, reach), F32), last, jnp.zeros((LANES - GAIN_LANE - blocks_own, reach), F32)],
        axis=0,
    )
    gain = mm(first, seated.astype(BF16), ((1,), (1,)))
    row_s[...] = jnp.zeros(row_s.shape, F32)
    row_s[0:1, 0:blocks_own] = down[...].astype(F32)
    out[pl.ds(SLOTS, tiles, CHUNK), :] = ids + (row_s[0:1, :] + gain[0:1, :])


def lateral_kernel(rows_in, section, reach_source, last_row, order0, order1, out, source):
    total = rows_in.shape[0]
    tiles = total // CHUNK
    blocks = section.shape[0]
    slot = iota((total, 1), 0).astype(F32)
    owner = jnp.floor((slot + 0.5) * (1.0 / CHUNK))
    within = slot - owner * CHUNK + ID_LANE
    lane = iota((total, LANES), 1).astype(F32)
    extras = rows_in[pl.ds(SLOTS, tiles, CHUNK), :]
    ids_here = iota((tiles, LANES), 1)
    ids_here = (ids_here >= ID_LANE) & (ids_here < ID_LANE + SLOTS)
    ids = jnp.where(ids_here, extras, 0.0).astype(BF16)
    spread = (iota((total, tiles), 1).astype(F32) == owner).astype(F32).astype(BF16)
    seat = jnp.where(lane == within, mm(spread, ids), 0.0)
    block = mm(seat.astype(BF16), jnp.ones((LANES, LANES), BF16)) - 1.0
    hot = (block == lane).astype(F32).astype(BF16)
    section_in = fold(mm(hot[:, :blocks], paired(section[...])))
    lateral = jnp.where(block >= 0.0, LATERAL_RATE * (rows_in[...] - section_in), 0.0)
    out[...] = lateral
    sums = fold(mm(hot, paired(lateral), ((0,), (0,))))[:blocks]
    src = reach_source[...] + RIVER_SHARE * sums
    source[...] = src
    ends = jnp.concatenate([src * last_row[...], jnp.zeros((LANES - blocks, LANES), F32)], axis=0)
    ends_hi, ends_lo = halves(ends)
    ones = jnp.ones((8, LANES), BF16)
    row = mm(ones, ends_hi, ((1,), (1,))) + mm(ones, ends_lo, ((1,), (1,)))
    out[pl.ds(SLOTS, tiles, CHUNK), :] = jnp.broadcast_to(row[0:1, :], (tiles, LANES))


def dense(ref, blocks, start, step, count):
    turns = LANES // blocks
    group = iota((count // turns, LANES), 1) // blocks
    rows = jnp.zeros((count // turns, LANES), F32)
    for turn in range(turns):
        x = ref[pl.ds(start + turn * step, count // turns, turns * step), :]
        x = pltpu.roll(x, turn * blocks, 1) if turn else x
        rows = jnp.where(group == turn, x, rows)
    return rows


def paths_kernel(own, one, two, three, reach):
    bands = 4
    band, me = lax.axis_index("band"), lax.axis_index("tile").astype(F32) + 1.0
    tiles = own.shape[0]
    blocks = LANES // bands
    group = iota((tiles, LANES), 1) // blocks
    downs = jnp.zeros((tiles, LANES), F32)
    gains = jnp.zeros((tiles, LANES), F32)
    for back, ref in enumerate((own, one, two, three)):
        here = group == band ^ back
        x = ref[...]
        down, gain = x, x
        for turn in (1, 2, 3):
            y = pltpu.roll(x, turn * blocks, 1)
            down = jnp.where(group == turn, y, down)
            gain = jnp.where(group == (turn + GAIN_LANE // blocks) % bands, y, gain)
        downs = jnp.where(here, down, downs)
        gains = jnp.where(here, gain, gains)
    high = jnp.floor(downs * (1.0 / LANES))
    tables = jnp.concatenate([high + 1.0, downs - high * LANES, gains], axis=0).astype(BF16)
    sources = dense(own, blocks, 0, 1, tiles)
    chunks = sources.shape[0]
    high = jnp.floor(sources * (1.0 / LANES))
    low = sources - high * LANES
    high = high + 1.0
    tile_row = iota((tiles, LANES), 0).astype(F32) + 1.0
    block_row = iota((LANES, LANES), 0).astype(F32)
    state = [(high[i : i + 1], low[i : i + 1], jnp.ones((1, LANES), F32)) for i in range(chunks)]
    for hop in range(LEVELS - 1):
        for i in range(0, chunks, 2):
            hits = [block_row == state[k][1] for k in (i, i + 1)]
            if hop < LEVELS - 2:
                hot = jnp.concatenate([jnp.where(hit, 1.0, 0.0).astype(BF16) for hit in hits], axis=1)
                founds = mm(tables, hot)
            for k, hit in zip((i, i + 1), hits):
                hi, lo, factor = state[k]
                cols = slice(k * LANES, (k + 1) * LANES)
                mine = jnp.where(hit, jnp.where(hi == me, factor, 0.0), 0.0)
                reach[:, cols] = mine if hop == 0 else reach[:, cols] + mine
                if hop < LEVELS - 2:
                    found = founds[:, (k - i) * LANES : (k - i + 1) * LANES]
                    here = tile_row == hi
                    picks = [
                        jnp.sum(jnp.where(here, found[p * tiles : (p + 1) * tiles], 0.0), axis=0, keepdims=True)
                        for p in range(3)
                    ]
                    state[k] = (picks[0], picks[1], factor * picks[2])


def gather_kernel(returned, reach, out):
    tiles = returned.shape[0] // CHUNK
    blocks = reach.shape[1] // tiles
    ends = dense(returned, blocks, SLOTS, CHUNK, tiles)
    total = jnp.zeros((LANES, LANES), F32)
    for i in range(ends.shape[0]):
        total = total + reach[:, i * LANES : (i + 1) * LANES] * ends[i : i + 1, :]
    hi, lo = halves(total)
    ones = jnp.ones((8, LANES), BF16)
    out[...] = mm(ones, hi, ((1,), (1,))) + mm(ones, lo, ((1,), (1,)))


def flow_kernel(source, inverse, base, column):
    blocks = source.shape[0]
    hi, lo = halves(source[...])
    first = (iota((blocks, LANES), 1) == 0).astype(F32).astype(BF16)
    stacked = jnp.concatenate([hi, lo, first], axis=0)
    row = iota((blocks, LANES), 0)
    base_now = jnp.zeros((blocks, LANES), F32)
    column_now = jnp.zeros((blocks, LANES), F32)
    for g in range(blocks):
        x = mm(stacked, inverse[g], ((1,), (1,)))
        base_now = jnp.where(row == g, x[:blocks] + x[blocks : 2 * blocks], base_now)
        column_now = jnp.where(row == g, x[2 * blocks :], column_now)
    base[...] = base_now
    column[...] = column_now


def discharge_kernel(base, column, own, one, two, three, out):
    blocks = base.shape[0]
    band = lax.axis_index("band")
    total = own[...] + one[...] + two[...] + three[...]
    turned = jnp.transpose(total)[:, 0:1]
    inflow = turned[0:blocks]
    for b in range(1, LANES // blocks):
        inflow = jnp.where(band == b, turned[b * blocks : (b + 1) * blocks], inflow)
    out[...] = base[...] + column[...] * inflow


def final_kernel(water, returned, slots, out):
    total = returned.shape[0]
    height = water.shape[0]
    groups = water.shape[1] // LANES
    slot_c = jnp.transpose(slots[...])[:, 0:1]
    rows = paired(returned[...])
    hot = iota((height * groups, total), 1).astype(F32) == slot_c
    lateral = fold(mm(jnp.where(hot, 1.0, 0.0).astype(BF16), rows))
    for c in range(groups):
        cols = slice(c * LANES, (c + 1) * LANES)
        out[:, cols] = water[:, cols] - PLAIN_SHARE * lateral[c * height : (c + 1) * height]


def strips_kernel(got_a, got_b, f0, f1, f2, f3, f4, side_a, side_b):
    fields = (f0, f1, f2, f3, f4)
    height, width = f0.shape
    tiles = height // 8 + 2
    lane = iota((8, LANES), 1)
    groups = side_a.shape[0] // 8
    odd_band, odd_tile = lax.axis_index("band") % 2 == 1, lax.axis_index("tile") % 2 == 1
    lefts = [jnp.zeros((8, LANES), F32) for _ in range(groups)]
    rights = [jnp.zeros((8, LANES), F32) for _ in range(groups)]
    for a, field in enumerate(fields):
        for i in range(tiles):
            strip = a * tiles + i
            v, off = strip // 16, (strip % 16) * 8
            here = (lane >= off) & (lane < off + 8)
            first, last = slice(0, LANES), slice(width - LANES, width)
            if i in (0, tiles - 1):
                rows = slice(a * HALO, a * HALO + 8)
                from_a = odd_band if i == 0 else jnp.logical_not(odd_band)
                x = jnp.where(from_a, got_a[rows, first], got_b[rows, first])
                y = jnp.where(from_a, got_a[rows, last], got_b[rows, last])
            else:
                rows = slice(8 * i - 8, 8 * i)
                x, y = field[rows, first], field[rows, last]
                if a == 0:
                    x, y = x + f1[rows, first], y + f1[rows, last]
            x = pltpu.roll(x, off, 1) if off else x
            y = pltpu.roll(y, (off + 8) % LANES, 1) if (off + 8) % LANES else y
            lefts[v] = jnp.where(here, x, lefts[v])
            rights[v] = jnp.where(here, y, rights[v])
    for v in range(groups):
        side_a[8 * v : 8 * v + 8, :] = jnp.where(odd_tile, lefts[v], rights[v])
        side_b[8 * v : 8 * v + 8, :] = jnp.where(odd_tile, rights[v], lefts[v])


def flood_kernel(
    got_a, got_b, col_a, col_b, f0, f1, f2, f3, f4,
    water_out, east_out, south_out,
    level_s, bed_s, rough_s, qe_s, qs_s, mbe_s, mbs_s,
):
    height, width = f0.shape
    tiles = height // 8 + 2
    wide = width + LANES
    lane1 = iota((8, LANES), 1)
    scratch = (level_s, bed_s, rough_s, qe_s, qs_s)
    share = TIME_STEP / CELL_WIDTH
    rate = GRAVITY * TIME_STEP
    slope_rate = share * rate / CELL_WIDTH
    tile_index, band_index = lax.axis_index("tile"), lax.axis_index("band")
    tile_last, band_last = lax.axis_size("tile") - 1, lax.axis_size("band") - 1
    odd_band, odd_tile = band_index % 2 == 1, tile_index % 2 == 1
    easts, wests = [], []
    for v in range(col_a.shape[0] // 8):
        x, y = col_a[8 * v : 8 * v + 8, :], col_b[8 * v : 8 * v + 8, :]
        easts.append(jnp.where(odd_tile, y, x))
        wests.append(jnp.where(odd_tile, x, y))
    for a, (field, dst) in enumerate(zip((f0, f1, f2, f3, f4), scratch)):
        for i in range(tiles):
            strip = a * tiles + i
            v, off = strip // 16, (strip % 16) * 8
            x, y = easts[v], wests[v]
            x = pltpu.roll(x, LANES - off, 1) if off else x
            y = pltpu.roll(y, (LANES - 8 - off) % LANES, 1) if (LANES - 8 - off) % LANES else y
            edge = jnp.where(lane1 < 8, x, jnp.where(lane1 >= LANES - 8, y, 0.0))
            if i in (0, tiles - 1):
                rows = slice(a * HALO, a * HALO + 8)
                from_a = odd_band if i == 0 else jnp.logical_not(odd_band)
                body = jnp.where(from_a, got_a[rows, :], got_b[rows, :])
            else:
                rows = slice(8 * i - 8, 8 * i)
                body = field[rows, :]
                if a == 0:
                    body = body + f1[rows, :]
            if a >= 2:
                scale = rate / share if a == 2 else share
                body, edge = scale * body, scale * edge
            dst[8 * i : 8 * i + 8, :width] = body
            dst[8 * i : 8 * i + 8, width:] = edge
    lane = iota((8, wide), 1)
    sub = iota((8, wide), 0)
    shut_e = ((lane == width - 1) & (tile_index == tile_last)) | ((lane == wide - 1) & (tile_index == 0))
    ce = jnp.where(shut_e, 0.0, slope_rate)
    shut_n = (sub == 7) & (band_index == 0)
    shut_s = (sub == 7) & (band_index == band_last)
    cs_first = jnp.where(shut_n, 0.0, slope_rate)
    cs_last = jnp.where(shut_s, 0.0, slope_rate)
    nxt = bed_s[0:8, :]
    nxt_up = pltpu.roll(nxt, 7, 0)
    for i in range(tiles):
        rows = slice(8 * i, 8 * i + 8)
        bed, up = nxt, nxt_up
        if i + 1 < tiles:
            nxt = bed_s[8 * i + 8 : 8 * i + 16, :]
            nxt_up = pltpu.roll(nxt, 7, 0)
        mbe_s[rows, :] = jnp.maximum(bed, pltpu.roll(bed, wide - 1, 1))
        mbs_s[rows, :] = jnp.maximum(bed, jnp.where(sub == 7, nxt_up, up))
        qe_s[rows, :] = jnp.where(shut_e, 0.0, qe_s[rows, :])
    last = slice(height, height + 8)
    qs_s[last, :] = jnp.where(shut_s, 0.0, qs_s[last, :])

    def face(here, ahead, bed_max, rough, old, factor):
        depth = jnp.maximum(jnp.maximum(here, ahead) - bed_max, DEPTH_FLOOR)
        drag = rough * jnp.abs(old) * jnp.exp2(-FRICTION_POWER * jnp.log2(depth)) + 1.0
        near = pl.reciprocal(drag, approx=True)
        return (old - factor * depth * (ahead - here)) * near

    def substep(_, carry):
        nxt = level_s[0:8, :]
        nxt_up = pltpu.roll(nxt, 7, 0)
        north_turned = jnp.zeros((8, wide), F32)
        for i in range(tiles):
            rows = slice(8 * i, 8 * i + 8)
            level, up = nxt, nxt_up
            if i + 1 < tiles:
                nxt = level_s[8 * i + 8 : 8 * i + 16, :]
                nxt_up = pltpu.roll(nxt, 7, 0)
            rough = rough_s[rows, :]
            cs = cs_first if i == 0 else cs_last if i == tiles - 2 else slope_rate
            qe = face(level, pltpu.roll(level, wide - 1, 1), mbe_s[rows, :], rough, qe_s[rows, :], ce)
            below_level = jnp.where(sub == 7, nxt_up, up)
            qs = face(level, below_level, mbs_s[rows, :], rough, qs_s[rows, :], cs)
            qe_s[rows, :] = qe
            qs_s[rows, :] = qs
            turned = pltpu.roll(qs, 1, 0)
            north = jnp.where(sub == 0, north_turned, turned)
            north_turned = turned
            gained = pltpu.roll(qe, 1, 1) - qe + north - qs
            level_s[rows, :] = level + gained
        return carry

    lax.fori_loop(0, SUBSTEPS, substep, 0)
    inner = slice(HALO, HALO + height)
    water_out[...] = level_s[inner, :width] - bed_s[inner, :width]
    east_out[...] = (1.0 / share) * qe_s[inner, :width]
    south_out[...] = (1.0 / share) * qs_s[inner, :width]


def shaped(*shape):
    return jax.ShapeDtypeStruct(shape, F32)


def call(kernel, out_shape, specs, scratch=(), flops=0, size=0, exps=0, limit=16 * 1024 * 1024):
    return pl.pallas_call(
        kernel,
        out_shape=out_shape,
        in_specs=specs,
        out_specs=jax.tree.map(lambda _: VMEM, out_shape),
        scratch_shapes=list(scratch),
        compiler_params=pltpu.CompilerParams(vmem_limit_bytes=limit),
        cost_estimate=pl.CostEstimate(flops=flops, bytes_accessed=size, transcendentals=exps),
        name=kernel.__name__,
    )


def per_device(
    water_depth, flux_east, flux_south, bed_level, roughness, link_rows, link_blocks,
    reach_inverse, reach_source, river_section, block_level, block_down,
):
    tiles = lax.axis_size("tile")
    bands = lax.axis_size("band")
    tile_index = lax.axis_index("tile")
    band_index = lax.axis_index("band")
    height, width = water_depth.shape
    blocks, reach = reach_source.shape
    total = tiles * CHUNK
    links = link_rows.shape[-1]
    ring = [[(i, i ^ k) for i in range(bands)] for k in range(bands)]

    down = block_down.reshape(1, blocks)
    edge = shaped(5 * HALO, width)
    payload, slots, last_row, edge_a, edge_b = call(
        pack_kernel,
        (shaped(total, LANES), shaped(8, links), shaped(blocks, reach), edge, edge),
        [HBM] * 9,
        scratch=[
            pltpu.VMEM((height, width), F32),
            pltpu.VMEM((height, width), F32),
            pltpu.VMEM((1, links), jnp.int32),
            pltpu.VMEM((1, links), jnp.int32),
            pltpu.VMEM((blocks, 16, reach), BF16),
            pltpu.VMEM((8, LANES), F32),
            pltpu.VMEM((1, blocks), jnp.int32),
            pltpu.SemaphoreType.DMA((12,)),
        ],
        limit=None,
        flops=10**9,
        size=10**6,
    )(
        water_depth,
        bed_level,
        link_rows.reshape(1, links),
        link_blocks.reshape(1, links),
        reach_inverse,
        roughness,
        flux_east,
        flux_south,
        down,
    )
    rows_in = lax.all_to_all(
        payload.reshape(tiles, CHUNK, 1, LANES), "tile", split_axis=0, concat_axis=0, tiled=True
    )

    fields = (water_depth, bed_level, roughness, flux_east, flux_south)
    def pairs(count, first):
        return [(j, i) for k in range(first, count - 1, 2) for i, j in ((k, k + 1), (k + 1, k))]

    got_a = lax.ppermute(edge_a, "band", pairs(bands, 0))
    got_b = lax.ppermute(edge_b, "band", pairs(bands, 1))
    side_a, side_b = call(
        strips_kernel, (shaped(48, LANES), shaped(48, LANES)), [VMEM] * 7, flops=10**6, size=10**6
    )(got_a, got_b, *fields)
    col_a = lax.ppermute(side_a, "tile", pairs(tiles, 0))
    col_b = lax.ppermute(side_b, "tile", pairs(tiles, 1))

    answer, source = call(
        lateral_kernel,
        (shaped(total, LANES), shaped(blocks, LANES)),
        [VMEM] * 4 + [ANY] * 2,
        flops=10**9,
        size=10**6,
    )(rows_in.reshape(total, LANES), river_section, reach_source, last_row, col_a, col_b)
    returned = lax.all_to_all(
        answer.reshape(tiles, CHUNK, 1, LANES), "tile", split_axis=0, concat_axis=0, tiled=True
    )

    wide = width + LANES
    tall = height + 2 * HALO
    water_now, final_east, final_south = call(
        flood_kernel,
        (shaped(height, width),) * 3,
        [VMEM] * 9,
        scratch=[pltpu.VMEM((tall, wide), F32)] * 7,
        flops=10**8,
        size=10**7,
        exps=10**7,
    )(got_a, got_b, col_a, col_b, *fields)
    base_flow, column = call(
        flow_kernel, (shaped(blocks, reach),) * 2, [VMEM] * 2, flops=10**8, size=10**6
    )(source, reach_inverse)
    extras = rows_in.reshape(tiles, CHUNK, LANES)[:, SLOTS, :]
    others = [lax.ppermute(extras, "band", ring[k]) for k in (1, 2, 3)]
    reached = call(
        paths_kernel, shaped(LANES, tiles * blocks), [VMEM] * 4, flops=10**9, size=10**6
    )(extras, *others)

    pushed = call(gather_kernel, shaped(8, LANES), [VMEM] * 2, flops=10**6, size=10**6)(
        returned.reshape(total, LANES), reached
    )
    parts = [pushed] + [lax.ppermute(pushed, "band", ring[k]) for k in (1, 2, 3)]
    final_depth = call(
        final_kernel, shaped(height, width), [VMEM] * 3, flops=10**9, size=10**6
    )(water_now, returned.reshape(total, LANES), slots)
    discharge = call(
        discharge_kernel, shaped(blocks, reach), [VMEM] * 6, flops=10**4, size=10**4
    )(base_flow, column, *parts)
    return (final_depth, final_east, final_south, discharge)


def solution(mesh):
    grid = P("band", "tile")
    owned = P(("tile", "band"))
    lists = P("tile", "band", None)
    return jax.shard_map(
        per_device,
        mesh=mesh,
        in_specs=(grid,) * 5 + (lists,) * 2 + (owned,) * 5,
        out_specs=(grid, grid, grid, owned),
        check_vma=False,
    )
```

```python
import functools

import jax
import jax.numpy as jnp
from jax import lax
from jax.experimental import pallas as pl
from jax.experimental.pallas import tpu as pltpu
from jax.sharding import PartitionSpec as P

SUBSTEPS = 8
LEVELS = 8
HALO = 8
LANES = 128
SLOTS = 16
CHUNK = SLOTS + 1
GAIN_LANE = 64
ID_LANE = 96

GRAVITY = 9.81
TIME_STEP = 3.0
CELL_WIDTH = 30.0
DEPTH_FLOOR = 0.2
FRICTION_POWER = 7.0 / 3.0
LATERAL_RATE = 0.2
PLAIN_SHARE = 0.8
RIVER_SHARE = 0.25

F32 = jnp.float32
BF16 = jnp.bfloat16
VMEM = pl.BlockSpec(memory_space=pltpu.VMEM)
HBM = pl.BlockSpec(memory_space=pltpu.HBM)
ANY = pl.BlockSpec(memory_space=pl.ANY)


def iota(shape, dim):
    return lax.broadcasted_iota(jnp.int32, shape, dim)


def halves(x):
    hi = x.astype(BF16)
    lo = (x - hi.astype(F32)).astype(BF16)
    return hi, lo


def paired(x):
    hi, lo = halves(x)
    return jnp.concatenate([hi, lo], axis=1)


def fold(x):
    return x[:, :LANES] + x[:, LANES:]


def mm(a, b, dims=((1,), (0,))):
    return lax.dot_general(a, b, (dims, ((), ())), preferred_element_type=F32)


def pack_kernel(
    water_h, bed_h, rows_h, blocks_h, inverse_h, rough_h, east_h, south_h, down_h,
    out_h, slots_h, last_h, edge_a_h, edge_b_h,
    water, bed, link_rows, link_blocks, tails, row_s, down,
    out, slots, last_out, edge_a, edge_b, sems, out_sems,
):
    blocks_own, reach = last_out.shape
    moves = (
        (rows_h, link_rows),
        (blocks_h, link_blocks),
        (water_h, water),
        (bed_h, bed),
        (inverse_h.at[:, reach - 16 : reach, :], tails),
        (down_h, down),
    )
    height = water.shape[0]
    odd = lax.axis_index("band") % 2
    start_a = pl.multiple_of((1 - odd) * (height - HALO), HALO)
    start_b = pl.multiple_of(odd * (height - HALO), HALO)
    for a, field in enumerate((rough_h, east_h, south_h)):
        rows = pl.ds((a + 2) * HALO, HALO)
        moves += (
            (field.at[pl.ds(start_a, HALO), :], edge_a.at[rows, :]),
            (field.at[pl.ds(start_b, HALO), :], edge_b.at[rows, :]),
        )
    copies = [pltpu.make_async_copy(src, dst, sems.at[i]) for i, (src, dst) in enumerate(moves)]
    for copy in copies:
        copy.start()
    sent = []

    def send(src, dst):
        sent.append(pltpu.make_async_copy(src, dst, out_sems.at[len(sent)]))
        sent[-1].start()

    copies[0].wait()
    copies[1].wait()
    rows = link_rows[...]
    blocks = link_blocks[...]
    links = rows.shape[1]
    groups = water.shape[1] // LANES
    tiles = out.shape[0] // CHUNK
    place = ((rows % groups) * height + rows // groups).astype(F32)
    dest = (blocks >> 7).astype(F32)
    local = (blocks & 31).astype(F32)
    pick = iota((8, links), 0)
    stacked = jnp.where(pick == 0, place, jnp.where(pick == 1, dest, local))
    turned = jnp.transpose(stacked)
    place_c, dest_c, local_c = turned[:, 0:1], turned[:, 1:2], turned[:, 2:3]
    earlier = (dest_c == dest) & (iota((links, links), 1) < iota((links, links), 0))
    ones = jnp.ones((links, LANES), BF16)
    rank = mm(earlier.astype(F32).astype(BF16), ones)
    position = dest_c * float(CHUNK) + rank
    position_c = position[:, 0:1]
    lane = iota((links, links), 1).astype(F32)
    slot_of = jnp.sum(jnp.where(place_c == lane, position_c, 0.0), axis=0, keepdims=True)
    slots[...] = jnp.broadcast_to(slot_of, slots.shape)
    send(slots, slots_h)
    copies[2].wait()
    copies[3].wait()
    level = water[...] + bed[...]
    for edge, start in ((edge_a, start_a), (edge_b, start_b)):
        edge[HALO : 2 * HALO, :] = bed[pl.ds(start, HALO), :]
        edge[0:HALO, :] = water[pl.ds(start, HALO), :] + bed[pl.ds(start, HALO), :]
    by_block = jnp.concatenate(
        [level[:, c * LANES : (c + 1) * LANES] for c in range(groups)], axis=0
    )
    by_block = paired(by_block)
    dest_hot = (iota((tiles, links), 0).astype(F32) == dest).astype(F32).astype(BF16)
    seat = iota((links, LANES), 1).astype(F32) - float(ID_LANE)
    rank_hot = jnp.where(rank == seat, local_c + 1.0, 0.0)
    ids = mm(dest_hot, rank_hot.astype(BF16))
    for copy in copies[4:]:
        copy.wait()
    last = tails[:, 15, :].astype(F32)
    last_out[...] = last
    send(last_out, last_h)
    send(edge_a, edge_a_h)
    send(edge_b, edge_b_h)
    first = (iota((8, reach), 1) == 0).astype(F32).astype(BF16)
    seated = jnp.concatenate(
        [jnp.zeros((GAIN_LANE, reach), F32), last, jnp.zeros((LANES - GAIN_LANE - blocks_own, reach), F32)],
        axis=0,
    )
    gain = mm(first, seated.astype(BF16), ((1,), (1,)))
    row_s[...] = jnp.zeros(row_s.shape, F32)
    row_s[0:1, 0:blocks_own] = down[...].astype(F32)
    extras = ids + (row_s[0:1, :] + gain[0:1, :])
    parts = 4
    size, chunks = out.shape[0] // parts, tiles // parts
    for part in range(parts):
        rows = slice(part * size, (part + 1) * size)
        hot = (iota((size, links), 0) + part * size).astype(F32) == slot_of
        out[rows, :] = fold(mm(jnp.where(hot, 1.0, 0.0).astype(BF16), by_block))
        out[pl.ds(part * size + SLOTS, chunks, CHUNK), :] = extras[part * chunks : (part + 1) * chunks]
        send(out.at[rows, :], out_h.at[rows, :])
    for copy in sent:
        copy.wait()


def lateral_kernel(rows_in, section, reach_source, last_row, order0, order1, out, source):
    total = rows_in.shape[0]
    tiles = total // CHUNK
    blocks = section.shape[0]
    slot = iota((total, 1), 0).astype(F32)
    owner = jnp.floor((slot + 0.5) * (1.0 / CHUNK))
    within = slot - owner * CHUNK + ID_LANE
    lane = iota((total, LANES), 1).astype(F32)
    extras = rows_in[pl.ds(SLOTS, tiles, CHUNK), :]
    ids_here = iota((tiles, LANES), 1)
    ids_here = (ids_here >= ID_LANE) & (ids_here < ID_LANE + SLOTS)
    ids = jnp.where(ids_here, extras, 0.0).astype(BF16)
    spread = (iota((total, tiles), 1).astype(F32) == owner).astype(F32).astype(BF16)
    seat = jnp.where(lane == within, mm(spread, ids), 0.0)
    block = mm(seat.astype(BF16), jnp.ones((LANES, LANES), BF16)) - 1.0
    hot = (block == lane).astype(F32).astype(BF16)
    rows = rows_in[...]
    counted = jnp.concatenate([paired(rows), jnp.ones((total, LANES), BF16)], axis=1)
    found = mm(hot, counted, ((0,), (0,)))[:blocks]
    sums = fold(found[:, : 2 * LANES]) - found[:, 2 * LANES :] * section[...]
    src = reach_source[...] + (RIVER_SHARE * LATERAL_RATE) * sums
    section_in = fold(mm(hot[:, :blocks], paired(section[...])))
    out[...] = jnp.where(block >= 0.0, LATERAL_RATE * (rows - section_in), 0.0)
    source[...] = src
    ends = jnp.concatenate([src * last_row[...], jnp.zeros((LANES - blocks, LANES), F32)], axis=0)
    ends_hi, ends_lo = halves(ends)
    ones = jnp.ones((8, LANES), BF16)
    row = mm(ones, ends_hi, ((1,), (1,))) + mm(ones, ends_lo, ((1,), (1,)))
    out[pl.ds(SLOTS, tiles, CHUNK), :] = jnp.broadcast_to(row[0:1, :], (tiles, LANES))


def dense(ref, blocks, start, step, count):
    turns = LANES // blocks
    group = iota((count // turns, LANES), 1) // blocks
    rows = jnp.zeros((count // turns, LANES), F32)
    for turn in range(turns):
        x = ref[pl.ds(start + turn * step, count // turns, turns * step), :]
        x = pltpu.roll(x, turn * blocks, 1) if turn else x
        rows = jnp.where(group == turn, x, rows)
    return rows


def paths_kernel(own, one, two, three, reach):
    bands = 4
    band, me = lax.axis_index("band"), lax.axis_index("tile").astype(F32) + 1.0
    tiles = own.shape[0]
    blocks = LANES // bands
    group = iota((tiles, LANES), 1) // blocks
    downs = jnp.zeros((tiles, LANES), F32)
    gains = jnp.zeros((tiles, LANES), F32)
    for back, ref in enumerate((own, one, two, three)):
        here = group == band ^ back
        x = ref[...]
        down, gain = x, x
        for turn in (1, 2, 3):
            y = pltpu.roll(x, turn * blocks, 1)
            down = jnp.where(group == turn, y, down)
            gain = jnp.where(group == (turn + GAIN_LANE // blocks) % bands, y, gain)
        downs = jnp.where(here, down, downs)
        gains = jnp.where(here, gain, gains)
    high = jnp.floor(downs * (1.0 / LANES))
    tables = jnp.concatenate([high + 1.0, downs - high * LANES, gains], axis=0).astype(BF16)
    sources = dense(own, blocks, 0, 1, tiles)
    chunks = sources.shape[0]
    high = jnp.floor(sources * (1.0 / LANES))
    low = sources - high * LANES
    high = high + 1.0
    tile_row = iota((tiles, LANES), 0).astype(F32) + 1.0
    block_row = iota((LANES, LANES), 0).astype(F32)
    state = [(high[i : i + 1], low[i : i + 1], jnp.ones((1, LANES), F32)) for i in range(chunks)]
    for hop in range(LEVELS - 1):
        for i in range(0, chunks, 2):
            hits = [block_row == state[k][1] for k in (i, i + 1)]
            if hop < LEVELS - 2:
                hot = jnp.concatenate([jnp.where(hit, 1.0, 0.0).astype(BF16) for hit in hits], axis=1)
                founds = mm(tables, hot)
            for k, hit in zip((i, i + 1), hits):
                hi, lo, factor = state[k]
                cols = slice(k * LANES, (k + 1) * LANES)
                mine = jnp.where(hit, jnp.where(hi == me, factor, 0.0), 0.0)
                reach[:, cols] = mine if hop == 0 else reach[:, cols] + mine
                if hop < LEVELS - 2:
                    found = founds[:, (k - i) * LANES : (k - i + 1) * LANES]
                    here = tile_row == hi
                    picks = [
                        jnp.sum(jnp.where(here, found[p * tiles : (p + 1) * tiles], 0.0), axis=0, keepdims=True)
                        for p in range(3)
                    ]
                    state[k] = (picks[0], picks[1], factor * picks[2])


def gather_kernel(returned, reach, out):
    tiles = returned.shape[0] // CHUNK
    blocks = reach.shape[1] // tiles
    ends = dense(returned, blocks, SLOTS, CHUNK, tiles)
    total = jnp.zeros((LANES, LANES), F32)
    for i in range(ends.shape[0]):
        total = total + reach[:, i * LANES : (i + 1) * LANES] * ends[i : i + 1, :]
    hi, lo = halves(total)
    ones = jnp.ones((8, LANES), BF16)
    out[...] = mm(ones, hi, ((1,), (1,))) + mm(ones, lo, ((1,), (1,)))


def flow_kernel(source, inverse, base, column):
    blocks = source.shape[0]
    hi, lo = halves(source[...])
    first = (iota((blocks, LANES), 1) == 0).astype(F32).astype(BF16)
    stacked = jnp.concatenate([hi, lo, first], axis=0)
    row = iota((blocks, LANES), 0)
    base_now = jnp.zeros((blocks, LANES), F32)
    column_now = jnp.zeros((blocks, LANES), F32)
    for g in range(blocks):
        x = mm(stacked, inverse[g], ((1,), (1,)))
        base_now = jnp.where(row == g, x[:blocks] + x[blocks : 2 * blocks], base_now)
        column_now = jnp.where(row == g, x[2 * blocks :], column_now)
    base[...] = base_now
    column[...] = column_now


def discharge_kernel(base, column, own, one, two, three, out):
    blocks = base.shape[0]
    band = lax.axis_index("band")
    total = own[...] + one[...] + two[...] + three[...]
    turned = jnp.transpose(total)[:, 0:1]
    inflow = turned[0:blocks]
    for b in range(1, LANES // blocks):
        inflow = jnp.where(band == b, turned[b * blocks : (b + 1) * blocks], inflow)
    out[...] = base[...] + column[...] * inflow


def hot_kernel(slots, out):
    slot_c = jnp.transpose(slots[...])[:, 0:1]
    hot = iota(out.shape, 1).astype(F32) == slot_c
    out[...] = jnp.where(hot, 1.0, 0.0).astype(BF16)


def final_kernel(water, returned, hot, out):
    height = water.shape[0]
    groups = water.shape[1] // LANES
    lateral = fold(mm(hot[...], paired(returned[...])))
    for c in range(groups):
        cols = slice(c * LANES, (c + 1) * LANES)
        out[:, cols] = water[:, cols] - PLAIN_SHARE * lateral[c * height : (c + 1) * height]


def strips_kernel(got_a, got_b, f0, f1, f2, f3, f4, side_a, side_b):
    fields = (f0, f1, f2, f3, f4)
    height, width = f0.shape
    tiles = height // 8 + 2
    lane = iota((8, LANES), 1)
    groups = side_a.shape[0] // 8
    odd_band, odd_tile = lax.axis_index("band") % 2 == 1, lax.axis_index("tile") % 2 == 1
    lefts = [jnp.zeros((8, LANES), F32) for _ in range(groups)]
    rights = [jnp.zeros((8, LANES), F32) for _ in range(groups)]
    for a, field in enumerate(fields):
        for i in range(tiles):
            strip = a * tiles + i
            v, off = strip // 16, (strip % 16) * 8
            here = (lane >= off) & (lane < off + 8)
            first, last = slice(0, LANES), slice(width - LANES, width)
            if i in (0, tiles - 1):
                rows = slice(a * HALO, a * HALO + 8)
                from_a = odd_band if i == 0 else jnp.logical_not(odd_band)
                x = jnp.where(from_a, got_a[rows, first], got_b[rows, first])
                y = jnp.where(from_a, got_a[rows, last], got_b[rows, last])
            else:
                rows = slice(8 * i - 8, 8 * i)
                x, y = field[rows, first], field[rows, last]
                if a == 0:
                    x, y = x + f1[rows, first], y + f1[rows, last]
            x = pltpu.roll(x, off, 1) if off else x
            y = pltpu.roll(y, (off + 8) % LANES, 1) if (off + 8) % LANES else y
            lefts[v] = jnp.where(here, x, lefts[v])
            rights[v] = jnp.where(here, y, rights[v])
    for v in range(groups):
        side_a[8 * v : 8 * v + 8, :] = jnp.where(odd_tile, lefts[v], rights[v])
        side_b[8 * v : 8 * v + 8, :] = jnp.where(odd_tile, rights[v], lefts[v])


def flood_kernel(
    got_a, got_b, col_a, col_b, f0, f1, f2, f3, f4,
    water_out, east_out, south_out,
    level_s, bed_s, rough_s, qe_s, qs_s, mbe_s, mbs_s,
):
    height, width = f0.shape
    tiles = height // 8 + 2
    wide = width + LANES
    lane1 = iota((8, LANES), 1)
    scratch = (level_s, bed_s, rough_s, qe_s, qs_s)
    share = TIME_STEP / CELL_WIDTH
    rate = GRAVITY * TIME_STEP
    slope_rate = share * rate / CELL_WIDTH
    tile_index, band_index = lax.axis_index("tile"), lax.axis_index("band")
    tile_last, band_last = lax.axis_size("tile") - 1, lax.axis_size("band") - 1
    odd_band, odd_tile = band_index % 2 == 1, tile_index % 2 == 1
    easts, wests = [], []
    for v in range(col_a.shape[0] // 8):
        x, y = col_a[8 * v : 8 * v + 8, :], col_b[8 * v : 8 * v + 8, :]
        easts.append(jnp.where(odd_tile, y, x))
        wests.append(jnp.where(odd_tile, x, y))
    for a, (field, dst) in enumerate(zip((f0, f1, f2, f3, f4), scratch)):
        for i in range(tiles):
            strip = a * tiles + i
            v, off = strip // 16, (strip % 16) * 8
            x, y = easts[v], wests[v]
            x = pltpu.roll(x, LANES - off, 1) if off else x
            y = pltpu.roll(y, (LANES - 8 - off) % LANES, 1) if (LANES - 8 - off) % LANES else y
            edge = jnp.where(lane1 < 8, x, jnp.where(lane1 >= LANES - 8, y, 0.0))
            if i in (0, tiles - 1):
                rows = slice(a * HALO, a * HALO + 8)
                from_a = odd_band if i == 0 else jnp.logical_not(odd_band)
                body = jnp.where(from_a, got_a[rows, :], got_b[rows, :])
            else:
                rows = slice(8 * i - 8, 8 * i)
                body = field[rows, :]
                if a == 0:
                    body = body + f1[rows, :]
            if a >= 2:
                scale = rate / share if a == 2 else share
                body, edge = scale * body, scale * edge
            dst[8 * i : 8 * i + 8, :width] = body
            dst[8 * i : 8 * i + 8, width:] = edge
    lane = iota((8, wide), 1)
    sub = iota((8, wide), 0)
    shut_e = ((lane == width - 1) & (tile_index == tile_last)) | ((lane == wide - 1) & (tile_index == 0))
    ce = jnp.where(shut_e, 0.0, slope_rate)
    shut_n = (sub == 7) & (band_index == 0)
    shut_s = (sub == 7) & (band_index == band_last)
    cs_first = jnp.where(shut_n, 0.0, slope_rate)
    cs_last = jnp.where(shut_s, 0.0, slope_rate)
    nxt = bed_s[0:8, :]
    nxt_up = pltpu.roll(nxt, 7, 0)
    for i in range(tiles):
        rows = slice(8 * i, 8 * i + 8)
        bed, up = nxt, nxt_up
        if i + 1 < tiles:
            nxt = bed_s[8 * i + 8 : 8 * i + 16, :]
            nxt_up = pltpu.roll(nxt, 7, 0)
        mbe_s[rows, :] = jnp.maximum(bed, pltpu.roll(bed, wide - 1, 1))
        mbs_s[rows, :] = jnp.maximum(bed, jnp.where(sub == 7, nxt_up, up))
        qe_s[rows, :] = jnp.where(shut_e, 0.0, qe_s[rows, :])
    last = slice(height, height + 8)
    qs_s[last, :] = jnp.where(shut_s, 0.0, qs_s[last, :])

    def face(here, ahead, bed_max, rough, old, factor):
        depth = jnp.maximum(jnp.maximum(here, ahead) - bed_max, DEPTH_FLOOR)
        drag = rough * jnp.abs(old) * jnp.exp2(-FRICTION_POWER * jnp.log2(depth)) + 1.0
        near = pl.reciprocal(drag, approx=True)
        return (old - factor * depth * (ahead - here)) * near

    def substep(_, carry):
        nxt = level_s[0:8, :]
        nxt_up = pltpu.roll(nxt, 7, 0)
        north_turned = jnp.zeros((8, wide), F32)
        for i in range(tiles):
            rows = slice(8 * i, 8 * i + 8)
            level, up = nxt, nxt_up
            if i + 1 < tiles:
                nxt = level_s[8 * i + 8 : 8 * i + 16, :]
                nxt_up = pltpu.roll(nxt, 7, 0)
            rough = rough_s[rows, :]
            cs = cs_first if i == 0 else cs_last if i == tiles - 2 else slope_rate
            qe = face(level, pltpu.roll(level, wide - 1, 1), mbe_s[rows, :], rough, qe_s[rows, :], ce)
            below_level = jnp.where(sub == 7, nxt_up, up)
            qs = face(level, below_level, mbs_s[rows, :], rough, qs_s[rows, :], cs)
            qe_s[rows, :] = qe
            qs_s[rows, :] = qs
            turned = pltpu.roll(qs, 1, 0)
            north = jnp.where(sub == 0, north_turned, turned)
            north_turned = turned
            gained = pltpu.roll(qe, 1, 1) - qe + north - qs
            level_s[rows, :] = level + gained
        return carry

    lax.fori_loop(0, SUBSTEPS, substep, 0)
    inner = slice(HALO, HALO + height)
    water_out[...] = level_s[inner, :width] - bed_s[inner, :width]
    east_out[...] = (1.0 / share) * qe_s[inner, :width]
    south_out[...] = (1.0 / share) * qs_s[inner, :width]


def shaped(*shape):
    return jax.ShapeDtypeStruct(shape, F32)


def call(kernel, out_shape, specs, scratch=(), flops=0, size=0, exps=0, limit=16 * 1024 * 1024, outside=False):
    return pl.pallas_call(
        kernel,
        out_shape=out_shape,
        in_specs=specs,
        out_specs=jax.tree.map(lambda _: HBM if outside else VMEM, out_shape),
        scratch_shapes=list(scratch),
        compiler_params=pltpu.CompilerParams(vmem_limit_bytes=limit),
        cost_estimate=pl.CostEstimate(flops=flops, bytes_accessed=size, transcendentals=exps),
        name=kernel.__name__,
    )


def per_device(
    water_depth, flux_east, flux_south, bed_level, roughness, link_rows, link_blocks,
    reach_inverse, reach_source, river_section, block_level, block_down,
):
    tiles = lax.axis_size("tile")
    bands = lax.axis_size("band")
    tile_index = lax.axis_index("tile")
    band_index = lax.axis_index("band")
    height, width = water_depth.shape
    blocks, reach = reach_source.shape
    total = tiles * CHUNK
    links = link_rows.shape[-1]
    ring = [[(i, i ^ k) for i in range(bands)] for k in range(bands)]

    down = block_down.reshape(1, blocks)
    edge = shaped(5 * HALO, width)
    payload, slots, last_row, edge_a, edge_b = call(
        pack_kernel,
        (shaped(total, LANES), shaped(8, links), shaped(blocks, reach), edge, edge),
        [HBM] * 9,
        scratch=[
            pltpu.VMEM((height, width), F32),
            pltpu.VMEM((height, width), F32),
            pltpu.VMEM((1, links), jnp.int32),
            pltpu.VMEM((1, links), jnp.int32),
            pltpu.VMEM((blocks, 16, reach), BF16),
            pltpu.VMEM((8, LANES), F32),
            pltpu.VMEM((1, blocks), jnp.int32),
            pltpu.VMEM((total, LANES), F32),
            pltpu.VMEM((8, links), F32),
            pltpu.VMEM((blocks, reach), F32),
            pltpu.VMEM((5 * HALO, width), F32),
            pltpu.VMEM((5 * HALO, width), F32),
            pltpu.SemaphoreType.DMA((12,)),
            pltpu.SemaphoreType.DMA((8,)),
        ],
        limit=None,
        outside=True,
        flops=10**9,
        size=10**6,
    )(
        water_depth,
        bed_level,
        link_rows.reshape(1, links),
        link_blocks.reshape(1, links),
        reach_inverse,
        roughness,
        flux_east,
        flux_south,
        down,
    )
    rows_in = lax.all_to_all(
        payload.reshape(tiles, CHUNK, 1, LANES), "tile", split_axis=0, concat_axis=0, tiled=True
    )

    fields = (water_depth, bed_level, roughness, flux_east, flux_south)
    def pairs(count, first):
        return [(j, i) for k in range(first, count - 1, 2) for i, j in ((k, k + 1), (k + 1, k))]

    got_a = lax.ppermute(edge_a, "band", pairs(bands, 0))
    got_b = lax.ppermute(edge_b, "band", pairs(bands, 1))
    side_a, side_b = call(
        strips_kernel, (shaped(48, LANES), shaped(48, LANES)), [VMEM] * 7, flops=10**6, size=10**6
    )(got_a, got_b, *fields)
    col_a = lax.ppermute(side_a, "tile", pairs(tiles, 0))
    col_b = lax.ppermute(side_b, "tile", pairs(tiles, 1))

    answer, source = call(
        lateral_kernel,
        (shaped(total, LANES), shaped(blocks, LANES)),
        [VMEM] * 4 + [ANY] * 2,
        flops=10**9,
        size=10**6,
    )(rows_in.reshape(total, LANES), river_section, reach_source, last_row, col_a, col_b)
    returned = lax.all_to_all(
        answer.reshape(tiles, CHUNK, 1, LANES), "tile", split_axis=0, concat_axis=0, tiled=True
    )

    wide = width + LANES
    tall = height + 2 * HALO
    water_now, final_east, final_south = call(
        flood_kernel,
        (shaped(height, width),) * 3,
        [VMEM] * 9,
        scratch=[pltpu.VMEM((tall, wide), F32)] * 7,
        flops=10**8,
        size=10**7,
        exps=10**7,
    )(got_a, got_b, col_a, col_b, *fields)
    base_flow, column = call(
        flow_kernel, (shaped(blocks, reach),) * 2, [VMEM] * 2, flops=10**8, size=10**6
    )(source, reach_inverse)
    extras = rows_in.reshape(tiles, CHUNK, LANES)[:, SLOTS, :]
    others = [lax.ppermute(extras, "band", ring[k]) for k in (1, 2, 3)]
    reached = call(
        paths_kernel, shaped(LANES, tiles * blocks), [VMEM] * 4, flops=10**9, size=10**6
    )(extras, *others)

    pushed = call(gather_kernel, shaped(8, LANES), [VMEM] * 2, flops=10**6, size=10**6)(
        returned.reshape(total, LANES), reached
    )
    parts = [pushed] + [lax.ppermute(pushed, "band", ring[k]) for k in (1, 2, 3)]
    hot = call(
        hot_kernel, jax.ShapeDtypeStruct((links, total), BF16), [VMEM], flops=10**8, size=10**6
    )(slots)
    final_depth = call(
        final_kernel, shaped(height, width), [VMEM] * 3, flops=10**9, size=10**6
    )(water_now, returned.reshape(total, LANES), hot)
    discharge = call(
        discharge_kernel, shaped(blocks, reach), [VMEM] * 6, flops=10**4, size=10**4
    )(base_flow, column, *parts)
    return (final_depth, final_east, final_south, discharge)


def solution(mesh):
    grid = P("band", "tile")
    owned = P(("tile", "band"))
    lists = P("tile", "band", None)
    return jax.shard_map(
        per_device,
        mesh=mesh,
        in_specs=(grid,) * 5 + (lists,) * 2 + (owned,) * 5,
        out_specs=(grid, grid, grid, owned),
        check_vma=False,
    )
```

```python
import functools

import jax
import jax.numpy as jnp
from jax import lax
from jax.experimental import pallas as pl
from jax.experimental.pallas import tpu as pltpu
from jax.sharding import PartitionSpec as P

SUBSTEPS = 8
LEVELS = 8
HALO = 8
LANES = 128
SLOTS = 16
CHUNK = SLOTS + 1
GAIN_LANE = 64
ID_LANE = 96

GRAVITY = 9.81
TIME_STEP = 3.0
CELL_WIDTH = 30.0
DEPTH_FLOOR = 0.2
FRICTION_POWER = 7.0 / 3.0
LATERAL_RATE = 0.2
PLAIN_SHARE = 0.8
RIVER_SHARE = 0.25

F32 = jnp.float32
BF16 = jnp.bfloat16
VMEM = pl.BlockSpec(memory_space=pltpu.VMEM)
HBM = pl.BlockSpec(memory_space=pltpu.HBM)
ANY = pl.BlockSpec(memory_space=pl.ANY)


def iota(shape, dim):
    return lax.broadcasted_iota(jnp.int32, shape, dim)


def halves(x):
    hi = x.astype(BF16)
    lo = (x - hi.astype(F32)).astype(BF16)
    return hi, lo


def paired(x):
    hi, lo = halves(x)
    return jnp.concatenate([hi, lo], axis=1)


def fold(x):
    return x[:, :LANES] + x[:, LANES:]


def mm(a, b, dims=((1,), (0,))):
    return lax.dot_general(a, b, (dims, ((), ())), preferred_element_type=F32)


def pack_kernel(
    water_h, bed_h, rows_h, blocks_h, inverse_h, rough_h, east_h, south_h, down_h,
    out_h, slots_h, last_h, edge_a_h, edge_b_h,
    water, bed, link_rows, link_blocks, tails, row_s, down,
    out, slots, last_out, edge_a, edge_b, sems, out_sems,
):
    blocks_own, reach = last_out.shape
    moves = (
        (rows_h, link_rows),
        (blocks_h, link_blocks),
        (water_h, water),
        (bed_h, bed),
        (inverse_h.at[:, reach - 16 : reach, :], tails),
        (down_h, down),
    )
    height = water.shape[0]
    odd = lax.axis_index("band") % 2
    start_a = pl.multiple_of((1 - odd) * (height - HALO), HALO)
    start_b = pl.multiple_of(odd * (height - HALO), HALO)
    for a, field in enumerate((rough_h, east_h, south_h)):
        rows = pl.ds((a + 2) * HALO, HALO)
        moves += (
            (field.at[pl.ds(start_a, HALO), :], edge_a.at[rows, :]),
            (field.at[pl.ds(start_b, HALO), :], edge_b.at[rows, :]),
        )
    copies = [pltpu.make_async_copy(src, dst, sems.at[i]) for i, (src, dst) in enumerate(moves)]
    for copy in copies:
        copy.start()
    sent = []

    def send(src, dst):
        sent.append(pltpu.make_async_copy(src, dst, out_sems.at[len(sent)]))
        sent[-1].start()

    copies[0].wait()
    copies[1].wait()
    rows = link_rows[...]
    blocks = link_blocks[...]
    links = rows.shape[1]
    groups = water.shape[1] // LANES
    tiles = out.shape[0] // CHUNK
    place = ((rows % groups) * height + rows // groups).astype(F32)
    dest = (blocks >> 7).astype(F32)
    local = (blocks & 31).astype(F32)
    pick = iota((8, links), 0)
    stacked = jnp.where(pick == 0, place, jnp.where(pick == 1, dest, local))
    turned = jnp.transpose(stacked)
    place_c, dest_c, local_c = turned[:, 0:1], turned[:, 1:2], turned[:, 2:3]
    earlier = (dest_c == dest) & (iota((links, links), 1) < iota((links, links), 0))
    ones = jnp.ones((links, LANES), BF16)
    rank = mm(earlier.astype(F32).astype(BF16), ones)
    position = dest_c * float(CHUNK) + rank
    position_c = position[:, 0:1]
    lane = iota((links, links), 1).astype(F32)
    slot_of = jnp.sum(jnp.where(place_c == lane, position_c, 0.0), axis=0, keepdims=True)
    slots[...] = jnp.broadcast_to(slot_of, slots.shape)
    send(slots, slots_h)
    copies[2].wait()
    copies[3].wait()
    level = water[...] + bed[...]
    for edge, start in ((edge_a, start_a), (edge_b, start_b)):
        edge[HALO : 2 * HALO, :] = bed[pl.ds(start, HALO), :]
        edge[0:HALO, :] = water[pl.ds(start, HALO), :] + bed[pl.ds(start, HALO), :]
    by_block = jnp.concatenate(
        [level[:, c * LANES : (c + 1) * LANES] for c in range(groups)], axis=0
    )
    by_block = paired(by_block)
    dest_hot = (iota((tiles, links), 0).astype(F32) == dest).astype(F32).astype(BF16)
    seat = iota((links, LANES), 1).astype(F32) - float(ID_LANE)
    rank_hot = jnp.where(rank == seat, local_c + 1.0, 0.0)
    ids = mm(dest_hot, rank_hot.astype(BF16))
    for copy in copies[4:]:
        copy.wait()
    last = tails[:, 15, :].astype(F32)
    last_out[...] = last
    send(last_out, last_h)
    send(edge_a, edge_a_h)
    send(edge_b, edge_b_h)
    first = (iota((8, reach), 1) == 0).astype(F32).astype(BF16)
    seated = jnp.concatenate(
        [jnp.zeros((GAIN_LANE, reach), F32), last, jnp.zeros((LANES - GAIN_LANE - blocks_own, reach), F32)],
        axis=0,
    )
    gain = mm(first, seated.astype(BF16), ((1,), (1,)))
    row_s[...] = jnp.zeros(row_s.shape, F32)
    row_s[0:1, 0:blocks_own] = down[...].astype(F32)
    extras = ids + (row_s[0:1, :] + gain[0:1, :])
    parts = 4
    size, chunks = out.shape[0] // parts, tiles // parts
    for part in range(parts):
        rows = slice(part * size, (part + 1) * size)
        hot = (iota((size, links), 0) + part * size).astype(F32) == slot_of
        out[rows, :] = fold(mm(jnp.where(hot, 1.0, 0.0).astype(BF16), by_block))
        out[pl.ds(part * size + SLOTS, chunks, CHUNK), :] = extras[part * chunks : (part + 1) * chunks]
        send(out.at[rows, :], out_h.at[rows, :])
    for copy in sent:
        copy.wait()


def lateral_kernel(rows_in, section, reach_source, last_row, order0, order1, out, source):
    total = rows_in.shape[0]
    tiles = total // CHUNK
    blocks = section.shape[0]
    slot = iota((total, 1), 0).astype(F32)
    owner = jnp.floor((slot + 0.5) * (1.0 / CHUNK))
    within = slot - owner * CHUNK + ID_LANE
    lane = iota((total, LANES), 1).astype(F32)
    extras = rows_in[pl.ds(SLOTS, tiles, CHUNK), :]
    ids_here = iota((tiles, LANES), 1)
    ids_here = (ids_here >= ID_LANE) & (ids_here < ID_LANE + SLOTS)
    ids = jnp.where(ids_here, extras, 0.0).astype(BF16)
    spread = (iota((total, tiles), 1).astype(F32) == owner).astype(F32).astype(BF16)
    seat = jnp.where(lane == within, mm(spread, ids), 0.0)
    block = mm(seat.astype(BF16), jnp.ones((LANES, LANES), BF16)) - 1.0
    hot = (block == lane).astype(F32).astype(BF16)
    rows = rows_in[...]
    counted = jnp.concatenate([paired(rows), jnp.ones((total, LANES), BF16)], axis=1)
    found = mm(hot, counted, ((0,), (0,)))[:blocks]
    sums = fold(found[:, : 2 * LANES]) - found[:, 2 * LANES :] * section[...]
    src = reach_source[...] + (RIVER_SHARE * LATERAL_RATE) * sums
    section_in = fold(mm(hot[:, :blocks], paired(section[...])))
    out[...] = jnp.where(block >= 0.0, LATERAL_RATE * (rows - section_in), 0.0)
    source[...] = src
    ends = jnp.concatenate([src * last_row[...], jnp.zeros((LANES - blocks, LANES), F32)], axis=0)
    ends_hi, ends_lo = halves(ends)
    ones = jnp.ones((8, LANES), BF16)
    row = mm(ones, ends_hi, ((1,), (1,))) + mm(ones, ends_lo, ((1,), (1,)))
    out[pl.ds(SLOTS, tiles, CHUNK), :] = jnp.broadcast_to(row[0:1, :], (tiles, LANES))


def dense(ref, blocks, start, step, count):
    turns = LANES // blocks
    group = iota((count // turns, LANES), 1) // blocks
    rows = jnp.zeros((count // turns, LANES), F32)
    for turn in range(turns):
        x = ref[pl.ds(start + turn * step, count // turns, turns * step), :]
        x = pltpu.roll(x, turn * blocks, 1) if turn else x
        rows = jnp.where(group == turn, x, rows)
    return rows


def paths_kernel(own, one, two, three, reach):
    bands = 4
    band, me = lax.axis_index("band"), lax.axis_index("tile").astype(F32) + 1.0
    tiles = own.shape[0]
    blocks = LANES // bands
    group = iota((tiles, LANES), 1) // blocks
    downs = jnp.zeros((tiles, LANES), F32)
    gains = jnp.zeros((tiles, LANES), F32)
    for back, ref in enumerate((own, one, two, three)):
        here = group == band ^ back
        x = ref[...]
        down, gain = x, x
        for turn in (1, 2, 3):
            y = pltpu.roll(x, turn * blocks, 1)
            down = jnp.where(group == turn, y, down)
            gain = jnp.where(group == (turn + GAIN_LANE // blocks) % bands, y, gain)
        downs = jnp.where(here, down, downs)
        gains = jnp.where(here, gain, gains)
    high = jnp.floor(downs * (1.0 / LANES))
    tables = jnp.concatenate([high + 1.0, downs - high * LANES, gains], axis=0).astype(BF16)
    sources = dense(own, blocks, 0, 1, tiles)
    chunks = sources.shape[0]
    high = jnp.floor(sources * (1.0 / LANES))
    low = sources - high * LANES
    high = high + 1.0
    tile_row = iota((tiles, LANES), 0).astype(F32) + 1.0
    block_row = iota((LANES, LANES), 0).astype(F32)
    state = [(high[i : i + 1], low[i : i + 1], jnp.ones((1, LANES), F32)) for i in range(chunks)]
    for hop in range(LEVELS - 1):
        for i in range(0, chunks, 2):
            hits = [block_row == state[k][1] for k in (i, i + 1)]
            if hop < LEVELS - 2:
                hot = jnp.concatenate([jnp.where(hit, 1.0, 0.0).astype(BF16) for hit in hits], axis=1)
                founds = mm(tables, hot)
            for k, hit in zip((i, i + 1), hits):
                hi, lo, factor = state[k]
                cols = slice(k * LANES, (k + 1) * LANES)
                mine = jnp.where(hit, jnp.where(hi == me, factor, 0.0), 0.0)
                reach[:, cols] = mine if hop == 0 else reach[:, cols] + mine
                if hop < LEVELS - 2:
                    found = founds[:, (k - i) * LANES : (k - i + 1) * LANES]
                    here = tile_row == hi
                    picks = [
                        jnp.sum(jnp.where(here, found[p * tiles : (p + 1) * tiles], 0.0), axis=0, keepdims=True)
                        for p in range(3)
                    ]
                    state[k] = (picks[0], picks[1], factor * picks[2])


def gather_kernel(returned, reach, out):
    tiles = returned.shape[0] // CHUNK
    blocks = reach.shape[1] // tiles
    ends = dense(returned, blocks, SLOTS, CHUNK, tiles)
    total = jnp.zeros((LANES, LANES), F32)
    for i in range(ends.shape[0]):
        total = total + reach[:, i * LANES : (i + 1) * LANES] * ends[i : i + 1, :]
    hi, lo = halves(total)
    ones = jnp.ones((8, LANES), BF16)
    out[...] = mm(ones, hi, ((1,), (1,))) + mm(ones, lo, ((1,), (1,)))


def flow_kernel(source, inverse, base, column):
    blocks = source.shape[0]
    hi, lo = halves(source[...])
    first = (iota((blocks, LANES), 1) == 0).astype(F32).astype(BF16)
    stacked = jnp.concatenate([hi, lo, first], axis=0)
    row = iota((blocks, LANES), 0)
    base_now = jnp.zeros((blocks, LANES), F32)
    column_now = jnp.zeros((blocks, LANES), F32)
    for g in range(blocks):
        x = mm(stacked, inverse[g], ((1,), (1,)))
        base_now = jnp.where(row == g, x[:blocks] + x[blocks : 2 * blocks], base_now)
        column_now = jnp.where(row == g, x[2 * blocks :], column_now)
    base[...] = base_now
    column[...] = column_now


def discharge_kernel(base, column, own, one, two, three, out):
    blocks = base.shape[0]
    band = lax.axis_index("band")
    total = own[...] + one[...] + two[...] + three[...]
    turned = jnp.transpose(total)[:, 0:1]
    inflow = turned[0:blocks]
    for b in range(1, LANES // blocks):
        inflow = jnp.where(band == b, turned[b * blocks : (b + 1) * blocks], inflow)
    out[...] = base[...] + column[...] * inflow


def hot_kernel(slots, out):
    slot_c = jnp.transpose(slots[...])[:, 0:1]
    hot = iota(out.shape, 1).astype(F32) == slot_c
    out[...] = jnp.where(hot, 1.0, 0.0).astype(BF16)


def final_kernel(water, returned, hot, out):
    height = water.shape[0]
    groups = water.shape[1] // LANES
    lateral = fold(mm(hot[...], paired(returned[...])))
    for c in range(groups):
        cols = slice(c * LANES, (c + 1) * LANES)
        out[:, cols] = water[:, cols] - PLAIN_SHARE * lateral[c * height : (c + 1) * height]


def strips_kernel(got_a, got_b, f0, f1, f2, f3, f4, order, side_a, side_b):
    fields = (f0, f1, f2, f3, f4)
    height, width = f0.shape
    tiles = height // 8 + 2
    lane = iota((8, LANES), 1)
    groups = side_a.shape[0] // 8
    odd_band, odd_tile = lax.axis_index("band") % 2 == 1, lax.axis_index("tile") % 2 == 1
    lefts = [jnp.zeros((8, LANES), F32) for _ in range(groups)]
    rights = [jnp.zeros((8, LANES), F32) for _ in range(groups)]
    for a, field in enumerate(fields):
        for i in range(tiles):
            strip = a * tiles + i
            v, off = strip // 16, (strip % 16) * 8
            here = (lane >= off) & (lane < off + 8)
            first, last = slice(0, LANES), slice(width - LANES, width)
            if i in (0, tiles - 1):
                rows = slice(a * HALO, a * HALO + 8)
                from_a = odd_band if i == 0 else jnp.logical_not(odd_band)
                x = jnp.where(from_a, got_a[rows, first], got_b[rows, first])
                y = jnp.where(from_a, got_a[rows, last], got_b[rows, last])
            else:
                rows = slice(8 * i - 8, 8 * i)
                x, y = field[rows, first], field[rows, last]
                if a == 0:
                    x, y = x + f1[rows, first], y + f1[rows, last]
            x = pltpu.roll(x, off, 1) if off else x
            y = pltpu.roll(y, (off + 8) % LANES, 1) if (off + 8) % LANES else y
            lefts[v] = jnp.where(here, x, lefts[v])
            rights[v] = jnp.where(here, y, rights[v])
    for v in range(groups):
        side_a[8 * v : 8 * v + 8, :] = jnp.where(odd_tile, lefts[v], rights[v])
        side_b[8 * v : 8 * v + 8, :] = jnp.where(odd_tile, rights[v], lefts[v])


def flood_kernel(
    got_a, got_b, col_a, col_b, f0, f1, f2, f3, f4,
    water_out, east_out, south_out,
    level_s, bed_s, rough_s, qe_s, qs_s, mbe_s, mbs_s,
):
    height, width = f0.shape
    tiles = height // 8 + 2
    wide = width + LANES
    lane1 = iota((8, LANES), 1)
    scratch = (level_s, bed_s, rough_s, qe_s, qs_s)
    share = TIME_STEP / CELL_WIDTH
    rate = GRAVITY * TIME_STEP
    slope_rate = share * rate / CELL_WIDTH
    tile_index, band_index = lax.axis_index("tile"), lax.axis_index("band")
    tile_last, band_last = lax.axis_size("tile") - 1, lax.axis_size("band") - 1
    odd_band, odd_tile = band_index % 2 == 1, tile_index % 2 == 1
    easts, wests = [], []
    for v in range(col_a.shape[0] // 8):
        x, y = col_a[8 * v : 8 * v + 8, :], col_b[8 * v : 8 * v + 8, :]
        easts.append(jnp.where(odd_tile, y, x))
        wests.append(jnp.where(odd_tile, x, y))
    for a, (field, dst) in enumerate(zip((f0, f1, f2, f3, f4), scratch)):
        for i in range(tiles):
            strip = a * tiles + i
            v, off = strip // 16, (strip % 16) * 8
            x, y = easts[v], wests[v]
            x = pltpu.roll(x, LANES - off, 1) if off else x
            y = pltpu.roll(y, (LANES - 8 - off) % LANES, 1) if (LANES - 8 - off) % LANES else y
            edge = jnp.where(lane1 < 8, x, jnp.where(lane1 >= LANES - 8, y, 0.0))
            if i in (0, tiles - 1):
                rows = slice(a * HALO, a * HALO + 8)
                from_a = odd_band if i == 0 else jnp.logical_not(odd_band)
                body = jnp.where(from_a, got_a[rows, :], got_b[rows, :])
            else:
                rows = slice(8 * i - 8, 8 * i)
                body = field[rows, :]
                if a == 0:
                    body = body + f1[rows, :]
            if a >= 2:
                scale = rate / share if a == 2 else share
                body, edge = scale * body, scale * edge
            dst[8 * i : 8 * i + 8, :width] = body
            dst[8 * i : 8 * i + 8, width:] = edge
    lane = iota((8, wide), 1)
    sub = iota((8, wide), 0)
    shut_e = ((lane == width - 1) & (tile_index == tile_last)) | ((lane == wide - 1) & (tile_index == 0))
    ce = jnp.where(shut_e, 0.0, slope_rate)
    shut_n = (sub == 7) & (band_index == 0)
    shut_s = (sub == 7) & (band_index == band_last)
    cs_first = jnp.where(shut_n, 0.0, slope_rate)
    cs_last = jnp.where(shut_s, 0.0, slope_rate)
    nxt = bed_s[0:8, :]
    nxt_up = pltpu.roll(nxt, 7, 0)
    for i in range(tiles):
        rows = slice(8 * i, 8 * i + 8)
        bed, up = nxt, nxt_up
        if i + 1 < tiles:
            nxt = bed_s[8 * i + 8 : 8 * i + 16, :]
            nxt_up = pltpu.roll(nxt, 7, 0)
        mbe_s[rows, :] = jnp.maximum(bed, pltpu.roll(bed, wide - 1, 1))
        mbs_s[rows, :] = jnp.maximum(bed, jnp.where(sub == 7, nxt_up, up))
        qe_s[rows, :] = jnp.where(shut_e, 0.0, qe_s[rows, :])
    last = slice(height, height + 8)
    qs_s[last, :] = jnp.where(shut_s, 0.0, qs_s[last, :])

    def face(here, ahead, bed_max, rough, old, factor):
        depth = jnp.maximum(jnp.maximum(here, ahead) - bed_max, DEPTH_FLOOR)
        drag = rough * jnp.abs(old) * jnp.exp2(-FRICTION_POWER * jnp.log2(depth)) + 1.0
        near = pl.reciprocal(drag, approx=True)
        return (old - factor * depth * (ahead - here)) * near

    def substep(_, carry):
        nxt = level_s[0:8, :]
        nxt_up = pltpu.roll(nxt, 7, 0)
        north_turned = jnp.zeros((8, wide), F32)
        for i in range(tiles):
            rows = slice(8 * i, 8 * i + 8)
            level, up = nxt, nxt_up
            if i + 1 < tiles:
                nxt = level_s[8 * i + 8 : 8 * i + 16, :]
                nxt_up = pltpu.roll(nxt, 7, 0)
            rough = rough_s[rows, :]
            cs = cs_first if i == 0 else cs_last if i == tiles - 2 else slope_rate
            qe = face(level, pltpu.roll(level, wide - 1, 1), mbe_s[rows, :], rough, qe_s[rows, :], ce)
            below_level = jnp.where(sub == 7, nxt_up, up)
            qs = face(level, below_level, mbs_s[rows, :], rough, qs_s[rows, :], cs)
            qe_s[rows, :] = qe
            qs_s[rows, :] = qs
            turned = pltpu.roll(qs, 1, 0)
            north = jnp.where(sub == 0, north_turned, turned)
            north_turned = turned
            gained = pltpu.roll(qe, 1, 1) - qe + north - qs
            level_s[rows, :] = level + gained
        return carry

    lax.fori_loop(0, SUBSTEPS, substep, 0)
    inner = slice(HALO, HALO + height)
    water_out[...] = level_s[inner, :width] - bed_s[inner, :width]
    east_out[...] = (1.0 / share) * qe_s[inner, :width]
    south_out[...] = (1.0 / share) * qs_s[inner, :width]


def shaped(*shape):
    return jax.ShapeDtypeStruct(shape, F32)


def call(kernel, out_shape, specs, scratch=(), flops=0, size=0, exps=0, limit=16 * 1024 * 1024, outside=False):
    return pl.pallas_call(
        kernel,
        out_shape=out_shape,
        in_specs=specs,
        out_specs=jax.tree.map(lambda _: HBM if outside else VMEM, out_shape),
        scratch_shapes=list(scratch),
        compiler_params=pltpu.CompilerParams(vmem_limit_bytes=limit),
        cost_estimate=pl.CostEstimate(flops=flops, bytes_accessed=size, transcendentals=exps),
        name=kernel.__name__,
    )


def per_device(
    water_depth, flux_east, flux_south, bed_level, roughness, link_rows, link_blocks,
    reach_inverse, reach_source, river_section, block_level, block_down,
):
    tiles = lax.axis_size("tile")
    bands = lax.axis_size("band")
    tile_index = lax.axis_index("tile")
    band_index = lax.axis_index("band")
    height, width = water_depth.shape
    blocks, reach = reach_source.shape
    total = tiles * CHUNK
    links = link_rows.shape[-1]
    ring = [[(i, i ^ k) for i in range(bands)] for k in range(bands)]

    down = block_down.reshape(1, blocks)
    edge = shaped(5 * HALO, width)
    payload, slots, last_row, edge_a, edge_b = call(
        pack_kernel,
        (shaped(total, LANES), shaped(8, links), shaped(blocks, reach), edge, edge),
        [HBM] * 9,
        scratch=[
            pltpu.VMEM((height, width), F32),
            pltpu.VMEM((height, width), F32),
            pltpu.VMEM((1, links), jnp.int32),
            pltpu.VMEM((1, links), jnp.int32),
            pltpu.VMEM((blocks, 16, reach), BF16),
            pltpu.VMEM((8, LANES), F32),
            pltpu.VMEM((1, blocks), jnp.int32),
            pltpu.VMEM((total, LANES), F32),
            pltpu.VMEM((8, links), F32),
            pltpu.VMEM((blocks, reach), F32),
            pltpu.VMEM((5 * HALO, width), F32),
            pltpu.VMEM((5 * HALO, width), F32),
            pltpu.SemaphoreType.DMA((12,)),
            pltpu.SemaphoreType.DMA((8,)),
        ],
        limit=None,
        outside=True,
        flops=10**9,
        size=10**6,
    )(
        water_depth,
        bed_level,
        link_rows.reshape(1, links),
        link_blocks.reshape(1, links),
        reach_inverse,
        roughness,
        flux_east,
        flux_south,
        down,
    )
    rows_in = lax.all_to_all(
        payload.reshape(tiles, CHUNK, 1, LANES), "tile", split_axis=0, concat_axis=0, tiled=True
    )

    fields = (water_depth, bed_level, roughness, flux_east, flux_south)
    def pairs(count, first):
        return [(j, i) for k in range(first, count - 1, 2) for i, j in ((k, k + 1), (k + 1, k))]

    got_a = lax.ppermute(edge_a, "band", pairs(bands, 0))
    got_b = lax.ppermute(edge_b, "band", pairs(bands, 1))
    hot = call(
        hot_kernel, jax.ShapeDtypeStruct((links, total), BF16), [VMEM], flops=10**8, size=10**6
    )(slots)
    side_a, side_b = call(
        strips_kernel, (shaped(48, LANES), shaped(48, LANES)), [VMEM] * 7 + [ANY], flops=10**6, size=10**6
    )(got_a, got_b, *fields, hot)
    col_a = lax.ppermute(side_a, "tile", pairs(tiles, 0))
    col_b = lax.ppermute(side_b, "tile", pairs(tiles, 1))

    answer, source = call(
        lateral_kernel,
        (shaped(total, LANES), shaped(blocks, LANES)),
        [VMEM] * 4 + [ANY] * 2,
        flops=10**9,
        size=10**6,
    )(rows_in.reshape(total, LANES), river_section, reach_source, last_row, col_a, col_b)
    returned = lax.all_to_all(
        answer.reshape(tiles, CHUNK, 1, LANES), "tile", split_axis=0, concat_axis=0, tiled=True
    )

    wide = width + LANES
    tall = height + 2 * HALO
    water_now, final_east, final_south = call(
        flood_kernel,
        (shaped(height, width),) * 3,
        [VMEM] * 9,
        scratch=[pltpu.VMEM((tall, wide), F32)] * 7,
        flops=10**8,
        size=10**7,
        exps=10**7,
    )(got_a, got_b, col_a, col_b, *fields)
    base_flow, column = call(
        flow_kernel, (shaped(blocks, reach),) * 2, [VMEM] * 2, flops=10**8, size=10**6
    )(source, reach_inverse)
    extras = rows_in.reshape(tiles, CHUNK, LANES)[:, SLOTS, :]
    others = [lax.ppermute(extras, "band", ring[k]) for k in (3, 2, 1)][::-1]
    reached = call(
        paths_kernel, shaped(LANES, tiles * blocks), [VMEM] * 4, flops=10**9, size=10**6
    )(extras, *others)

    pushed = call(gather_kernel, shaped(8, LANES), [VMEM] * 2, flops=10**6, size=10**6)(
        returned.reshape(total, LANES), reached
    )
    parts = [pushed] + [lax.ppermute(pushed, "band", ring[k]) for k in (3, 2, 1)]
    final_depth = call(
        final_kernel, shaped(height, width), [VMEM] * 3, flops=10**9, size=10**6
    )(water_now, returned.reshape(total, LANES), hot)
    discharge = call(
        discharge_kernel, shaped(blocks, reach), [VMEM] * 6, flops=10**4, size=10**4
    )(base_flow, column, *parts)
    return (final_depth, final_east, final_south, discharge)


def solution(mesh):
    grid = P("band", "tile")
    owned = P(("tile", "band"))
    lists = P("tile", "band", None)
    return jax.shard_map(
        per_device,
        mesh=mesh,
        in_specs=(grid,) * 5 + (lists,) * 2 + (owned,) * 5,
        out_specs=(grid, grid, grid, owned),
        check_vma=False,
    )
```

```python
import jax
import jax.numpy as jnp
from jax import lax
from jax.experimental import pallas as pl
from jax.experimental.pallas import tpu as pltpu
from jax.sharding import PartitionSpec as P

SUBSTEPS = 8
LEVELS = 8
HALO = 8
LANES = 128
SLOTS = 16
CHUNK = SLOTS + 1
GAIN_LANE = 64
ID_LANE = 96

GRAVITY = 9.81
TIME_STEP = 3.0
CELL_WIDTH = 30.0
DEPTH_FLOOR = 0.2
FRICTION_POWER = 7.0 / 3.0
LATERAL_RATE = 0.2
PLAIN_SHARE = 0.8
RIVER_SHARE = 0.25

F32 = jnp.float32
BF16 = jnp.bfloat16
VMEM = pl.BlockSpec(memory_space=pltpu.VMEM)
HBM = pl.BlockSpec(memory_space=pltpu.HBM)
ANY = pl.BlockSpec(memory_space=pl.ANY)


def iota(shape, dim):
    return lax.broadcasted_iota(jnp.int32, shape, dim)


def halves(x):
    hi = x.astype(BF16)
    lo = (x - hi.astype(F32)).astype(BF16)
    return hi, lo


def paired(x):
    hi, lo = halves(x)
    return jnp.concatenate([hi, lo], axis=1)


def fold(x):
    return x[:, :LANES] + x[:, LANES:]


def mm(a, b, dims=((1,), (0,))):
    return lax.dot_general(a, b, (dims, ((), ())), preferred_element_type=F32)


def pack_kernel(
    water_h, bed_h, rows_h, blocks_h, inverse_h, rough_h, east_h, south_h, down_h,
    out_h, slots_h, last_h, edge_a_h, edge_b_h,
    water, bed, link_rows, link_blocks, tails, row_s, down,
    out, slots, last_out, edge_a, edge_b, sems, out_sems,
):
    blocks_own, reach = last_out.shape
    moves = (
        (rows_h, link_rows),
        (blocks_h, link_blocks),
        (water_h, water),
        (bed_h, bed),
        (inverse_h.at[:, reach - 16 : reach, :], tails),
        (down_h, down),
    )
    height = water.shape[0]
    odd = lax.axis_index("band") % 2
    start_a = pl.multiple_of((1 - odd) * (height - HALO), HALO)
    start_b = pl.multiple_of(odd * (height - HALO), HALO)
    for a, field in enumerate((rough_h, east_h, south_h)):
        rows = pl.ds((a + 2) * HALO, HALO)
        moves += (
            (field.at[pl.ds(start_a, HALO), :], edge_a.at[rows, :]),
            (field.at[pl.ds(start_b, HALO), :], edge_b.at[rows, :]),
        )
    copies = [pltpu.make_async_copy(src, dst, sems.at[i]) for i, (src, dst) in enumerate(moves)]
    for copy in copies:
        copy.start()
    sent = []

    def send(src, dst):
        sent.append(pltpu.make_async_copy(src, dst, out_sems.at[len(sent)]))
        sent[-1].start()

    copies[0].wait()
    copies[1].wait()
    rows = link_rows[...]
    blocks = link_blocks[...]
    links = rows.shape[1]
    groups = water.shape[1] // LANES
    tiles = out.shape[0] // CHUNK
    place = ((rows % groups) * height + rows // groups).astype(F32)
    dest = (blocks >> 7).astype(F32)
    local = (blocks & 31).astype(F32)
    pick = iota((8, links), 0)
    stacked = jnp.where(pick == 0, place, jnp.where(pick == 1, dest, local))
    turned = jnp.transpose(stacked)
    place_c, dest_c, local_c = turned[:, 0:1], turned[:, 1:2], turned[:, 2:3]
    earlier = (dest_c == dest) & (iota((links, links), 1) < iota((links, links), 0))
    ones = jnp.ones((links, LANES), BF16)
    rank = mm(earlier.astype(F32).astype(BF16), ones)
    position = dest_c * float(CHUNK) + rank
    position_c = position[:, 0:1]
    lane = iota((links, links), 1).astype(F32)
    slot_of = jnp.sum(jnp.where(place_c == lane, position_c, 0.0), axis=0, keepdims=True)
    slots[...] = jnp.broadcast_to(slot_of, slots.shape)
    send(slots, slots_h)
    copies[2].wait()
    copies[3].wait()
    level = water[...] + bed[...]
    for edge, start in ((edge_a, start_a), (edge_b, start_b)):
        edge[HALO : 2 * HALO, :] = bed[pl.ds(start, HALO), :]
        edge[0:HALO, :] = water[pl.ds(start, HALO), :] + bed[pl.ds(start, HALO), :]
    by_block = jnp.concatenate(
        [level[:, c * LANES : (c + 1) * LANES] for c in range(groups)], axis=0
    )
    by_block = paired(by_block)
    dest_hot = (iota((tiles, links), 0).astype(F32) == dest).astype(F32).astype(BF16)
    seat = iota((links, LANES), 1).astype(F32) - float(ID_LANE)
    rank_hot = jnp.where(rank == seat, local_c + 1.0, 0.0)
    ids = mm(dest_hot, rank_hot.astype(BF16))
    for copy in copies[4:]:
        copy.wait()
    last = tails[...].astype(F32)[:, 15, :]
    last_out[...] = last
    send(last_out, last_h)
    send(edge_a, edge_a_h)
    send(edge_b, edge_b_h)
    first = (iota((8, reach), 1) == 0).astype(F32).astype(BF16)
    seated = jnp.concatenate(
        [jnp.zeros((GAIN_LANE, reach), F32), last, jnp.zeros((LANES - GAIN_LANE - blocks_own, reach), F32)],
        axis=0,
    )
    gain = mm(first, seated.astype(BF16), ((1,), (1,)))
    row_s[...] = jnp.zeros(row_s.shape, F32)
    row_s[0:1, 0:blocks_own] = down[...].astype(F32)
    extras = ids + (row_s[0:1, :] + gain[0:1, :])
    parts = 4
    size, chunks = out.shape[0] // parts, tiles // parts
    for part in range(parts):
        rows = slice(part * size, (part + 1) * size)
        hot = (iota((size, links), 0) + part * size).astype(F32) == slot_of
        out[rows, :] = fold(mm(jnp.where(hot, 1.0, 0.0).astype(BF16), by_block))
        out[pl.ds(part * size + SLOTS, chunks, CHUNK), :] = extras[part * chunks : (part + 1) * chunks]
        send(out.at[rows, :], out_h.at[rows, :])
    for copy in sent:
        copy.wait()


def lateral_kernel(rows_in, section, reach_source, last_row, order0, order1, out, source):
    total = rows_in.shape[0]
    tiles = total // CHUNK
    blocks = section.shape[0]
    slot = iota((total, 1), 0).astype(F32)
    owner = jnp.floor((slot + 0.5) * (1.0 / CHUNK))
    within = slot - owner * CHUNK + ID_LANE
    lane = iota((total, LANES), 1).astype(F32)
    extras = rows_in[pl.ds(SLOTS, tiles, CHUNK), :]
    ids_here = iota((tiles, LANES), 1)
    ids_here = (ids_here >= ID_LANE) & (ids_here < ID_LANE + SLOTS)
    ids = jnp.where(ids_here, extras, 0.0).astype(BF16)
    spread = (iota((total, tiles), 1).astype(F32) == owner).astype(F32).astype(BF16)
    seat = jnp.where(lane == within, mm(spread, ids), 0.0)
    block = mm(seat.astype(BF16), jnp.ones((LANES, LANES), BF16)) - 1.0
    hot = (block == lane).astype(F32).astype(BF16)
    rows = rows_in[...]
    counted = jnp.concatenate([paired(rows), jnp.ones((total, LANES), BF16)], axis=1)
    found = mm(hot, counted, ((0,), (0,)))[:blocks]
    sums = fold(found[:, : 2 * LANES]) - found[:, 2 * LANES :] * section[...]
    src = reach_source[...] + (RIVER_SHARE * LATERAL_RATE) * sums
    section_in = fold(mm(hot[:, :blocks], paired(section[...])))
    out[...] = jnp.where(block >= 0.0, LATERAL_RATE * (rows - section_in), 0.0)
    source[...] = src
    ends = jnp.concatenate([src * last_row[...], jnp.zeros((LANES - blocks, LANES), F32)], axis=0)
    ends_hi, ends_lo = halves(ends)
    ones = jnp.ones((8, LANES), BF16)
    row = mm(ones, ends_hi, ((1,), (1,))) + mm(ones, ends_lo, ((1,), (1,)))
    out[pl.ds(SLOTS, tiles, CHUNK), :] = jnp.broadcast_to(row[0:1, :], (tiles, LANES))


def dense(ref, blocks, start, step, count):
    turns = LANES // blocks
    group = iota((count // turns, LANES), 1) // blocks
    rows = jnp.zeros((count // turns, LANES), F32)
    for turn in range(turns):
        x = ref[pl.ds(start + turn * step, count // turns, turns * step), :]
        x = pltpu.roll(x, turn * blocks, 1) if turn else x
        rows = jnp.where(group == turn, x, rows)
    return rows


def paths_kernel(own, one, two, three, reach):
    bands = 4
    band, me = lax.axis_index("band"), lax.axis_index("tile").astype(F32) + 1.0
    tiles = own.shape[0]
    blocks = LANES // bands
    group = iota((tiles, LANES), 1) // blocks
    downs = jnp.zeros((tiles, LANES), F32)
    gains = jnp.zeros((tiles, LANES), F32)
    for back, ref in enumerate((own, one, two, three)):
        here = group == band ^ back
        x = ref[...]
        down, gain = x, x
        for turn in (1, 2, 3):
            y = pltpu.roll(x, turn * blocks, 1)
            down = jnp.where(group == turn, y, down)
            gain = jnp.where(group == (turn + GAIN_LANE // blocks) % bands, y, gain)
        downs = jnp.where(here, down, downs)
        gains = jnp.where(here, gain, gains)
    high = jnp.floor(downs * (1.0 / LANES))
    tables = jnp.concatenate([high + 1.0, downs - high * LANES, gains], axis=0).astype(BF16)
    sources = dense(own, blocks, 0, 1, tiles)
    chunks = sources.shape[0]
    high = jnp.floor(sources * (1.0 / LANES))
    low = sources - high * LANES
    high = high + 1.0
    tile_row = iota((tiles, LANES), 0).astype(F32) + 1.0
    block_row = iota((LANES, LANES), 0).astype(F32)
    state = [(high[i : i + 1], low[i : i + 1], jnp.ones((1, LANES), F32)) for i in range(chunks)]
    for hop in range(LEVELS - 1):
        for i in range(0, chunks, 2):
            hits = [block_row == state[k][1] for k in (i, i + 1)]
            if hop < LEVELS - 2:
                hot = jnp.concatenate([jnp.where(hit, 1.0, 0.0).astype(BF16) for hit in hits], axis=1)
                founds = mm(tables, hot)
            for k, hit in zip((i, i + 1), hits):
                hi, lo, factor = state[k]
                cols = slice(k * LANES, (k + 1) * LANES)
                mine = jnp.where(hit, jnp.where(hi == me, factor, 0.0), 0.0)
                reach[:, cols] = mine if hop == 0 else reach[:, cols] + mine
                if hop < LEVELS - 2:
                    found = founds[:, (k - i) * LANES : (k - i + 1) * LANES]
                    here = tile_row == hi
                    picks = [
                        jnp.sum(jnp.where(here, found[p * tiles : (p + 1) * tiles], 0.0), axis=0, keepdims=True)
                        for p in range(3)
                    ]
                    state[k] = (picks[0], picks[1], factor * picks[2])


def gather_kernel(returned, reach, out):
    tiles = returned.shape[0] // CHUNK
    blocks = reach.shape[1] // tiles
    ends = dense(returned, blocks, SLOTS, CHUNK, tiles)
    total = jnp.zeros((LANES, LANES), F32)
    for i in range(ends.shape[0]):
        total = total + reach[:, i * LANES : (i + 1) * LANES] * ends[i : i + 1, :]
    hi, lo = halves(total)
    ones = jnp.ones((8, LANES), BF16)
    out[...] = mm(ones, hi, ((1,), (1,))) + mm(ones, lo, ((1,), (1,)))


def flow_kernel(source, inverse, base, column):
    blocks = source.shape[0]
    hi, lo = halves(source[...])
    first = (iota((blocks, LANES), 1) == 0).astype(F32).astype(BF16)
    stacked = jnp.concatenate([hi, lo, first], axis=0)
    row = iota((blocks, LANES), 0)
    base_now = jnp.zeros((blocks, LANES), F32)
    column_now = jnp.zeros((blocks, LANES), F32)
    for g in range(blocks):
        x = mm(stacked, inverse[g], ((1,), (1,)))
        base_now = jnp.where(row == g, x[:blocks] + x[blocks : 2 * blocks], base_now)
        column_now = jnp.where(row == g, x[2 * blocks :], column_now)
    base[...] = base_now
    column[...] = column_now


def discharge_kernel(base, column, own, one, two, three, out):
    blocks = base.shape[0]
    band = lax.axis_index("band")
    total = own[...] + one[...] + two[...] + three[...]
    turned = jnp.transpose(total)[:, 0:1]
    inflow = turned[0:blocks]
    for b in range(1, LANES // blocks):
        inflow = jnp.where(band == b, turned[b * blocks : (b + 1) * blocks], inflow)
    out[...] = base[...] + column[...] * inflow


def hot_kernel(slots, out):
    slot_c = jnp.transpose(slots[...])[:, 0:1]
    hot = iota(out.shape, 1).astype(F32) == slot_c
    out[...] = jnp.where(hot, 1.0, 0.0).astype(BF16)


def final_kernel(water, returned, hot, out):
    height = water.shape[0]
    groups = water.shape[1] // LANES
    lateral = fold(mm(hot[...], paired(returned[...])))
    for c in range(groups):
        cols = slice(c * LANES, (c + 1) * LANES)
        out[:, cols] = water[:, cols] - PLAIN_SHARE * lateral[c * height : (c + 1) * height]


def strips_kernel(got_a, got_b, f0, f1, f2, f3, f4, order, side_a, side_b):
    fields = (f0, f1, f2, f3, f4)
    height, width = f0.shape
    tiles = height // 8 + 2
    lane = iota((8, LANES), 1)
    groups = side_a.shape[0] // 8
    odd_band, odd_tile = lax.axis_index("band") % 2 == 1, lax.axis_index("tile") % 2 == 1
    lefts = [jnp.zeros((8, LANES), F32) for _ in range(groups)]
    rights = [jnp.zeros((8, LANES), F32) for _ in range(groups)]
    for a, field in enumerate(fields):
        for i in range(tiles):
            strip = a * tiles + i
            v, off = strip // 16, (strip % 16) * 8
            here = (lane >= off) & (lane < off + 8)
            first, last = slice(0, LANES), slice(width - LANES, width)
            if i in (0, tiles - 1):
                rows = slice(a * HALO, a * HALO + 8)
                from_a = odd_band if i == 0 else jnp.logical_not(odd_band)
                x = jnp.where(from_a, got_a[rows, first], got_b[rows, first])
                y = jnp.where(from_a, got_a[rows, last], got_b[rows, last])
            else:
                rows = slice(8 * i - 8, 8 * i)
                x, y = field[rows, first], field[rows, last]
                if a == 0:
                    x, y = x + f1[rows, first], y + f1[rows, last]
            x = pltpu.roll(x, off, 1) if off else x
            y = pltpu.roll(y, (off + 8) % LANES, 1) if (off + 8) % LANES else y
            lefts[v] = jnp.where(here, x, lefts[v])
            rights[v] = jnp.where(here, y, rights[v])
    for v in range(groups):
        side_a[8 * v : 8 * v + 8, :] = jnp.where(odd_tile, lefts[v], rights[v])
        side_b[8 * v : 8 * v + 8, :] = jnp.where(odd_tile, rights[v], lefts[v])


def flood_kernel(
    got_a, got_b, col_a, col_b, f0, f1, f2, f3, f4,
    water_out, east_out, south_out,
    level_s, bed_s, rough_s, qe_s, qs_s, mbe_s, mbs_s,
):
    height, width = f0.shape
    tiles = height // 8 + 2
    wide = width + LANES
    lane1 = iota((8, LANES), 1)
    scratch = (level_s, bed_s, rough_s, qe_s, qs_s)
    share = TIME_STEP / CELL_WIDTH
    rate = GRAVITY * TIME_STEP
    slope_rate = share * rate / CELL_WIDTH
    tile_index, band_index = lax.axis_index("tile"), lax.axis_index("band")
    tile_last, band_last = lax.axis_size("tile") - 1, lax.axis_size("band") - 1
    odd_band, odd_tile = band_index % 2 == 1, tile_index % 2 == 1
    easts, wests = [], []
    for v in range(col_a.shape[0] // 8):
        x, y = col_a[8 * v : 8 * v + 8, :], col_b[8 * v : 8 * v + 8, :]
        easts.append(jnp.where(odd_tile, y, x))
        wests.append(jnp.where(odd_tile, x, y))
    for a, (field, dst) in enumerate(zip((f0, f1, f2, f3, f4), scratch)):
        for i in range(tiles):
            strip = a * tiles + i
            v, off = strip // 16, (strip % 16) * 8
            x, y = easts[v], wests[v]
            x = pltpu.roll(x, LANES - off, 1) if off else x
            y = pltpu.roll(y, (LANES - 8 - off) % LANES, 1) if (LANES - 8 - off) % LANES else y
            edge = jnp.where(lane1 < 8, x, jnp.where(lane1 >= LANES - 8, y, 0.0))
            if i in (0, tiles - 1):
                rows = slice(a * HALO, a * HALO + 8)
                from_a = odd_band if i == 0 else jnp.logical_not(odd_band)
                body = jnp.where(from_a, got_a[rows, :], got_b[rows, :])
            else:
                rows = slice(8 * i - 8, 8 * i)
                body = field[rows, :]
                if a == 0:
                    body = body + f1[rows, :]
            if a >= 2:
                scale = rate / share if a == 2 else share
                body, edge = scale * body, scale * edge
            dst[8 * i : 8 * i + 8, :width] = body
            dst[8 * i : 8 * i + 8, width:] = edge
    lane = iota((8, wide), 1)
    sub = iota((8, wide), 0)
    shut_e = ((lane == width - 1) & (tile_index == tile_last)) | ((lane == wide - 1) & (tile_index == 0))
    ce = jnp.where(shut_e, 0.0, slope_rate)
    shut_n = (sub == 7) & (band_index == 0)
    shut_s = (sub == 7) & (band_index == band_last)
    cs_first = jnp.where(shut_n, 0.0, slope_rate)
    cs_last = jnp.where(shut_s, 0.0, slope_rate)
    nxt = bed_s[0:8, :]
    nxt_up = pltpu.roll(nxt, 7, 0)
    for i in range(tiles):
        rows = slice(8 * i, 8 * i + 8)
        bed, up = nxt, nxt_up
        if i + 1 < tiles:
            nxt = bed_s[8 * i + 8 : 8 * i + 16, :]
            nxt_up = pltpu.roll(nxt, 7, 0)
        mbe_s[rows, :] = jnp.maximum(bed, pltpu.roll(bed, wide - 1, 1))
        mbs_s[rows, :] = jnp.maximum(bed, jnp.where(sub == 7, nxt_up, up))
        qe_s[rows, :] = jnp.where(shut_e, 0.0, qe_s[rows, :])
    last = slice(height, height + 8)
    qs_s[last, :] = jnp.where(shut_s, 0.0, qs_s[last, :])

    def face(here, ahead, bed_max, rough, old, factor):
        depth = jnp.maximum(jnp.maximum(here, ahead) - bed_max, DEPTH_FLOOR)
        drag = rough * jnp.abs(old) * jnp.exp2(-FRICTION_POWER * jnp.log2(depth)) + 1.0
        near = pl.reciprocal(drag, approx=True)
        return (old - factor * depth * (ahead - here)) * near

    def substep(_, carry):
        nxt = level_s[0:8, :]
        nxt_up = pltpu.roll(nxt, 7, 0)
        north_turned = jnp.zeros((8, wide), F32)
        for i in range(tiles):
            rows = slice(8 * i, 8 * i + 8)
            level, up = nxt, nxt_up
            if i + 1 < tiles:
                nxt = level_s[8 * i + 8 : 8 * i + 16, :]
                nxt_up = pltpu.roll(nxt, 7, 0)
            rough = rough_s[rows, :]
            cs = cs_first if i == 0 else cs_last if i == tiles - 2 else slope_rate
            qe = face(level, pltpu.roll(level, wide - 1, 1), mbe_s[rows, :], rough, qe_s[rows, :], ce)
            below_level = jnp.where(sub == 7, nxt_up, up)
            qs = face(level, below_level, mbs_s[rows, :], rough, qs_s[rows, :], cs)
            qe_s[rows, :] = qe
            qs_s[rows, :] = qs
            turned = pltpu.roll(qs, 1, 0)
            north = jnp.where(sub == 0, north_turned, turned)
            north_turned = turned
            gained = pltpu.roll(qe, 1, 1) - qe + north - qs
            level_s[rows, :] = level + gained
        return carry

    lax.fori_loop(0, SUBSTEPS, substep, 0)
    inner = slice(HALO, HALO + height)
    water_out[...] = level_s[inner, :width] - bed_s[inner, :width]
    east_out[...] = (1.0 / share) * qe_s[inner, :width]
    south_out[...] = (1.0 / share) * qs_s[inner, :width]


def shaped(*shape):
    return jax.ShapeDtypeStruct(shape, F32)


def call(kernel, out_shape, specs, scratch=(), flops=0, size=0, exps=0, limit=16 * 1024 * 1024, outside=False):
    return pl.pallas_call(
        kernel,
        out_shape=out_shape,
        in_specs=specs,
        out_specs=jax.tree.map(lambda _: HBM if outside else VMEM, out_shape),
        scratch_shapes=list(scratch),
        compiler_params=pltpu.CompilerParams(vmem_limit_bytes=limit),
        cost_estimate=pl.CostEstimate(flops=flops, bytes_accessed=size, transcendentals=exps),
        name=kernel.__name__,
    )


def per_device(
    water_depth, flux_east, flux_south, bed_level, roughness, link_rows, link_blocks,
    reach_inverse, reach_source, river_section, block_level, block_down,
):
    tiles = lax.axis_size("tile")
    bands = lax.axis_size("band")
    tile_index = lax.axis_index("tile")
    band_index = lax.axis_index("band")
    height, width = water_depth.shape
    blocks, reach = reach_source.shape
    total = tiles * CHUNK
    links = link_rows.shape[-1]
    ring = [[(i, i ^ k) for i in range(bands)] for k in range(bands)]

    down = block_down.reshape(1, blocks)
    edge = shaped(5 * HALO, width)
    payload, slots, last_row, edge_a, edge_b = call(
        pack_kernel,
        (shaped(total, LANES), shaped(8, links), shaped(blocks, reach), edge, edge),
        [HBM] * 9,
        scratch=[
            pltpu.VMEM((height, width), F32),
            pltpu.VMEM((height, width), F32),
            pltpu.VMEM((1, links), jnp.int32),
            pltpu.VMEM((1, links), jnp.int32),
            pltpu.VMEM((blocks, 16, reach), BF16),
            pltpu.VMEM((8, LANES), F32),
            pltpu.VMEM((1, blocks), jnp.int32),
            pltpu.VMEM((total, LANES), F32),
            pltpu.VMEM((8, links), F32),
            pltpu.VMEM((blocks, reach), F32),
            pltpu.VMEM((5 * HALO, width), F32),
            pltpu.VMEM((5 * HALO, width), F32),
            pltpu.SemaphoreType.DMA((12,)),
            pltpu.SemaphoreType.DMA((8,)),
        ],
        limit=None,
        outside=True,
        flops=10**9,
        size=10**6,
    )(
        water_depth,
        bed_level,
        link_rows.reshape(1, links),
        link_blocks.reshape(1, links),
        reach_inverse,
        roughness,
        flux_east,
        flux_south,
        down,
    )
    rows_in = lax.all_to_all(
        payload.reshape(tiles, CHUNK, 1, LANES), "tile", split_axis=0, concat_axis=0, tiled=True
    )

    fields = (water_depth, bed_level, roughness, flux_east, flux_south)
    def pairs(count, first):
        return [(j, i) for k in range(first, count - 1, 2) for i, j in ((k, k + 1), (k + 1, k))]

    got_a = lax.ppermute(edge_a, "band", pairs(bands, 0))
    got_b = lax.ppermute(edge_b, "band", pairs(bands, 1))
    hot = call(
        hot_kernel, jax.ShapeDtypeStruct((links, total), BF16), [VMEM], flops=10**8, size=10**6
    )(slots)
    side_a, side_b = call(
        strips_kernel, (shaped(48, LANES), shaped(48, LANES)), [VMEM] * 7 + [ANY], flops=10**6, size=10**6
    )(got_a, got_b, *fields, hot)
    col_a = lax.ppermute(side_a, "tile", pairs(tiles, 0))
    col_b = lax.ppermute(side_b, "tile", pairs(tiles, 1))

    answer, source = call(
        lateral_kernel,
        (shaped(total, LANES), shaped(blocks, LANES)),
        [VMEM] * 4 + [ANY] * 2,
        flops=10**9,
        size=10**6,
    )(rows_in.reshape(total, LANES), river_section, reach_source, last_row, col_a, col_b)
    returned = lax.all_to_all(
        answer.reshape(tiles, CHUNK, 1, LANES), "tile", split_axis=0, concat_axis=0, tiled=True
    )

    wide = width + LANES
    tall = height + 2 * HALO
    water_now, final_east, final_south = call(
        flood_kernel,
        (shaped(height, width),) * 3,
        [VMEM] * 9,
        scratch=[pltpu.VMEM((tall, wide), F32)] * 7,
        flops=10**8,
        size=10**7,
        exps=10**7,
    )(got_a, got_b, col_a, col_b, *fields)
    base_flow, column = call(
        flow_kernel, (shaped(blocks, reach),) * 2, [VMEM] * 2, flops=10**8, size=10**6
    )(source, reach_inverse)
    extras = rows_in.reshape(tiles, CHUNK, LANES)[:, SLOTS, :]
    others = [lax.ppermute(extras, "band", ring[k]) for k in (3, 2, 1)][::-1]
    reached = call(
        paths_kernel, shaped(LANES, tiles * blocks), [VMEM] * 4, flops=10**9, size=10**6
    )(extras, *others)

    pushed = call(gather_kernel, shaped(8, LANES), [VMEM] * 2, flops=10**6, size=10**6)(
        returned.reshape(total, LANES), reached
    )
    parts = [pushed] + [lax.ppermute(pushed, "band", ring[k]) for k in (3, 2, 1)]
    final_depth = call(
        final_kernel, shaped(height, width), [VMEM] * 3, flops=10**9, size=10**6
    )(water_now, returned.reshape(total, LANES), hot)
    discharge = call(
        discharge_kernel, shaped(blocks, reach), [VMEM] * 6, flops=10**4, size=10**4
    )(base_flow, column, *parts)
    return (final_depth, final_east, final_south, discharge)


def solution(mesh):
    grid = P("band", "tile")
    owned = P(("tile", "band"))
    lists = P("tile", "band", None)
    return jax.shard_map(
        per_device,
        mesh=mesh,
        in_specs=(grid,) * 5 + (lists,) * 2 + (owned,) * 5,
        out_specs=(grid, grid, grid, owned),
        check_vma=False,
    )
```

```python
import jax
import jax.numpy as jnp
from jax import lax
from jax.experimental import pallas as pl
from jax.experimental.pallas import tpu as pltpu
from jax.sharding import PartitionSpec as P

SUBSTEPS = 8
LEVELS = 8
HALO = 8
LANES = 128
SLOTS = 16
CHUNK = SLOTS + 1
GAIN_LANE = 64
ID_LANE = 96

GRAVITY = 9.81
TIME_STEP = 3.0
CELL_WIDTH = 30.0
DEPTH_FLOOR = 0.2
FRICTION_POWER = 7.0 / 3.0
LATERAL_RATE = 0.2
PLAIN_SHARE = 0.8
RIVER_SHARE = 0.25

F32 = jnp.float32
BF16 = jnp.bfloat16
VMEM = pl.BlockSpec(memory_space=pltpu.VMEM)
HBM = pl.BlockSpec(memory_space=pltpu.HBM)
ANY = pl.BlockSpec(memory_space=pl.ANY)


def iota(shape, dim):
    return lax.broadcasted_iota(jnp.int32, shape, dim)


def halves(x):
    hi = x.astype(BF16)
    lo = (x - hi.astype(F32)).astype(BF16)
    return hi, lo


def paired(x):
    hi, lo = halves(x)
    return jnp.concatenate([hi, lo], axis=1)


def fold(x):
    return x[:, :LANES] + x[:, LANES:]


def mm(a, b, dims=((1,), (0,))):
    return lax.dot_general(a, b, (dims, ((), ())), preferred_element_type=F32)


def pack_kernel(
    water_h, bed_h, rows_h, blocks_h, inverse_h, rough_h, east_h, south_h, down_h,
    out_h, slots_h, last_h, edge_a_h, edge_b_h,
    water, bed, link_rows, link_blocks, tails, row_s, down,
    out, slots, last_out, edge_a, edge_b, sems, out_sems,
):
    blocks_own, reach = last_out.shape
    moves = (
        (rows_h, link_rows),
        (blocks_h, link_blocks),
        (water_h, water),
        (bed_h, bed),
        (inverse_h.at[:, reach - 16 : reach, :], tails),
        (down_h, down),
    )
    height = water.shape[0]
    odd = lax.axis_index("band") % 2
    start_a = pl.multiple_of((1 - odd) * (height - HALO), HALO)
    start_b = pl.multiple_of(odd * (height - HALO), HALO)
    for a, field in enumerate((rough_h, east_h, south_h)):
        rows = pl.ds((a + 2) * HALO, HALO)
        moves += (
            (field.at[pl.ds(start_a, HALO), :], edge_a.at[rows, :]),
            (field.at[pl.ds(start_b, HALO), :], edge_b.at[rows, :]),
        )
    copies = [pltpu.make_async_copy(src, dst, sems.at[i]) for i, (src, dst) in enumerate(moves)]
    for copy in copies:
        copy.start()
    sent = []

    def send(src, dst):
        sent.append(pltpu.make_async_copy(src, dst, out_sems.at[len(sent)]))
        sent[-1].start()

    copies[0].wait()
    copies[1].wait()
    rows = link_rows[...]
    blocks = link_blocks[...]
    links = rows.shape[1]
    groups = water.shape[1] // LANES
    tiles = out.shape[0] // CHUNK
    place = ((rows % groups) * height + rows // groups).astype(F32)
    dest = (blocks >> 7).astype(F32)
    local = (blocks & 31).astype(F32)
    pick = iota((8, links), 0)
    stacked = jnp.where(pick == 0, place, jnp.where(pick == 1, dest, local))
    turned = jnp.transpose(stacked)
    place_c, dest_c, local_c = turned[:, 0:1], turned[:, 1:2], turned[:, 2:3]
    earlier = (dest_c == dest) & (iota((links, links), 1) < iota((links, links), 0))
    ones = jnp.ones((links, LANES), BF16)
    rank = mm(earlier.astype(F32).astype(BF16), ones)
    position = dest_c * float(CHUNK) + rank
    position_c = position[:, 0:1]
    lane = iota((links, links), 1).astype(F32)
    slot_of = jnp.sum(jnp.where(place_c == lane, position_c, 0.0), axis=0, keepdims=True)
    slots[...] = jnp.broadcast_to(slot_of, slots.shape)
    send(slots, slots_h)
    copies[2].wait()
    copies[3].wait()
    level = water[...] + bed[...]
    for edge, start in ((edge_a, start_a), (edge_b, start_b)):
        edge[HALO : 2 * HALO, :] = bed[pl.ds(start, HALO), :]
        edge[0:HALO, :] = water[pl.ds(start, HALO), :] + bed[pl.ds(start, HALO), :]
    by_block = jnp.concatenate(
        [level[:, c * LANES : (c + 1) * LANES] for c in range(groups)], axis=0
    )
    by_block = paired(by_block)
    dest_hot = (iota((tiles, links), 0).astype(F32) == dest).astype(F32).astype(BF16)
    seat = iota((links, LANES), 1).astype(F32) - float(ID_LANE)
    rank_hot = jnp.where(rank == seat, local_c + 1.0, 0.0)
    ids = mm(dest_hot, rank_hot.astype(BF16))
    for copy in copies[4:]:
        copy.wait()
    last = tails[...].astype(F32)[:, 15, :]
    last_out[...] = last
    send(last_out, last_h)
    send(edge_a, edge_a_h)
    send(edge_b, edge_b_h)
    first = (iota((8, reach), 1) == 0).astype(F32).astype(BF16)
    seated = jnp.concatenate(
        [jnp.zeros((GAIN_LANE, reach), F32), last, jnp.zeros((LANES - GAIN_LANE - blocks_own, reach), F32)],
        axis=0,
    )
    gain = mm(first, seated.astype(BF16), ((1,), (1,)))
    row_s[...] = jnp.zeros(row_s.shape, F32)
    row_s[0:1, 0:blocks_own] = down[...].astype(F32)
    extras = ids + (row_s[0:1, :] + gain[0:1, :])
    parts = 4
    size, chunks = out.shape[0] // parts, tiles // parts
    for part in range(parts):
        rows = slice(part * size, (part + 1) * size)
        hot = (iota((size, links), 0) + part * size).astype(F32) == slot_of
        out[rows, :] = fold(mm(jnp.where(hot, 1.0, 0.0).astype(BF16), by_block))
        out[pl.ds(part * size + SLOTS, chunks, CHUNK), :] = extras[part * chunks : (part + 1) * chunks]
        send(out.at[rows, :], out_h.at[rows, :])
    for copy in sent:
        copy.wait()


def lateral_kernel(
    rows_in, section, reach_source, last_row, spread, seats, order0, order1, out, source
):
    total = rows_in.shape[0]
    tiles = total // CHUNK
    blocks = section.shape[0]
    lane = iota((total, LANES), 1).astype(F32)
    extras = rows_in[pl.ds(SLOTS, tiles, CHUNK), :]
    ids_here = iota((tiles, LANES), 1)
    ids_here = (ids_here >= ID_LANE) & (ids_here < ID_LANE + SLOTS)
    ids = jnp.where(ids_here, extras, 0.0).astype(BF16)
    seat = seats[...] * mm(spread[...], ids)
    block = mm(seat.astype(BF16), jnp.ones((LANES, LANES), BF16)) - 1.0
    hot = (block == lane).astype(F32).astype(BF16)
    rows = rows_in[...]
    counted = jnp.concatenate([paired(rows), jnp.ones((total, LANES), BF16)], axis=1)
    found = mm(hot, counted, ((0,), (0,)))[:blocks]
    sums = fold(found[:, : 2 * LANES]) - found[:, 2 * LANES :] * section[...]
    src = reach_source[...] + (RIVER_SHARE * LATERAL_RATE) * sums
    section_in = fold(mm(hot[:, :blocks], paired(section[...])))
    out[...] = jnp.where(block >= 0.0, LATERAL_RATE * (rows - section_in), 0.0)
    source[...] = src
    ends = jnp.concatenate([src * last_row[...], jnp.zeros((LANES - blocks, LANES), F32)], axis=0)
    ends_hi, ends_lo = halves(ends)
    ones = jnp.ones((8, LANES), BF16)
    row = mm(ones, ends_hi, ((1,), (1,))) + mm(ones, ends_lo, ((1,), (1,)))
    out[pl.ds(SLOTS, tiles, CHUNK), :] = jnp.broadcast_to(row[0:1, :], (tiles, LANES))


def dense(ref, blocks, start, step, count):
    turns = LANES // blocks
    group = iota((count // turns, LANES), 1) // blocks
    rows = jnp.zeros((count // turns, LANES), F32)
    for turn in range(turns):
        x = ref[pl.ds(start + turn * step, count // turns, turns * step), :]
        x = pltpu.roll(x, turn * blocks, 1) if turn else x
        rows = jnp.where(group == turn, x, rows)
    return rows


def paths_kernel(own, one, two, three, reach):
    bands = 4
    band, me = lax.axis_index("band"), lax.axis_index("tile").astype(F32) + 1.0
    tiles = own.shape[0]
    blocks = LANES // bands
    group = iota((tiles, LANES), 1) // blocks
    downs = jnp.zeros((tiles, LANES), F32)
    gains = jnp.zeros((tiles, LANES), F32)
    for back, ref in enumerate((own, one, two, three)):
        here = group == band ^ back
        x = ref[...]
        down, gain = x, x
        for turn in (1, 2, 3):
            y = pltpu.roll(x, turn * blocks, 1)
            down = jnp.where(group == turn, y, down)
            gain = jnp.where(group == (turn + GAIN_LANE // blocks) % bands, y, gain)
        downs = jnp.where(here, down, downs)
        gains = jnp.where(here, gain, gains)
    high = jnp.floor(downs * (1.0 / LANES))
    tables = jnp.concatenate([high + 1.0, downs - high * LANES, gains], axis=0).astype(BF16)
    sources = dense(own, blocks, 0, 1, tiles)
    chunks = sources.shape[0]
    high = jnp.floor(sources * (1.0 / LANES))
    low = sources - high * LANES
    high = high + 1.0
    tile_row = iota((tiles, LANES), 0).astype(F32) + 1.0
    block_row = iota((LANES, LANES), 0).astype(F32)
    state = [(high[i : i + 1], low[i : i + 1], jnp.ones((1, LANES), F32)) for i in range(chunks)]
    for hop in range(LEVELS - 1):
        for i in range(0, chunks, 2):
            hits = [block_row == state[k][1] for k in (i, i + 1)]
            if hop < LEVELS - 2:
                hot = jnp.concatenate([jnp.where(hit, 1.0, 0.0).astype(BF16) for hit in hits], axis=1)
                founds = mm(tables, hot)
            for k, hit in zip((i, i + 1), hits):
                hi, lo, factor = state[k]
                cols = slice(k * LANES, (k + 1) * LANES)
                mine = jnp.where(hit, jnp.where(hi == me, factor, 0.0), 0.0)
                reach[:, cols] = mine if hop == 0 else reach[:, cols] + mine
                if hop < LEVELS - 2:
                    found = founds[:, (k - i) * LANES : (k - i + 1) * LANES]
                    here = tile_row == hi
                    picks = [
                        jnp.sum(jnp.where(here, found[p * tiles : (p + 1) * tiles], 0.0), axis=0, keepdims=True)
                        for p in range(3)
                    ]
                    state[k] = (picks[0], picks[1], factor * picks[2])


def gather_kernel(returned, reach, out):
    tiles = returned.shape[0] // CHUNK
    blocks = reach.shape[1] // tiles
    ends = dense(returned, blocks, SLOTS, CHUNK, tiles)
    total = jnp.zeros((LANES, LANES), F32)
    for i in range(ends.shape[0]):
        total = total + reach[:, i * LANES : (i + 1) * LANES] * ends[i : i + 1, :]
    hi, lo = halves(total)
    ones = jnp.ones((8, LANES), BF16)
    out[...] = mm(ones, hi, ((1,), (1,))) + mm(ones, lo, ((1,), (1,)))


def flow_kernel(source, inverse, base, column):
    blocks = source.shape[0]
    hi, lo = halves(source[...])
    first = (iota((blocks, LANES), 1) == 0).astype(F32).astype(BF16)
    stacked = jnp.concatenate([hi, lo, first], axis=0)
    row = iota((blocks, LANES), 0)
    base_now = jnp.zeros((blocks, LANES), F32)
    column_now = jnp.zeros((blocks, LANES), F32)
    for g in range(blocks):
        x = mm(stacked, inverse[g], ((1,), (1,)))
        base_now = jnp.where(row == g, x[:blocks] + x[blocks : 2 * blocks], base_now)
        column_now = jnp.where(row == g, x[2 * blocks :], column_now)
    base[...] = base_now
    column[...] = column_now


def discharge_kernel(base, column, own, one, two, three, out):
    blocks = base.shape[0]
    band = lax.axis_index("band")
    total = own[...] + one[...] + two[...] + three[...]
    turned = jnp.transpose(total)[:, 0:1]
    inflow = turned[0:blocks]
    for b in range(1, LANES // blocks):
        inflow = jnp.where(band == b, turned[b * blocks : (b + 1) * blocks], inflow)
    out[...] = base[...] + column[...] * inflow


def hot_kernel(slots, out, spread, seats):
    total, tiles = spread.shape
    slot = iota((total, 1), 0).astype(F32)
    owner = jnp.floor((slot + 0.5) * (1.0 / CHUNK))
    within = slot - owner * CHUNK + ID_LANE
    spread[...] = (iota((total, tiles), 1).astype(F32) == owner).astype(F32).astype(BF16)
    seats[...] = (iota((total, LANES), 1).astype(F32) == within).astype(F32)
    slot_c = jnp.transpose(slots[...])[:, 0:1]
    hot = iota(out.shape, 1).astype(F32) == slot_c
    out[...] = jnp.where(hot, 1.0, 0.0).astype(BF16)


def final_kernel(water, returned, hot, out):
    height = water.shape[0]
    groups = water.shape[1] // LANES
    lateral = fold(mm(hot[...], paired(returned[...])))
    for c in range(groups):
        cols = slice(c * LANES, (c + 1) * LANES)
        out[:, cols] = water[:, cols] - PLAIN_SHARE * lateral[c * height : (c + 1) * height]


def strips_kernel(got_a, got_b, f0, f1, f2, f3, f4, order, side_a, side_b):
    fields = (f0, f1, f2, f3, f4)
    height, width = f0.shape
    tiles = height // 8 + 2
    lane = iota((8, LANES), 1)
    groups = side_a.shape[0] // 8
    odd_band, odd_tile = lax.axis_index("band") % 2 == 1, lax.axis_index("tile") % 2 == 1
    lefts = [jnp.zeros((8, LANES), F32) for _ in range(groups)]
    rights = [jnp.zeros((8, LANES), F32) for _ in range(groups)]
    for a, field in enumerate(fields):
        for i in range(tiles):
            strip = a * tiles + i
            v, off = strip // 16, (strip % 16) * 8
            here = (lane >= off) & (lane < off + 8)
            first, last = slice(0, LANES), slice(width - LANES, width)
            if i in (0, tiles - 1):
                rows = slice(a * HALO, a * HALO + 8)
                from_a = odd_band if i == 0 else jnp.logical_not(odd_band)
                x = jnp.where(from_a, got_a[rows, first], got_b[rows, first])
                y = jnp.where(from_a, got_a[rows, last], got_b[rows, last])
            else:
                rows = slice(8 * i - 8, 8 * i)
                x, y = field[rows, first], field[rows, last]
                if a == 0:
                    x, y = x + f1[rows, first], y + f1[rows, last]
            x = pltpu.roll(x, off, 1) if off else x
            y = pltpu.roll(y, (off + 8) % LANES, 1) if (off + 8) % LANES else y
            lefts[v] = jnp.where(here, x, lefts[v])
            rights[v] = jnp.where(here, y, rights[v])
    for v in range(groups):
        side_a[8 * v : 8 * v + 8, :] = jnp.where(odd_tile, lefts[v], rights[v])
        side_b[8 * v : 8 * v + 8, :] = jnp.where(odd_tile, rights[v], lefts[v])


def flood_kernel(
    got_a, got_b, col_a, col_b, f0, f1, f2, f3, f4,
    water_out, east_out, south_out,
    level_s, bed_s, rough_s, qe_s, qs_s, mbe_s, mbs_s,
):
    height, width = f0.shape
    tiles = height // 8 + 2
    wide = width + LANES
    lane1 = iota((8, LANES), 1)
    scratch = (level_s, bed_s, rough_s, qe_s, qs_s)
    share = TIME_STEP / CELL_WIDTH
    rate = GRAVITY * TIME_STEP
    slope_rate = share * rate / CELL_WIDTH
    tile_index, band_index = lax.axis_index("tile"), lax.axis_index("band")
    tile_last, band_last = lax.axis_size("tile") - 1, lax.axis_size("band") - 1
    odd_band, odd_tile = band_index % 2 == 1, tile_index % 2 == 1
    easts, wests = [], []
    for v in range(col_a.shape[0] // 8):
        x, y = col_a[8 * v : 8 * v + 8, :], col_b[8 * v : 8 * v + 8, :]
        easts.append(jnp.where(odd_tile, y, x))
        wests.append(jnp.where(odd_tile, x, y))
    for a, (field, dst) in enumerate(zip((f0, f1, f2, f3, f4), scratch)):
        for i in range(tiles):
            strip = a * tiles + i
            v, off = strip // 16, (strip % 16) * 8
            x, y = easts[v], wests[v]
            x = pltpu.roll(x, LANES - off, 1) if off else x
            y = pltpu.roll(y, (LANES - 8 - off) % LANES, 1) if (LANES - 8 - off) % LANES else y
            edge = jnp.where(lane1 < 8, x, jnp.where(lane1 >= LANES - 8, y, 0.0))
            if i in (0, tiles - 1):
                rows = slice(a * HALO, a * HALO + 8)
                from_a = odd_band if i == 0 else jnp.logical_not(odd_band)
                body = jnp.where(from_a, got_a[rows, :], got_b[rows, :])
            else:
                rows = slice(8 * i - 8, 8 * i)
                body = field[rows, :]
                if a == 0:
                    body = body + f1[rows, :]
            if a >= 2:
                scale = rate / share if a == 2 else share
                body, edge = scale * body, scale * edge
            dst[8 * i : 8 * i + 8, :width] = body
            dst[8 * i : 8 * i + 8, width:] = edge
    lane = iota((8, wide), 1)
    sub = iota((8, wide), 0)
    shut_e = ((lane == width - 1) & (tile_index == tile_last)) | ((lane == wide - 1) & (tile_index == 0))
    ce = jnp.where(shut_e, 0.0, slope_rate)
    shut_n = (sub == 7) & (band_index == 0)
    shut_s = (sub == 7) & (band_index == band_last)
    cs_first = jnp.where(shut_n, 0.0, slope_rate)
    cs_last = jnp.where(shut_s, 0.0, slope_rate)
    nxt = bed_s[0:8, :]
    nxt_up = pltpu.roll(nxt, 7, 0)
    for i in range(tiles):
        rows = slice(8 * i, 8 * i + 8)
        bed, up = nxt, nxt_up
        if i + 1 < tiles:
            nxt = bed_s[8 * i + 8 : 8 * i + 16, :]
            nxt_up = pltpu.roll(nxt, 7, 0)
        mbe_s[rows, :] = jnp.maximum(bed, pltpu.roll(bed, wide - 1, 1))
        mbs_s[rows, :] = jnp.maximum(bed, jnp.where(sub == 7, nxt_up, up))
        qe_s[rows, :] = jnp.where(shut_e, 0.0, qe_s[rows, :])
    last = slice(height, height + 8)
    qs_s[last, :] = jnp.where(shut_s, 0.0, qs_s[last, :])

    def face(here, ahead, bed_max, rough, old, factor):
        depth = jnp.maximum(jnp.maximum(here, ahead) - bed_max, DEPTH_FLOOR)
        drag = rough * jnp.abs(old) * jnp.exp2(-FRICTION_POWER * jnp.log2(depth)) + 1.0
        near = pl.reciprocal(drag, approx=True)
        return (old - factor * depth * (ahead - here)) * near

    def substep(_, carry):
        nxt = level_s[0:8, :]
        nxt_up = pltpu.roll(nxt, 7, 0)
        north_turned = jnp.zeros((8, wide), F32)
        for i in range(tiles):
            rows = slice(8 * i, 8 * i + 8)
            level, up = nxt, nxt_up
            if i + 1 < tiles:
                nxt = level_s[8 * i + 8 : 8 * i + 16, :]
                nxt_up = pltpu.roll(nxt, 7, 0)
            rough = rough_s[rows, :]
            cs = cs_first if i == 0 else cs_last if i == tiles - 2 else slope_rate
            qe = face(level, pltpu.roll(level, wide - 1, 1), mbe_s[rows, :], rough, qe_s[rows, :], ce)
            below_level = jnp.where(sub == 7, nxt_up, up)
            qs = face(level, below_level, mbs_s[rows, :], rough, qs_s[rows, :], cs)
            qe_s[rows, :] = qe
            qs_s[rows, :] = qs
            turned = pltpu.roll(qs, 1, 0)
            north = jnp.where(sub == 0, north_turned, turned)
            north_turned = turned
            gained = pltpu.roll(qe, 1, 1) - qe + north - qs
            level_s[rows, :] = level + gained
        return carry

    lax.fori_loop(0, SUBSTEPS, substep, 0)
    inner = slice(HALO, HALO + height)
    water_out[...] = level_s[inner, :width] - bed_s[inner, :width]
    east_out[...] = (1.0 / share) * qe_s[inner, :width]
    south_out[...] = (1.0 / share) * qs_s[inner, :width]


def shaped(*shape):
    return jax.ShapeDtypeStruct(shape, F32)


def call(kernel, out_shape, specs, scratch=(), flops=0, size=0, exps=0, limit=16 * 1024 * 1024, outside=False):
    return pl.pallas_call(
        kernel,
        out_shape=out_shape,
        in_specs=specs,
        out_specs=jax.tree.map(lambda _: HBM if outside else VMEM, out_shape),
        scratch_shapes=list(scratch),
        compiler_params=pltpu.CompilerParams(vmem_limit_bytes=limit),
        cost_estimate=pl.CostEstimate(flops=flops, bytes_accessed=size, transcendentals=exps),
        name=kernel.__name__,
    )


def per_device(
    water_depth, flux_east, flux_south, bed_level, roughness, link_rows, link_blocks,
    reach_inverse, reach_source, river_section, block_level, block_down,
):
    tiles = lax.axis_size("tile")
    bands = lax.axis_size("band")
    tile_index = lax.axis_index("tile")
    band_index = lax.axis_index("band")
    height, width = water_depth.shape
    blocks, reach = reach_source.shape
    total = tiles * CHUNK
    links = link_rows.shape[-1]
    ring = [[(i, i ^ k) for i in range(bands)] for k in range(bands)]

    down = block_down.reshape(1, blocks)
    edge = shaped(5 * HALO, width)
    payload, slots, last_row, edge_a, edge_b = call(
        pack_kernel,
        (shaped(total, LANES), shaped(8, links), shaped(blocks, reach), edge, edge),
        [HBM] * 9,
        scratch=[
            pltpu.VMEM((height, width), F32),
            pltpu.VMEM((height, width), F32),
            pltpu.VMEM((1, links), jnp.int32),
            pltpu.VMEM((1, links), jnp.int32),
            pltpu.VMEM((blocks, 16, reach), BF16),
            pltpu.VMEM((8, LANES), F32),
            pltpu.VMEM((1, blocks), jnp.int32),
            pltpu.VMEM((total, LANES), F32),
            pltpu.VMEM((8, links), F32),
            pltpu.VMEM((blocks, reach), F32),
            pltpu.VMEM((5 * HALO, width), F32),
            pltpu.VMEM((5 * HALO, width), F32),
            pltpu.SemaphoreType.DMA((12,)),
            pltpu.SemaphoreType.DMA((8,)),
        ],
        limit=None,
        outside=True,
        flops=10**9,
        size=10**6,
    )(
        water_depth,
        bed_level,
        link_rows.reshape(1, links),
        link_blocks.reshape(1, links),
        reach_inverse,
        roughness,
        flux_east,
        flux_south,
        down,
    )
    rows_in = lax.all_to_all(
        payload.reshape(tiles, CHUNK, 1, LANES), "tile", split_axis=0, concat_axis=0, tiled=True
    )

    fields = (water_depth, bed_level, roughness, flux_east, flux_south)
    def pairs(count, first):
        return [(j, i) for k in range(first, count - 1, 2) for i, j in ((k, k + 1), (k + 1, k))]

    got_a = lax.ppermute(edge_a, "band", pairs(bands, 0))
    got_b = lax.ppermute(edge_b, "band", pairs(bands, 1))
    hot, spread, seats = call(
        hot_kernel,
        (
            jax.ShapeDtypeStruct((links, total), BF16),
            jax.ShapeDtypeStruct((total, tiles), BF16),
            shaped(total, LANES),
        ),
        [VMEM],
        flops=10**8,
        size=10**6,
    )(slots)
    side_a, side_b = call(
        strips_kernel, (shaped(48, LANES), shaped(48, LANES)), [VMEM] * 7 + [ANY], flops=10**6, size=10**6
    )(got_a, got_b, *fields, hot)
    col_a = lax.ppermute(side_a, "tile", pairs(tiles, 0))
    col_b = lax.ppermute(side_b, "tile", pairs(tiles, 1))

    answer, source = call(
        lateral_kernel,
        (shaped(total, LANES), shaped(blocks, LANES)),
        [VMEM] * 6 + [ANY] * 2,
        flops=10**9,
        size=10**6,
    )(rows_in.reshape(total, LANES), river_section, reach_source, last_row, spread, seats, col_a, col_b)
    returned = lax.all_to_all(
        answer.reshape(tiles, CHUNK, 1, LANES), "tile", split_axis=0, concat_axis=0, tiled=True
    )

    wide = width + LANES
    tall = height + 2 * HALO
    water_now, final_east, final_south = call(
        flood_kernel,
        (shaped(height, width),) * 3,
        [VMEM] * 9,
        scratch=[pltpu.VMEM((tall, wide), F32)] * 7,
        flops=10**8,
        size=10**7,
        exps=10**7,
    )(got_a, got_b, col_a, col_b, *fields)
    base_flow, column = call(
        flow_kernel, (shaped(blocks, reach),) * 2, [VMEM] * 2, flops=10**8, size=10**6
    )(source, reach_inverse)
    extras = rows_in.reshape(tiles, CHUNK, LANES)[:, SLOTS, :]
    others = [lax.ppermute(extras, "band", ring[k]) for k in (3, 2, 1)][::-1]
    reached = call(
        paths_kernel, shaped(LANES, tiles * blocks), [VMEM] * 4, flops=10**9, size=10**6
    )(extras, *others)

    pushed = call(gather_kernel, shaped(8, LANES), [VMEM] * 2, flops=10**6, size=10**6)(
        returned.reshape(total, LANES), reached
    )
    parts = [pushed] + [lax.ppermute(pushed, "band", ring[k]) for k in (3, 2, 1)]
    final_depth = call(
        final_kernel, shaped(height, width), [VMEM] * 3, flops=10**9, size=10**6
    )(water_now, returned.reshape(total, LANES), hot)
    discharge = call(
        discharge_kernel, shaped(blocks, reach), [VMEM] * 6, flops=10**4, size=10**4
    )(base_flow, column, *parts)
    return (final_depth, final_east, final_south, discharge)


def solution(mesh):
    grid = P("band", "tile")
    owned = P(("tile", "band"))
    lists = P("tile", "band", None)
    return jax.shard_map(
        per_device,
        mesh=mesh,
        in_specs=(grid,) * 5 + (lists,) * 2 + (owned,) * 5,
        out_specs=(grid, grid, grid, owned),
        check_vma=False,
    )
```
